256 devices in a mesh: gx: 16 (over z, x_hi), gy: 16 (over x_lo, y, core).
Axes of the slice: x: 4 (x_hi: 2, x_lo: 2; x = x_hi * 2 + x_lo), y: 4, z: 8, core: 2. Of those that a mesh axis runs over, the one named last changes fastest.
Arguments:
- coarse: float32 [5, 128, 128, 128], P(None, 'gx', 'gy'), may hold values from -6 to 6
- fine_density_state: float32 [512, 5, 16, 16, 128], P(('gx', 'gy')), may hold values from -6 to 6
- corners: int32 [512, 3], replicated, may hold values from -1 to 240, as said below
- ghost_source: int32 [512, 6], replicated, may hold values from -1 to 511, as said below
- courant: float32 [3, 5], replicated, may hold values from -0.3 to 0.3
- reaction: float32 [5, 5], replicated, may hold values from -1 to 1
Outputs:
- coarse_new: float32 [5, 128, 128, 128], P(None, 'gx', 'gy')
- fine_new: float32 [512, 5, 16, 16, 128], P(('gx', 'gy'))
The draws below stay inside these ranges and needn't reach their ends.
Inputs may be any that keep to these rules, and one draw needn't show every extreme that they name: `corners`: row s is the lower fine corner of the box in slot s, slot s held by device s // 2 (device index gx * 16 + gy), or -1 -1 -1 for an empty slot. Corners are multiples of 16, 16 and 128; a box lies over the coarse columns of a device with the same gx index as the device holding its slot; no two boxes at one place; each gx index has 8 boxes; a device holds at most 2 boxes and some device of each gx index exactly 2. `ghost_source`: for faces west, east, south, north, bottom, top of the box in slot s: the slot of the box on the other side, or -1 where that place is not refined or lies outside the grid's bottom or top; all -1 for empty slots.
All inputs are finite; a program needn't handle non-finite values.
Results may differ from the reference program's by a relative error of at most 0.0003.
Values sent between devices are 32-bit elements; how exact they have to be, the bound alone decides.
No kernel may reach another device: no remote copies, remote signals or barrier semaphores. Data moves between devices by JAX's collectives and lax.ppermute only.
A program may use at most 192 MiB of HBM per device.

```python
import jax
import jax.numpy as jnp
from jax import lax

SPECIES_COUNT = 5
COARSE_X_CELLS = 8
COARSE_Y_CELLS = 8
COARSE_Z_CELLS = 128
SLOTS = 2
BOX_GRP = 8
NX = 128
NY = 128
TOTAL_BOX_SLOTS = 512
N_GX = 16
N_GY = 16


def layout(key):
    slots_group = N_GY * SLOTS
    places = 2 * N_GY

    def group(group_index):
        group_key = jax.random.fold_in(key, group_index)
        pick_key, busy_key, rank_key = jax.random.split(group_key, 3)
        shuffled = jax.random.permutation(pick_key, places)
        position = jnp.arange(places)
        first_rule = jnp.where(shuffled == places - 1, -1, position)
        last_rule = jnp.where(shuffled < 2, shuffled - 2 * places, position)
        priority = jnp.where(group_index == 0, first_rule, jnp.where(group_index == N_GX - 1, last_rule, position))
        chosen = shuffled[jnp.argsort(priority, stable=True)][:BOX_GRP]
        busiest = jnp.where(group_index == N_GX - 1, N_GY - 1, jax.random.randint(busy_key, (), 0, N_GY))
        ranking = jax.random.permutation(rank_key, slots_group)
        owners = jnp.arange(slots_group) // SLOTS
        scores = ranking + jnp.where(owners == busiest, -2 * slots_group, 0)
        ordered = jnp.argsort(scores, stable=True)[:BOX_GRP]
        return (chosen, ordered)
    chosen, ordered = jax.vmap(group)(jnp.arange(N_GX))
    group_ids = jnp.arange(N_GX)[:, None] + jnp.zeros_like(chosen)
    slot_index_list = (group_ids * slots_group + ordered).astype(jnp.int32)
    col_ids = chosen // 2
    half_ids = chosen % 2
    placed_boxes = jnp.stack((group_ids * 2 * COARSE_X_CELLS, col_ids * 2 * COARSE_Y_CELLS, half_ids * COARSE_Z_CELLS), axis=-1).astype(jnp.int32)
    corners = jnp.full((TOTAL_BOX_SLOTS, 3), -1, jnp.int32).at[slot_index_list.reshape(-1)].set(placed_boxes.reshape(-1, 3))
    position_slot = jnp.full((N_GX, N_GY, 2), -1, jnp.int32).at[group_ids, col_ids, half_ids].set(slot_index_list)
    west_slot = position_slot[(group_ids - 1) % N_GX, col_ids, half_ids]
    east_slot = position_slot[(group_ids + 1) % N_GX, col_ids, half_ids]
    south_slot = position_slot[group_ids, (col_ids - 1) % N_GY, half_ids]
    north_slot = position_slot[group_ids, (col_ids + 1) % N_GY, half_ids]
    bottom_slot = jnp.where(half_ids == 1, position_slot[group_ids, col_ids, 0], -1)
    top_slot = jnp.where(half_ids == 0, position_slot[group_ids, col_ids, 1], -1)
    listed_entries = jnp.stack((west_slot, east_slot, south_slot, north_slot, bottom_slot, top_slot), axis=-1).astype(jnp.int32)
    source_terms = jnp.full((TOTAL_BOX_SLOTS, 6), -1, jnp.int32).at[slot_index_list.reshape(-1)].set(listed_entries.reshape(-1, 6))
    return (corners, source_terms)


def draw_corners(key, part):
    return layout(key)[0]


def draw_ghost_source(key, part):
    return layout(key)[1]


def level_of(rng, dims, cuts, least, top_value):
    loudness = 1.0
    for dim, shards_of in cuts:
        draws = jax.random.uniform(jax.random.fold_in(jax.random.fold_in(rng, 6), dim), (shards_of,), jnp.float32, least / len(cuts), top_value / len(cuts))
        loudness = loudness * jnp.repeat(jnp.exp(draws), dims[dim] // shards_of).reshape((-1,) + (1,) * (len(dims) - 1 - dim))
    return loudness


def bell_draw(own_key, shape, deviation, bound, pieces=(), held_as=jnp.bfloat16):
    result = deviation * jax.random.normal(own_key, shape, jnp.float32)
    if pieces:
        result = result * level_of(own_key, shape, pieces, -0.22, 0.18)
    return jnp.clip(result, -bound, bound).astype(held_as)


def setup_inputs(seed: int = 0) -> dict:
    arg_keys = jax.random.split(jax.random.key(seed), 7)
    coarse = bell_draw(arg_keys[0], (SPECIES_COUNT, NX, NY, COARSE_Z_CELLS), 1.0, 6.0, ((1, 16), (2, 16)), jnp.float32)
    fine_density_state = bell_draw(arg_keys[1], (TOTAL_BOX_SLOTS, SPECIES_COUNT, 2 * COARSE_X_CELLS, 2 * COARSE_Y_CELLS, COARSE_Z_CELLS), 1.0, 6.0, ((0, 256),), jnp.float32)
    corners = draw_corners(jax.random.fold_in(arg_keys[6], 71), 0)
    ghost_source = draw_ghost_source(jax.random.fold_in(arg_keys[6], 71), 0)
    courant = jnp.clip(jax.random.uniform(arg_keys[4], (3, SPECIES_COUNT), jnp.float32, -0.3, 0.3), -0.3, 0.3)
    reaction = bell_draw(arg_keys[5], (SPECIES_COUNT, SPECIES_COUNT), 0.2, 1.0, (), jnp.float32)
    return dict(coarse=coarse, fine_density_state=fine_density_state, corners=corners, ghost_source=ghost_source, courant=courant, reaction=reaction)


def advance(value_entries, planes, rate_up, rate_down, reaction, factor):
    west_face, east_face, south_face, north_face, bottom_face, top_face = planes
    flux_first = rate_up[0][:, None, None, None] * jnp.concatenate((west_face[:, None], value_entries), axis=1) + rate_down[0][:, None, None, None] * jnp.concatenate((value_entries, east_face[:, None]), axis=1)
    flux_second = rate_up[1][:, None, None, None] * jnp.concatenate((south_face[:, :, None], value_entries), axis=2) + rate_down[1][:, None, None, None] * jnp.concatenate((value_entries, north_face[:, :, None]), axis=2)
    flux_third = rate_up[2][:, None, None, None] * jnp.concatenate((bottom_face[..., None], value_entries), axis=3) + rate_down[2][:, None, None, None] * jnp.concatenate((value_entries, top_face[..., None]), axis=3)
    mixing = jnp.einsum("ce,exyz->cxyz", reaction, value_entries, precision=lax.Precision.HIGHEST)
    updated = value_entries - (flux_first[:, 1:] - flux_first[:, :-1]) - (flux_second[:, :, 1:] - flux_second[:, :, :-1]) - (flux_third[..., 1:] - flux_third[..., :-1]) + factor * mixing
    return updated, flux_first, flux_second, flux_third


def inject(surface):
    return jnp.repeat(jnp.repeat(surface, 2, axis=1), 2, axis=2)


def coarsen(face, first, second):
    return face.reshape(face.shape[0], face.shape[1], first, 2, second, 2).sum(axis=(3, 5))


def reference(coarse, fine_density_state, corners, ghost_source, courant, reaction):
    depth_half = COARSE_Z_CELLS // 2
    rate_up = jnp.maximum(courant, 0.0)
    rate_down = jnp.minimum(courant, 0.0)
    no_inflow = jnp.zeros((SPECIES_COUNT, NX, NY), jnp.float32)
    borders = (coarse[:, -1], coarse[:, 0], coarse[:, :, -1], coarse[:, :, 0], no_inflow, no_inflow)
    provisional, coarse_x, coarse_y, coarse_z = advance(coarse, borders, rate_up, rate_down, reaction, 1.0)
    middle = 0.5 * (coarse + provisional)
    is_live = corners[:, 0] >= 0
    start_x = jnp.where(is_live, corners[:, 0] // 2, 0).astype(jnp.int32)
    start_y = jnp.where(is_live, corners[:, 1] // 2, 0).astype(jnp.int32)
    start_z = jnp.where(is_live, corners[:, 2] // 2, 0).astype(jnp.int32)
    home_z = start_z // depth_half

    def coarse_faces(coarse_field):
        padded = jnp.pad(coarse_field, ((0, 0), (0, 0), (0, 0), (1, 1)))

        def one_slot(corner_x, corner_y, corner_z):
            anchor = jnp.zeros((), jnp.int32)
            west_face = lax.dynamic_slice(coarse_field, (anchor, (corner_x - 1) % NX, corner_y, corner_z), (SPECIES_COUNT, 1, COARSE_Y_CELLS, depth_half))[:, 0]
            east_face = lax.dynamic_slice(coarse_field, (anchor, (corner_x + COARSE_X_CELLS) % NX, corner_y, corner_z), (SPECIES_COUNT, 1, COARSE_Y_CELLS, depth_half))[:, 0]
            south_face = lax.dynamic_slice(coarse_field, (anchor, corner_x, (corner_y - 1) % NY, corner_z), (SPECIES_COUNT, COARSE_X_CELLS, 1, depth_half))[:, :, 0]
            north_face = lax.dynamic_slice(coarse_field, (anchor, corner_x, (corner_y + COARSE_Y_CELLS) % NY, corner_z), (SPECIES_COUNT, COARSE_X_CELLS, 1, depth_half))[:, :, 0]
            bottom_face = lax.dynamic_slice(padded, (anchor, corner_x, corner_y, corner_z), (SPECIES_COUNT, COARSE_X_CELLS, COARSE_Y_CELLS, 1))[..., 0]
            top_face = lax.dynamic_slice(padded, (anchor, corner_x, corner_y, corner_z + depth_half + 1), (SPECIES_COUNT, COARSE_X_CELLS, COARSE_Y_CELLS, 1))[..., 0]
            return tuple(inject(surface) for surface in (west_face, east_face, south_face, north_face, bottom_face, top_face))

        return jax.vmap(one_slot)(start_x, start_y, start_z)

    value_entries = fine_density_state
    face_sums = None
    for coarse_field in (coarse, middle):
        from_coarse = coarse_faces(coarse_field)
        own_faces = (value_entries[:, :, -1], value_entries[:, :, 0], value_entries[:, :, :, -1], value_entries[:, :, :, 0], value_entries[..., -1], value_entries[..., 0])
        ghost_faces = tuple(
            jnp.where((ghost_source[:, face_index] >= 0)[:, None, None, None],
                      jnp.take(own_faces[face_index], jnp.maximum(ghost_source[:, face_index], 0), axis=0),
                      from_coarse[face_index])
            for face_index in range(6))
        value_entries, flux_first, flux_second, flux_third = jax.vmap(advance, in_axes=(0, 0, None, None, None, None))(value_entries, ghost_faces, rate_up, rate_down, reaction, 0.5)
        boundary = (flux_first[:, :, 0], flux_first[:, :, -1], flux_second[:, :, :, 0], flux_second[:, :, :, -1], flux_third[..., 0], flux_third[..., -1])
        face_sums = boundary if face_sums is None else tuple(older + newer for older, newer in zip(face_sums, boundary))
    fine_new = jnp.where(is_live[:, None, None, None, None], value_entries, 0.0)

    fine_sums = (coarsen(face_sums[0], COARSE_Y_CELLS, depth_half), coarsen(face_sums[1], COARSE_Y_CELLS, depth_half),
                 coarsen(face_sums[2], COARSE_X_CELLS, depth_half), coarsen(face_sums[3], COARSE_X_CELLS, depth_half),
                 coarsen(face_sums[4], COARSE_X_CELLS, COARSE_Y_CELLS), coarsen(face_sums[5], COARSE_X_CELLS, COARSE_Y_CELLS))

    def coarse_flux(corner_x, corner_y, corner_z):
        anchor = jnp.zeros((), jnp.int32)
        west_face = lax.dynamic_slice(coarse_x, (anchor, corner_x, corner_y, corner_z), (SPECIES_COUNT, 1, COARSE_Y_CELLS, depth_half))[:, 0]
        east_face = lax.dynamic_slice(coarse_x, (anchor, corner_x + COARSE_X_CELLS, corner_y, corner_z), (SPECIES_COUNT, 1, COARSE_Y_CELLS, depth_half))[:, 0]
        south_face = lax.dynamic_slice(coarse_y, (anchor, corner_x, corner_y, corner_z), (SPECIES_COUNT, COARSE_X_CELLS, 1, depth_half))[:, :, 0]
        north_face = lax.dynamic_slice(coarse_y, (anchor, corner_x, corner_y + COARSE_Y_CELLS, corner_z), (SPECIES_COUNT, COARSE_X_CELLS, 1, depth_half))[:, :, 0]
        bottom_face = lax.dynamic_slice(coarse_z, (anchor, corner_x, corner_y, corner_z), (SPECIES_COUNT, COARSE_X_CELLS, COARSE_Y_CELLS, 1))[..., 0]
        top_face = lax.dynamic_slice(coarse_z, (anchor, corner_x, corner_y, corner_z + depth_half), (SPECIES_COUNT, COARSE_X_CELLS, COARSE_Y_CELLS, 1))[..., 0]
        return west_face, east_face, south_face, north_face, bottom_face, top_face

    coarse_sums = jax.vmap(coarse_flux)(start_x, start_y, start_z)
    reflux_flags = is_live[:, None] & (ghost_source < 0)
    reflux_flags = reflux_flags.at[:, 4].set(reflux_flags[:, 4] & (home_z == 1))
    reflux_flags = reflux_flags.at[:, 5].set(reflux_flags[:, 5] & (home_z == 0))
    signs = (1.0, -1.0, 1.0, -1.0, 1.0, -1.0)
    changes = [signs[face_index] * (coarse_sums[face_index] - fine_sums[face_index] / 8.0) for face_index in range(6)]
    changes = [jnp.where(reflux_flags[:, face_index][:, None, None, None], changes[face_index], 0.0) for face_index in range(6)]

    range_x = jnp.arange(COARSE_X_CELLS, dtype=jnp.int32)
    range_y = jnp.arange(COARSE_Y_CELLS, dtype=jnp.int32)
    range_z = jnp.arange(depth_half, dtype=jnp.int32)
    along_y = start_y[:, None, None] + range_y[None, :, None]
    along_z = start_z[:, None, None] + range_z[None, None, :]
    across_x = start_x[:, None, None] + range_x[None, :, None]
    corrections = jnp.zeros((SPECIES_COUNT, NX, NY, COARSE_Z_CELLS), jnp.float32)
    corrections = corrections.at[:, ((start_x - 1) % NX)[:, None, None], along_y, along_z].add(jnp.moveaxis(changes[0], 0, 1))
    corrections = corrections.at[:, ((start_x + COARSE_X_CELLS) % NX)[:, None, None], along_y, along_z].add(jnp.moveaxis(changes[1], 0, 1))
    corrections = corrections.at[:, across_x, ((start_y - 1) % NY)[:, None, None], along_z].add(jnp.moveaxis(changes[2], 0, 1))
    corrections = corrections.at[:, across_x, ((start_y + COARSE_Y_CELLS) % NY)[:, None, None], along_z].add(jnp.moveaxis(changes[3], 0, 1))
    flat_y = start_y[:, None, None] + range_y[None, None, :]
    corrections = corrections.at[:, across_x, flat_y, jnp.maximum(start_z - 1, 0)[:, None, None]].add(jnp.moveaxis(changes[4], 0, 1))
    corrections = corrections.at[:, across_x, flat_y, jnp.minimum(start_z + depth_half, COARSE_Z_CELLS - 1)[:, None, None]].add(jnp.moveaxis(changes[5], 0, 1))
    coarse_new = provisional + corrections

    mean_values = value_entries.reshape(TOTAL_BOX_SLOTS, SPECIES_COUNT, COARSE_X_CELLS, 2, COARSE_Y_CELLS, 2, depth_half, 2).mean(axis=(3, 5, 7))
    target_x = jnp.where(is_live, start_x, NX)[:, None, None, None] + range_x[None, :, None, None]
    target_y = start_y[:, None, None, None] + range_y[None, None, :, None]
    target_z = start_z[:, None, None, None] + range_z[None, None, None, :]
    coarse_new = coarse_new.at[:, target_x, target_y, target_z].set(jnp.moveaxis(mean_values, 0, 1), mode="drop")
    return coarse_new, fine_new
```

```python
import functools

import jax
import jax.numpy as jnp
from jax import lax
from jax.experimental import pallas as pl
from jax.experimental.pallas import tpu as pltpu
from jax.sharding import PartitionSpec as P

SPECIES = 5
GX = 16
GY = 16
BOXES = 8
PAIRS = 8
ROW_SLOTS = 32
FINE_ROWS = 160
PIECE_ROWS = 184
STRIDE = 16
LIST_STRIDE = 40
F32 = jnp.float32
SLOT, COL, HALF, WEST, EAST, SOUTH, NORTH, BOTTOM, TOP, OPEN_Y, BELOW, ABOVE = range(12)

VMEM = pl.BlockSpec(memory_space=pltpu.VMEM)
SMEM = pl.BlockSpec(memory_space=pltpu.SMEM)


def place():
    j = lax.axis_index("gy")
    return j // 2, lax.rem(j, 2)


def table_kernel(corners, sources, table, listed, ranks):
    row = lax.axis_index("gx")
    a, b = place()
    groups = [lax.rem(row + GX - 1 + r, GX) for r in range(3)]
    for r in range(3):

        def scan(t, count, r=r):
            live = corners[0, groups[r] * ROW_SLOTS + t] >= 0
            listed[r * LIST_STRIDE + count] = t
            ranks[r * ROW_SLOTS + t] = count
            return count + jnp.where(live, 1, 0)

        lax.fori_loop(0, ROW_SLOTS, scan, jnp.int32(0), unroll=8)

    def rank(r, source):
        found = ranks[r * ROW_SLOTS + lax.rem(jnp.maximum(source, 0), ROW_SLOTS)]
        return jnp.where(source >= 0, found, -1)

    for i in range(BOXES):
        t = listed[LIST_STRIDE + i]
        slot = groups[1] * ROW_SLOTS + t
        west, east, south, north, bottom, top = [sources[f, slot] for f in range(6)]
        base = STRIDE * i
        table[base + SLOT] = t
        table[base + COL] = corners[1, slot] // 16
        table[base + HALF] = corners[2, slot] // 128
        table[base + WEST] = jnp.where(a > 0, i, rank(0, west))
        table[base + EAST] = jnp.where(a < PAIRS - 1, i, rank(2, east))
        table[base + SOUTH] = jnp.where(b > 0, i, rank(1, south))
        table[base + NORTH] = jnp.where(b < 1, i, rank(1, north))
        table[base + BOTTOM] = rank(1, bottom)
        table[base + TOP] = rank(1, top)
        table[base + OPEN_Y] = jnp.where(jnp.where(b > 0, south, north) < 0, 1, 0)
        for r, face, field in ((0, 1, BELOW), (2, 0, ABOVE)):
            beside = groups[r] * ROW_SLOTS + listed[r * LIST_STRIDE + i]
            where = corners[1, beside] // 16 * 2 + corners[2, beside] // 128
            table[base + field] = jnp.where(sources[face, beside] < 0, where, -1)
        for field in range(12, STRIDE):
            table[base + field] = 0


def pack_kernel(coarse, fine, out):
    for j in range(GY):
        a, b = j // 2, j % 2
        part = fine[:, :, 2 * a : 2 * a + 2, 8 * b : 8 * b + 8, :]
        out[j, :FINE_ROWS, :] = part.reshape(FINE_ROWS, 128)
        for s in range(SPECIES):
            out[j, FINE_ROWS + 4 * s : FINE_ROWS + 4 * s + 4, :] = coarse[s, a, 4 * b : 4 * b + 4, :]
        out[j, FINE_ROWS + 20 :, :] = jnp.zeros((4, 128), F32)


def unpack_kernel(received, coarse, fine):
    for j in range(GY):
        a, b = j // 2, j % 2
        part = received[j, :FINE_ROWS, :].reshape(2, SPECIES, 2, 8, 128)
        fine[:, :, 2 * a : 2 * a + 2, 8 * b : 8 * b + 8, :] = part
        for s in range(SPECIES):
            coarse[s, a, 4 * b : 4 * b + 4, :] = received[j, FINE_ROWS + 4 * s : FINE_ROWS + 4 * s + 4, :]


def compact_kernel(table, received, plane0, plane1):
    for i in range(BOXES):
        t = table[STRIDE * i + SLOT]
        start = pl.multiple_of(lax.rem(t, 2) * 80, 8)
        box = received[t // 2, pl.ds(start, 80), :].reshape(SPECIES, 2, 8, 128)
        plane0[i] = box[:, 0]
        plane1[i] = box[:, 1]
    for c in range(GY):
        for s in range(SPECIES):
            rows = received[c, FINE_ROWS + 4 * s : FINE_ROWS + 4 * s + 4, :]
            low = 4 * (c % 2)
            plane0[BOXES + c // 2, s, low : low + 4, :] = rows
            plane1[BOXES + c // 2, s, low : low + 4, :] = rows


def iotas():
    return lax.broadcasted_iota(jnp.int32, (8, 128), 0), lax.broadcasted_iota(jnp.int32, (8, 128), 1)


def take(tile, index, axis):
    return jnp.take_along_axis(tile, index, axis=axis, mode="promise_in_bounds")


def turn(tile, shift, axis):
    return pltpu.roll(tile, shift % tile.shape[axis], axis)


def rates_of(courant):
    up = [[jnp.maximum(courant[d, s], 0.0) for s in range(SPECIES)] for d in range(3)]
    down = [[jnp.minimum(courant[d, s], 0.0) for s in range(SPECIES)] for d in range(3)]
    return up, down


def moved(value, sides, up, down, reaction, others, s, factor):
    total = value
    for d, (lower, upper) in enumerate(sides):
        total = total - (up[d][s] * (value - lower) + down[d][s] * (upper - value))
    mixing = reaction[s, 0] * others[0]
    for e in range(1, SPECIES):
        mixing = mixing + reaction[s, e] * others[e]
    return total + factor * mixing


def fine_step(i, table, own, west, east, peer, up, down, reaction, write):
    rows, lanes = iotas()
    _, b = place()
    field = lambda f: table[STRIDE * i + f]
    col, half = field(COL), field(HALF)
    pair = BOXES + col // 2
    row_index = 4 * lax.rem(col, 2) + rows // 2
    lane_index = 64 * half + lanes // 2
    outer = lax.rem(jnp.where(b > 0, col + 1, col + GY - 1), GY)
    outer_row = 4 * lax.rem(outer, 2) + jnp.where(b > 0, 0, 3)
    found = [field(f) for f in (WEST, EAST, SOUTH, NORTH, BOTTOM, TOP)]
    there = [source >= 0 for source in found]
    at = [jnp.maximum(source, 0) for source in found]
    values = [[own[xi][i, s] for s in range(SPECIES)] for xi in range(2)]
    for s in range(SPECIES):
        beside = take(own[0][pair, s], row_index, 0)
        across = turn(beside, 64, 1)
        below = jnp.where(half > 0, across, 0.0)
        above = jnp.where(half > 0, 0.0, across)
        coarse_west = take(take(west[pair, s], row_index, 0), lane_index, 1)
        coarse_east = take(take(east[pair, s], row_index, 0), lane_index, 1)
        edge = jnp.broadcast_to(peer[0][BOXES + outer // 2, s, pl.ds(outer_row, 1), :], (8, 128))
        edge = take(edge, lane_index, 1)
        ghost_west = jnp.where(there[0], west[at[0], s], coarse_west)
        ghost_east = jnp.where(there[1], east[at[1], s], coarse_east)
        for xi in range(2):
            value = values[xi][s]
            south = jnp.where(there[2], peer[xi][at[2], s], edge)
            north = jnp.where(there[3], peer[xi][at[3], s], edge)
            bottom = jnp.where(there[4], own[xi][at[4], s], below)
            top = jnp.where(there[5], own[xi][at[5], s], above)
            sides = (
                (ghost_west, values[1][s]) if xi == 0 else (values[0][s], ghost_east),
                (
                    turn(jnp.where(rows == 7, south, value), 1, 0),
                    turn(jnp.where(rows == 0, north, value), -1, 0),
                ),
                (
                    turn(jnp.where(lanes == 127, bottom, value), 1, 1),
                    turn(jnp.where(lanes == 0, top, value), -1, 1),
                ),
            )
            write(xi, s, moved(value, sides, up, down, reaction, values[xi], s, 0.5))


def first_kernel(table, courant, reaction, own0, own1, west, east, peer0, peer1, new0, new1, provisional):
    rows, lanes = iotas()
    _, b = place()
    up, down = rates_of(courant)
    quarter = lax.rem(rows, 4)

    def coarse_pair(cp, carry):
        before = BOXES + lax.rem(cp + PAIRS - 1, PAIRS)
        after = BOXES + lax.rem(cp + 1, PAIRS)
        here = BOXES + cp
        values = [own0[here, s] for s in range(SPECIES)]
        for s in range(SPECIES):
            value = values[s]
            peer = peer0[here, s]
            outer_low = turn(jnp.where(rows == 7, peer0[before, s], peer), 1, 0)
            outer_high = turn(jnp.where(rows == 0, peer0[after, s], peer), -1, 0)
            south = jnp.where(b > 0, turn(peer, 5, 0), outer_low)
            north = jnp.where(b > 0, outer_high, turn(peer, 3, 0))
            sides = (
                (west[here, s], east[here, s]),
                (
                    jnp.where(quarter == 0, south, turn(value, 1, 0)),
                    jnp.where(quarter == 3, north, turn(value, -1, 0)),
                ),
                (
                    turn(jnp.where(lanes == 127, 0.0, value), 1, 1),
                    turn(jnp.where(lanes == 0, 0.0, value), -1, 1),
                ),
            )
            result = moved(value, sides, up, down, reaction, values, s, 1.0)
            provisional[cp, s] = result
            middle = 0.5 * (value + result)
            new0[here, s] = middle
            new1[here, s] = middle
        return carry

    lax.fori_loop(0, PAIRS, coarse_pair, 0)
    new = (new0, new1)

    def box(i, carry):
        def write(xi, s, result):
            new[xi][i, s] = result

        fine_step(i, table, (own0, own1), west, east, (peer0, peer1), up, down, reaction, write)
        return carry

    lax.fori_loop(0, BOXES, box, 0)


def second_kernel(
    table, courant, reaction, old0, old1, old_west, old_east, old_peer0, old_peer1,
    own0, own1, west, east, peer0, peer1, provisional, out, coarse_new,
):
    rows, lanes = iotas()
    a, b = place()
    up, down = rates_of(courant)
    row_fold = lax.rem(2 * rows, 8)
    lane_fold = lax.rem(2 * lanes, 128)
    fold_rows = lambda tile: take(tile + turn(tile, -1, 0), row_fold, 0)
    fold_lanes = lambda tile: take(tile + turn(tile, -1, 1), lane_fold, 1)
    coarse_new[...] = provisional[...]

    def clear(j, carry):
        out[j, :FINE_ROWS, :] = jnp.zeros((FINE_ROWS, 128), F32)
        out[j, FINE_ROWS + 20 :, :] = jnp.zeros((4, 128), F32)
        return carry

    lax.fori_loop(0, GY, clear, 0)

    def box(i, carry):
        field = lambda f: table[STRIDE * i + f]
        t, col, half = field(SLOT), field(COL), field(HALF)
        start = lax.rem(t, 2) * 80

        def write(xi, s, result):
            out[t // 2, pl.ds(pl.multiple_of(start + (2 * s + xi) * 8, 8), 8), :] = result

        fine_step(i, table, (own0, own1), west, east, (peer0, peer1), up, down, reaction, write)

        cp = col // 2
        pair = BOXES + cp
        in_rows = rows // 4 == lax.rem(col, 2)
        is_high = half > 0
        open_z = jnp.where(is_high, field(BOTTOM), field(TOP)) < 0
        outer = lax.rem(jnp.where(b > 0, col + GY - 1, col + 1), GY)
        outer_row = 4 * lax.rem(outer, 2) + jnp.where(b > 0, 3, 0)
        inner_row = 4 * lax.rem(col, 2) + jnp.where(b > 0, 0, 3)
        outer_pair = outer // 2
        fine_row = jnp.where(b > 0, 0, 7)
        in_half = lanes[:1] // 64 == half
        for s in range(SPECIES):
            coarse = old0[pair, s]
            both = coarse + own0[pair, s]
            total = fold_rows((old0[i, s] + old1[i, s]) + (own0[i, s] + own1[i, s]))
            beside = jnp.where(is_high, turn(total, 63, 1), turn(total, 65, 1))
            across = jnp.where(is_high, turn(coarse, -1, 1), turn(coarse, 1, 1))
            rate_out = jnp.where(is_high, up[2][s], down[2][s])
            rate_in = jnp.where(is_high, down[2][s], up[2][s])
            change = (rate_out * coarse + rate_in * across) - (rate_out * 0.5 * both + rate_in * 0.125 * beside)
            change = jnp.where(is_high, change, -change)
            here = in_rows & (lanes == jnp.where(is_high, 63, 64)) & open_z
            coarse_new[cp, s] = coarse_new[cp, s] + jnp.where(here, change, 0.0)

            line = pl.ds(fine_row, 1)
            total = (old_peer0[i, s, line, :] + old_peer1[i, s, line, :]) + (
                peer0[i, s, line, :] + peer1[i, s, line, :]
            )
            beside = fold_lanes(jnp.broadcast_to(total, (8, 128)))[:1]
            at = pl.ds(outer_row, 1)
            coarse = old0[BOXES + outer_pair, s, at, :]
            both = coarse + own0[BOXES + outer_pair, s, at, :]
            across = old_peer0[pair, s, pl.ds(inner_row, 1), :]
            rate_out = jnp.where(b > 0, up[1][s], down[1][s])
            rate_in = jnp.where(b > 0, down[1][s], up[1][s])
            change = (rate_out * coarse + rate_in * across) - (rate_out * 0.5 * both + rate_in * 0.125 * beside)
            change = jnp.where(b > 0, change, -change)
            here = in_half & (field(OPEN_Y) > 0)
            coarse_new[outer_pair, s, at, :] = coarse_new[outer_pair, s, at, :] + jnp.where(here, change, 0.0)
        return carry

    lax.fori_loop(0, BOXES, box, 0)

    def cross(name, old_side, side, rates_out, rates_in, sign):
        def face(i, carry):
            code = table[STRIDE * i + name]

            @pl.when(code >= 0)
            def _():
                cp = code // 4
                here = (rows // 4 == lax.rem(code // 2, 2)) & (lanes // 64 == lax.rem(code, 2))
                for s in range(SPECIES):
                    beside = fold_lanes(fold_rows(old_side[i, s] + side[i, s]))
                    coarse = old0[BOXES + cp, s]
                    both = coarse + own0[BOXES + cp, s]
                    across = old_side[BOXES + cp, s]
                    change = (rates_out[s] * coarse + rates_in[s] * across) - (
                        rates_out[s] * 0.5 * both + rates_in[s] * 0.125 * beside
                    )
                    coarse_new[cp, s] = coarse_new[cp, s] + jnp.where(here, sign * change, 0.0)

            return carry

        lax.fori_loop(0, BOXES, face, 0)

    @pl.when(a == 0)
    def _():
        cross(BELOW, old_west, west, down[0], up[0], -1.0)

    @pl.when(a == PAIRS - 1)
    def _():
        cross(ABOVE, old_east, east, up[0], down[0], 1.0)

    def cover(i, carry):
        t, col, half = [table[STRIDE * i + f] for f in (SLOT, COL, HALF)]
        start = pl.multiple_of(lax.rem(t, 2) * 80, 8)
        here = (rows // 4 == lax.rem(col, 2)) & (lanes // 64 == half)
        result = out[t // 2, pl.ds(start, 80), :].reshape(SPECIES, 2, 8, 128)
        for s in range(SPECIES):
            mean = 0.125 * fold_lanes(fold_rows(result[s, 0] + result[s, 1]))
            coarse_new[col // 2, s] = jnp.where(here, mean, coarse_new[col // 2, s])
        return carry

    lax.fori_loop(0, BOXES, cover, 0)
    for c in range(GY):
        for s in range(SPECIES):
            low = 4 * (c % 2)
            out[c, FINE_ROWS + 4 * s : FINE_ROWS + 4 * s + 4, :] = coarse_new[c // 2, s, low : low + 4, :]


def call(kernel, out_shape, operands, smem, scratch=(), out_smem=False):
    many = isinstance(out_shape, (list, tuple))
    out_spec = SMEM if out_smem else VMEM
    return pl.pallas_call(
        kernel,
        out_shape=out_shape,
        in_specs=[SMEM] * smem + [VMEM] * (len(operands) - smem),
        out_specs=[out_spec] * len(out_shape) if many else out_spec,
        scratch_shapes=list(scratch),
        compiler_params=pltpu.CompilerParams(vmem_limit_bytes=40 * 1024 * 1024),
    )(*operands)


def shift(value, step):
    size = GX * GY
    return lax.ppermute(value, ("gx", "gy"), [(i, (i + step) % size) for i in range(size)])


def swap(value):
    return lax.ppermute(value, "gy", [(i, i ^ 1) for i in range(GY)])


def spread(pieces):
    return lax.all_to_all(pieces, "gy", 0, 0, tiled=True)


def shards(coarse, fine, corners, ghost_source, courant, reaction):
    shape = lambda *dims: jax.ShapeDtypeStruct(dims, F32)
    pieces = shape(GY, PIECE_ROWS, 128)
    plane = shape(BOXES + PAIRS, SPECIES, 8, 128)
    tiles = shape(PAIRS, SPECIES, 8, 128)
    table = call(
        table_kernel,
        jax.ShapeDtypeStruct((BOXES * STRIDE,), jnp.int32),
        (corners.T, ghost_source.T),
        2,
        (pltpu.SMEM((3 * LIST_STRIDE,), jnp.int32), pltpu.SMEM((3 * ROW_SLOTS,), jnp.int32)),
        True,
    )
    received = spread(call(pack_kernel, pieces, (coarse, fine), 0))
    old0, old1 = call(compact_kernel, (plane, plane), (table, received), 1)
    old = (old0, old1, shift(old1, 2), shift(old0, -2), swap(old0), swap(old1))
    new0, new1, provisional = call(first_kernel, (plane, plane, tiles), (table, courant, reaction) + old, 3)
    new = (new0, new1, shift(new1, 2), shift(new0, -2), swap(new0), swap(new1))
    back = call(
        second_kernel,
        pieces,
        (table, courant, reaction) + old + new + (provisional,),
        3,
        (pltpu.VMEM((PAIRS, SPECIES, 8, 128), F32),),
    )
    return call(unpack_kernel, (shape(*coarse.shape), shape(*fine.shape)), (spread(back),), 0)


def solution(mesh):
    fine_spec = P(("gx", "gy"), None, None, None, None)
    coarse_spec = P(None, "gx", "gy", None)
    return jax.shard_map(
        shards,
        mesh=mesh,
        in_specs=(coarse_spec, fine_spec, P(), P(), P(), P()),
        out_specs=(coarse_spec, fine_spec),
        check_vma=False,
    )
```

```python
import functools

import jax
import jax.numpy as jnp
from jax import lax
from jax.experimental import pallas as pl
from jax.experimental.pallas import tpu as pltpu
from jax.sharding import PartitionSpec as P

PLANE_OF = (0, 1, 2, 3, 7, 6, 5, 4)
SPECIES = 5
GX = 16
GY = 16
BOXES = 8
PAIRS = 8
ROW_SLOTS = 32
FINE_ROWS = 160
PIECE_ROWS = 184
STRIDE = 16
LIST_STRIDE = 40
F32 = jnp.float32
SLOT, COL, HALF, WEST, EAST, SOUTH, NORTH, BOTTOM, TOP, OPEN_Y, BELOW, ABOVE = range(12)

VMEM = pl.BlockSpec(memory_space=pltpu.VMEM)
SMEM = pl.BlockSpec(memory_space=pltpu.SMEM)


def place():
    j = lax.axis_index("gy")
    q = j // 2
    return jnp.where(q < 4, q, 11 - q), lax.rem(j, 2)


def table_kernel(corners, sources, table, listed, ranks):
    row = lax.axis_index("gx")
    a, b = place()
    groups = [lax.rem(row + GX - 1 + r, GX) for r in range(3)]
    for r in range(3):

        def scan(t, count, r=r):
            live = corners[0, groups[r] * ROW_SLOTS + t] >= 0
            listed[r * LIST_STRIDE + count] = t
            ranks[r * ROW_SLOTS + t] = count
            return count + jnp.where(live, 1, 0)

        lax.fori_loop(0, ROW_SLOTS, scan, jnp.int32(0), unroll=8)

    def rank(r, source):
        found = ranks[r * ROW_SLOTS + lax.rem(jnp.maximum(source, 0), ROW_SLOTS)]
        return jnp.where(source >= 0, found, -1)

    for i in range(BOXES):
        t = listed[LIST_STRIDE + i]
        slot = groups[1] * ROW_SLOTS + t
        west, east, south, north, bottom, top = [sources[f, slot] for f in range(6)]
        base = STRIDE * i
        table[base + SLOT] = t
        table[base + COL] = corners[1, slot] // 16
        table[base + HALF] = corners[2, slot] // 128
        table[base + WEST] = jnp.where(a > 0, i, rank(0, west))
        table[base + EAST] = jnp.where(a < PAIRS - 1, i, rank(2, east))
        table[base + SOUTH] = jnp.where(b > 0, i, rank(1, south))
        table[base + NORTH] = jnp.where(b < 1, i, rank(1, north))
        table[base + BOTTOM] = rank(1, bottom)
        table[base + TOP] = rank(1, top)
        table[base + OPEN_Y] = jnp.where(jnp.where(b > 0, south, north) < 0, 1, 0)
        for r, face, field in ((0, 1, BELOW), (2, 0, ABOVE)):
            beside = groups[r] * ROW_SLOTS + listed[r * LIST_STRIDE + i]
            where = corners[1, beside] // 16 * 2 + corners[2, beside] // 128
            table[base + field] = jnp.where(sources[face, beside] < 0, where, -1)
        for field in range(12, STRIDE):
            table[base + field] = 0


def pack_kernel(coarse, fine, out):
    for j in range(GY):
        a, b = PLANE_OF[j // 2], j % 2
        part = fine[:, :, 2 * a : 2 * a + 2, 8 * b : 8 * b + 8, :]
        out[j, :FINE_ROWS, :] = part.reshape(FINE_ROWS, 128)
        for s in range(SPECIES):
            out[j, FINE_ROWS + 4 * s : FINE_ROWS + 4 * s + 4, :] = coarse[s, a, 4 * b : 4 * b + 4, :]
        out[j, FINE_ROWS + 20 :, :] = jnp.zeros((4, 128), F32)


def unpack_kernel(received, coarse, fine):
    for j in range(GY):
        a, b = PLANE_OF[j // 2], j % 2
        part = received[j, :FINE_ROWS, :].reshape(2, SPECIES, 2, 8, 128)
        fine[:, :, 2 * a : 2 * a + 2, 8 * b : 8 * b + 8, :] = part
        for s in range(SPECIES):
            coarse[s, a, 4 * b : 4 * b + 4, :] = received[j, FINE_ROWS + 4 * s : FINE_ROWS + 4 * s + 4, :]


def compact_kernel(table, received, plane0, plane1):
    for i in range(BOXES):
        t = table[STRIDE * i + SLOT]
        start = pl.multiple_of(lax.rem(t, 2) * 80, 8)
        box = received[t // 2, pl.ds(start, 80), :].reshape(SPECIES, 2, 8, 128)
        plane0[i] = box[:, 0]
        plane1[i] = box[:, 1]
    for c in range(GY):
        for s in range(SPECIES):
            rows = received[c, FINE_ROWS + 4 * s : FINE_ROWS + 4 * s + 4, :]
            low = 4 * (c % 2)
            plane0[BOXES + c // 2, s, low : low + 4, :] = rows
            plane1[BOXES + c // 2, s, low : low + 4, :] = rows


def iotas():
    return lax.broadcasted_iota(jnp.int32, (8, 128), 0), lax.broadcasted_iota(jnp.int32, (8, 128), 1)


def take(tile, index, axis):
    return jnp.take_along_axis(tile, index, axis=axis, mode="promise_in_bounds")


def turn(tile, shift, axis):
    return pltpu.roll(tile, shift % tile.shape[axis], axis)


def rates_of(courant):
    up = [[jnp.maximum(courant[d, s], 0.0) for s in range(SPECIES)] for d in range(3)]
    down = [[jnp.minimum(courant[d, s], 0.0) for s in range(SPECIES)] for d in range(3)]
    return up, down


def moved(value, sides, up, down, reaction, others, s, factor):
    total = value
    for d, (lower, upper) in enumerate(sides):
        total = total - (up[d][s] * (value - lower) + down[d][s] * (upper - value))
    mixing = reaction[s, 0] * others[0]
    for e in range(1, SPECIES):
        mixing = mixing + reaction[s, e] * others[e]
    return total + factor * mixing


def fine_step(i, table, own, west, east, peer, up, down, reaction, write):
    rows, lanes = iotas()
    _, b = place()
    field = lambda f: table[STRIDE * i + f]
    col, half = field(COL), field(HALF)
    pair = BOXES + col // 2
    row_index = 4 * lax.rem(col, 2) + rows // 2
    lane_index = 64 * half + lanes // 2
    outer = lax.rem(jnp.where(b > 0, col + 1, col + GY - 1), GY)
    outer_row = 4 * lax.rem(outer, 2) + jnp.where(b > 0, 0, 3)
    found = [field(f) for f in (WEST, EAST, SOUTH, NORTH, BOTTOM, TOP)]
    there = [source >= 0 for source in found]
    at = [jnp.maximum(source, 0) for source in found]
    values = [[own[xi][i, s] for s in range(SPECIES)] for xi in range(2)]
    for s in range(SPECIES):
        beside = take(own[0][pair, s], row_index, 0)
        across = turn(beside, 64, 1)
        below = jnp.where(half > 0, across, 0.0)
        above = jnp.where(half > 0, 0.0, across)
        coarse_west = take(take(west[pair, s], row_index, 0), lane_index, 1)
        coarse_east = take(take(east[pair, s], row_index, 0), lane_index, 1)
        edge = jnp.broadcast_to(peer[0][BOXES + outer // 2, s, pl.ds(outer_row, 1), :], (8, 128))
        edge = take(edge, lane_index, 1)
        ghost_west = jnp.where(there[0], west[at[0], s], coarse_west)
        ghost_east = jnp.where(there[1], east[at[1], s], coarse_east)
        for xi in range(2):
            value = values[xi][s]
            south = jnp.where(there[2], peer[xi][at[2], s], edge)
            north = jnp.where(there[3], peer[xi][at[3], s], edge)
            bottom = jnp.where(there[4], own[xi][at[4], s], below)
            top = jnp.where(there[5], own[xi][at[5], s], above)
            sides = (
                (ghost_west, values[1][s]) if xi == 0 else (values[0][s], ghost_east),
                (
                    turn(jnp.where(rows == 7, south, value), 1, 0),
                    turn(jnp.where(rows == 0, north, value), -1, 0),
                ),
                (
                    turn(jnp.where(lanes == 127, bottom, value), 1, 1),
                    turn(jnp.where(lanes == 0, top, value), -1, 1),
                ),
            )
            write(xi, s, moved(value, sides, up, down, reaction, values[xi], s, 0.5))


def first_kernel(table, courant, reaction, own0, own1, west, east, peer0, peer1, new0, new1, provisional):
    rows, lanes = iotas()
    _, b = place()
    up, down = rates_of(courant)
    quarter = lax.rem(rows, 4)

    def coarse_pair(cp, carry):
        before = BOXES + lax.rem(cp + PAIRS - 1, PAIRS)
        after = BOXES + lax.rem(cp + 1, PAIRS)
        here = BOXES + cp
        values = [own0[here, s] for s in range(SPECIES)]
        for s in range(SPECIES):
            value = values[s]
            peer = peer0[here, s]
            outer_low = turn(jnp.where(rows == 7, peer0[before, s], peer), 1, 0)
            outer_high = turn(jnp.where(rows == 0, peer0[after, s], peer), -1, 0)
            south = jnp.where(b > 0, turn(peer, 5, 0), outer_low)
            north = jnp.where(b > 0, outer_high, turn(peer, 3, 0))
            sides = (
                (west[here, s], east[here, s]),
                (
                    jnp.where(quarter == 0, south, turn(value, 1, 0)),
                    jnp.where(quarter == 3, north, turn(value, -1, 0)),
                ),
                (
                    turn(jnp.where(lanes == 127, 0.0, value), 1, 1),
                    turn(jnp.where(lanes == 0, 0.0, value), -1, 1),
                ),
            )
            result = moved(value, sides, up, down, reaction, values, s, 1.0)
            provisional[cp, s] = result
            middle = 0.5 * (value + result)
            new0[here, s] = middle
            new1[here, s] = middle
        return carry

    lax.fori_loop(0, PAIRS, coarse_pair, 0)
    new = (new0, new1)

    def box(i, carry):
        def write(xi, s, result):
            new[xi][i, s] = result

        fine_step(i, table, (own0, own1), west, east, (peer0, peer1), up, down, reaction, write)
        return carry

    lax.fori_loop(0, BOXES, box, 0)


def second_kernel(
    table, courant, reaction, old0, old1, old_west, old_east, old_peer0, old_peer1,
    own0, own1, west, east, peer0, peer1, provisional, out, coarse_new,
):
    rows, lanes = iotas()
    a, b = place()
    up, down = rates_of(courant)
    row_fold = lax.rem(2 * rows, 8)
    lane_fold = lax.rem(2 * lanes, 128)
    fold_rows = lambda tile: take(tile + turn(tile, -1, 0), row_fold, 0)
    fold_lanes = lambda tile: take(tile + turn(tile, -1, 1), lane_fold, 1)
    coarse_new[...] = provisional[...]

    def clear(j, carry):
        out[j, :FINE_ROWS, :] = jnp.zeros((FINE_ROWS, 128), F32)
        out[j, FINE_ROWS + 20 :, :] = jnp.zeros((4, 128), F32)
        return carry

    lax.fori_loop(0, GY, clear, 0)

    def box(i, carry):
        field = lambda f: table[STRIDE * i + f]
        t, col, half = field(SLOT), field(COL), field(HALF)
        start = lax.rem(t, 2) * 80

        def write(xi, s, result):
            out[t // 2, pl.ds(pl.multiple_of(start + (2 * s + xi) * 8, 8), 8), :] = result

        fine_step(i, table, (own0, own1), west, east, (peer0, peer1), up, down, reaction, write)

        cp = col // 2
        pair = BOXES + cp
        in_rows = rows // 4 == lax.rem(col, 2)
        is_high = half > 0
        open_z = jnp.where(is_high, field(BOTTOM), field(TOP)) < 0
        outer = lax.rem(jnp.where(b > 0, col + GY - 1, col + 1), GY)
        outer_row = 4 * lax.rem(outer, 2) + jnp.where(b > 0, 3, 0)
        inner_row = 4 * lax.rem(col, 2) + jnp.where(b > 0, 0, 3)
        outer_pair = outer // 2
        fine_row = jnp.where(b > 0, 0, 7)
        in_half = lanes[:1] // 64 == half
        for s in range(SPECIES):
            coarse = old0[pair, s]
            both = coarse + own0[pair, s]
            total = fold_rows((old0[i, s] + old1[i, s]) + (own0[i, s] + own1[i, s]))
            beside = jnp.where(is_high, turn(total, 63, 1), turn(total, 65, 1))
            across = jnp.where(is_high, turn(coarse, -1, 1), turn(coarse, 1, 1))
            rate_out = jnp.where(is_high, up[2][s], down[2][s])
            rate_in = jnp.where(is_high, down[2][s], up[2][s])
            change = (rate_out * coarse + rate_in * across) - (rate_out * 0.5 * both + rate_in * 0.125 * beside)
            change = jnp.where(is_high, change, -change)
            here = in_rows & (lanes == jnp.where(is_high, 63, 64)) & open_z
            coarse_new[cp, s] = coarse_new[cp, s] + jnp.where(here, change, 0.0)

            line = pl.ds(fine_row, 1)
            total = (old_peer0[i, s, line, :] + old_peer1[i, s, line, :]) + (
                peer0[i, s, line, :] + peer1[i, s, line, :]
            )
            beside = fold_lanes(jnp.broadcast_to(total, (8, 128)))[:1]
            at = pl.ds(outer_row, 1)
            coarse = old0[BOXES + outer_pair, s, at, :]
            both = coarse + own0[BOXES + outer_pair, s, at, :]
            across = old_peer0[pair, s, pl.ds(inner_row, 1), :]
            rate_out = jnp.where(b > 0, up[1][s], down[1][s])
            rate_in = jnp.where(b > 0, down[1][s], up[1][s])
            change = (rate_out * coarse + rate_in * across) - (rate_out * 0.5 * both + rate_in * 0.125 * beside)
            change = jnp.where(b > 0, change, -change)
            here = in_half & (field(OPEN_Y) > 0)
            coarse_new[outer_pair, s, at, :] = coarse_new[outer_pair, s, at, :] + jnp.where(here, change, 0.0)
        return carry

    lax.fori_loop(0, BOXES, box, 0)

    def cross(name, old_side, side, rates_out, rates_in, sign):
        def face(i, carry):
            code = table[STRIDE * i + name]

            @pl.when(code >= 0)
            def _():
                cp = code // 4
                here = (rows // 4 == lax.rem(code // 2, 2)) & (lanes // 64 == lax.rem(code, 2))
                for s in range(SPECIES):
                    beside = fold_lanes(fold_rows(old_side[i, s] + side[i, s]))
                    coarse = old0[BOXES + cp, s]
                    both = coarse + own0[BOXES + cp, s]
                    across = old_side[BOXES + cp, s]
                    change = (rates_out[s] * coarse + rates_in[s] * across) - (
                        rates_out[s] * 0.5 * both + rates_in[s] * 0.125 * beside
                    )
                    coarse_new[cp, s] = coarse_new[cp, s] + jnp.where(here, sign * change, 0.0)

            return carry

        lax.fori_loop(0, BOXES, face, 0)

    @pl.when(a == 0)
    def _():
        cross(BELOW, old_west, west, down[0], up[0], -1.0)

    @pl.when(a == PAIRS - 1)
    def _():
        cross(ABOVE, old_east, east, up[0], down[0], 1.0)

    def cover(i, carry):
        t, col, half = [table[STRIDE * i + f] for f in (SLOT, COL, HALF)]
        start = pl.multiple_of(lax.rem(t, 2) * 80, 8)
        here = (rows // 4 == lax.rem(col, 2)) & (lanes // 64 == half)
        result = out[t // 2, pl.ds(start, 80), :].reshape(SPECIES, 2, 8, 128)
        for s in range(SPECIES):
            mean = 0.125 * fold_lanes(fold_rows(result[s, 0] + result[s, 1]))
            coarse_new[col // 2, s] = jnp.where(here, mean, coarse_new[col // 2, s])
        return carry

    lax.fori_loop(0, BOXES, cover, 0)
    for c in range(GY):
        for s in range(SPECIES):
            low = 4 * (c % 2)
            out[c, FINE_ROWS + 4 * s : FINE_ROWS + 4 * s + 4, :] = coarse_new[c // 2, s, low : low + 4, :]


def call(kernel, out_shape, operands, smem, scratch=(), out_smem=False):
    many = isinstance(out_shape, (list, tuple))
    out_spec = SMEM if out_smem else VMEM
    return pl.pallas_call(
        kernel,
        out_shape=out_shape,
        in_specs=[SMEM] * smem + [VMEM] * (len(operands) - smem),
        out_specs=[out_spec] * len(out_shape) if many else out_spec,
        scratch_shapes=list(scratch),
        compiler_params=pltpu.CompilerParams(vmem_limit_bytes=40 * 1024 * 1024),
    )(*operands)


def shift(value, step):
    size = GX * PAIRS
    device = lambda n, b: n // PAIRS * GY + 2 * PLANE_OF.index(n % PAIRS) + b
    pairs = [(device(n, b), device((n + step) % size, b)) for n in range(size) for b in range(2)]
    return lax.ppermute(value, ("gx", "gy"), pairs)


def swap(value):
    return lax.ppermute(value, "gy", [(i, i ^ 1) for i in range(GY)])


def spread(pieces):
    return lax.all_to_all(pieces, "gy", 0, 0, tiled=True)


def shards(coarse, fine, corners, ghost_source, courant, reaction):
    shape = lambda *dims: jax.ShapeDtypeStruct(dims, F32)
    pieces = shape(GY, PIECE_ROWS, 128)
    plane = shape(BOXES + PAIRS, SPECIES, 8, 128)
    tiles = shape(PAIRS, SPECIES, 8, 128)
    table = call(
        table_kernel,
        jax.ShapeDtypeStruct((BOXES * STRIDE,), jnp.int32),
        (corners.T, ghost_source.T),
        2,
        (pltpu.SMEM((3 * LIST_STRIDE,), jnp.int32), pltpu.SMEM((3 * ROW_SLOTS,), jnp.int32)),
        True,
    )
    received = spread(call(pack_kernel, pieces, (coarse, fine), 0))
    old0, old1 = call(compact_kernel, (plane, plane), (table, received), 1)
    old = (old0, old1, shift(old1, 1), shift(old0, -1), swap(old0), swap(old1))
    new0, new1, provisional = call(first_kernel, (plane, plane, tiles), (table, courant, reaction) + old, 3)
    new = (new0, new1, shift(new1, 1), shift(new0, -1), swap(new0), swap(new1))
    back = call(
        second_kernel,
        pieces,
        (table, courant, reaction) + old + new + (provisional,),
        3,
        (pltpu.VMEM((PAIRS, SPECIES, 8, 128), F32),),
    )
    return call(unpack_kernel, (shape(*coarse.shape), shape(*fine.shape)), (spread(back),), 0)


def solution(mesh):
    fine_spec = P(("gx", "gy"), None, None, None, None)
    coarse_spec = P(None, "gx", "gy", None)
    return jax.shard_map(
        shards,
        mesh=mesh,
        in_specs=(coarse_spec, fine_spec, P(), P(), P(), P()),
        out_specs=(coarse_spec, fine_spec),
        check_vma=False,
    )
```

```python
import jax
import jax.numpy as jnp
from jax import lax
from jax.experimental import pallas as pl
from jax.experimental.pallas import tpu as pltpu
from jax.sharding import PartitionSpec as P

CHIP_OF = (0, 1, 2, 3, 7, 6, 5, 4)
SPECIES = 5
GX = 16
GY = 16
BOXES = 8
CHUNKS = 8
QUADS = 4
ROW_SLOTS = 32
FINE_ROWS = 160
PIECE_ROWS = 184
EDGE_ROWS = 80
EDGE_COARSE = 40
STRIDE = 16
LIST_STRIDE = 40
F32 = jnp.float32
SLOT, COL, HALF, WEST, EAST, SOUTH, NORTH, BOTTOM, TOP, OPEN_Z = range(10)
BESIDE = BOXES * STRIDE
TABLE = BESIDE + 2 * GY

VMEM = pl.BlockSpec(memory_space=pltpu.VMEM)
SMEM = pl.BlockSpec(memory_space=pltpu.SMEM)


def device_of(m, part, row):
    turned = (GY // 2) * (row % 2) if isinstance(row, int) else (GY // 2) * lax.rem(row, 2)
    place = 2 * CHIP_OF[m] + part + turned
    return place % GY if isinstance(row, int) else lax.rem(place, GY)


def chunk():
    turned = (GY // 2) * lax.rem(lax.axis_index("gx"), 2)
    j = lax.rem(lax.axis_index("gy") + turned, GY)
    q = j // 2
    return jnp.where(q < 4, q, 11 - q), lax.rem(j, 2)


def table_kernel(corners, sources, table, listed, ranks):
    row = lax.axis_index("gx")
    m, part = chunk()
    groups = [lax.rem(row + GX - 1 + r, GX) for r in range(3)]
    for r in range(3):

        def scan(t, count, r=r):
            live = corners[0, groups[r] * ROW_SLOTS + t] >= 0
            listed[r * LIST_STRIDE + count] = t
            ranks[r * ROW_SLOTS + t] = count
            return count + jnp.where(live, 1, 0)

        lax.fori_loop(0, ROW_SLOTS, scan, jnp.int32(0), unroll=8)

    def rank(r, source):
        found = ranks[r * ROW_SLOTS + lax.rem(jnp.maximum(source, 0), ROW_SLOTS)]
        return jnp.where(source >= 0, found, -1)

    for i in range(BOXES):
        t = listed[LIST_STRIDE + i]
        slot = groups[1] * ROW_SLOTS + t
        west, east, south, north, bottom, top = [sources[f, slot] for f in range(6)]
        half = corners[2, slot] // 128
        base = STRIDE * i
        table[base + SLOT] = t
        table[base + COL] = corners[1, slot] // 16
        table[base + HALF] = half
        table[base + WEST] = jnp.where(part > 0, i, rank(0, west))
        table[base + EAST] = jnp.where(part > 0, rank(2, east), i)
        table[base + SOUTH] = rank(1, south)
        table[base + NORTH] = rank(1, north)
        table[base + BOTTOM] = jnp.where(m > 0, i, rank(1, bottom))
        table[base + TOP] = jnp.where(m < CHUNKS - 1, i, rank(1, top))
        table[base + OPEN_Z] = jnp.where(jnp.where(half > 0, bottom, top) < 0, 1, 0)
        for field in range(10, STRIDE):
            table[base + field] = 0
    for k in range(2 * GY):
        table[BESIDE + k] = -1
    side = jnp.where(part > 0, 2, 0)
    face = jnp.where(part > 0, 0, 1)
    group = jnp.where(part > 0, groups[2], groups[0])
    for i in range(BOXES):
        beside = group * ROW_SLOTS + listed[side * LIST_STRIDE + i]
        spot = corners[1, beside] // 16 * 2 + corners[2, beside] // 128
        table[BESIDE + spot] = jnp.where(sources[face, beside] < 0, i, -1)


def pack_kernel(coarse, fine, out):
    row = lax.axis_index("gx")
    for k in range(2):
        for s in range(SPECIES):
            turned = fine[k, s].reshape(256, 128).T
            at = (k * SPECIES + s) * 16
            for m in range(CHUNKS):
                for part in range(2):
                    block = turned[16 * m : 16 * m + 16, 128 * part : 128 * part + 128]
                    out[device_of(m, part, row), at : at + 16, :] = block
    for p in range(3):
        at = FINE_ROWS + 8 * p
        for part in range(2):
            blocks = []
            for s in (2 * p, 2 * p + 1):
                block = coarse[min(s, 4), 4 * part : 4 * part + 4].reshape(32, 128)
                blocks += [block, pltpu.roll(block, 64, 1)]
            turned = jnp.concatenate(blocks).T
            for m in range(CHUNKS):
                out[device_of(m, part, row), at : at + 8, :] = turned[8 * m : 8 * m + 8]


def unpack_kernel(received, coarse, fine):
    row = lax.axis_index("gx")
    for k in range(2):
        for s in range(SPECIES):
            at = (k * SPECIES + s) * 16
            for part in range(2):
                rows = [received[device_of(m, part, row), at : at + 16, :] for m in range(CHUNKS)]
                fine[k, s, 8 * part : 8 * part + 8] = jnp.concatenate(rows).T.reshape(8, 16, 128)
    left = lax.broadcasted_iota(jnp.int32, (32, 128), 1) < 64
    for p in range(3):
        at = FINE_ROWS + 8 * p
        rows = [received[device_of(m, part, row), at : at + 8, :] for part in range(2) for m in range(CHUNKS)]
        block = jnp.concatenate(rows).T
        for s in range(2 * p, min(2 * p + 2, SPECIES)):
            at_s = 64 * (s - 2 * p)
            low, high = block[at_s : at_s + 32], block[at_s + 32 : at_s + 64]
            coarse[s, 0:4] = jnp.where(left, low, pltpu.roll(high, 64, 1)).reshape(4, 8, 128)
            coarse[s, 4:8] = jnp.where(left, pltpu.roll(low, 64, 1), high).reshape(4, 8, 128)


def iotas():
    return lax.broadcasted_iota(jnp.int32, (8, 128), 0), lax.broadcasted_iota(jnp.int32, (8, 128), 1)


def take(tile, index, axis):
    return jnp.take_along_axis(tile, index, axis=axis, mode="promise_in_bounds")


def turn(tile, shift, axis):
    return pltpu.roll(tile, shift % tile.shape[axis], axis)


def line(ref, index):
    return jnp.broadcast_to(ref[pl.ds(index, 1), :], (8, 128))


def edges(fine, coarse, up_out, down_out, outer_out, inner_out):
    _, lanes = iotas()
    _, part = chunk()
    last = part > 0
    for s in range(SPECIES):
        up_out[8 * s : 8 * s + 8, :] = fine[1][:, s, 7, :]
        down_out[8 * s : 8 * s + 8, :] = fine[0][:, s, 0, :]
        for h in range(2):
            at = EDGE_COARSE + (2 * s + h) * QUADS
            up_out[at : at + QUADS, :] = coarse[:, s, h, 7, :]
            down_out[at : at + QUADS, :] = coarse[:, s, h, 0, :]
        column = 32 * lax.rem(lanes // 8, 4) + lax.rem(lanes, 8)
        for r in range(2):
            faces = [jnp.zeros((8, 128), F32)] * 4
            for i in range(BOXES):
                here = lanes // 16 == i
                tile = fine[r][i, s]
                faces[0] = jnp.where(here, turn(tile, 16 * i, 1), faces[0])
                faces[1] = jnp.where(here, turn(tile, 16 * i + 16, 1), faces[1])
            for q in range(QUADS):
                here = lanes // 32 == q
                tile = coarse[q, s, r]
                faces[2] = jnp.where(here, take(tile, column, 1), faces[2])
                faces[3] = jnp.where(here, take(tile, column + 24, 1), faces[3])
            outer_out[0, s, r] = jnp.where(last, faces[1], faces[0])
            inner_out[0, s, r] = jnp.where(last, faces[0], faces[1])
            outer_out[1, s, r] = jnp.where(last, faces[3], faces[2])
            inner_out[1, s, r] = jnp.where(last, faces[2], faces[3])


def compact_kernel(table, received, fine0, fine1, coarse, up_out, down_out, outer_out, inner_out):
    _, lanes = iotas()
    for i in range(BOXES):
        t = table[STRIDE * i + SLOT]
        start = pl.multiple_of(lax.rem(t, 2) * 80, 8)
        box = received[t // 2, pl.ds(start, 80), :].reshape(SPECIES, 2, 8, 128)
        fine0[i] = box[:, 0]
        fine1[i] = box[:, 1]
    for q in range(QUADS):
        for p in range(3):
            at = FINE_ROWS + 8 * p
            tiles = [received[4 * q + o, at : at + 8, :] for o in range(4)]
            for k in range(4 if p < 2 else 2):
                tile = turn(tiles[0], -32 * k, 1)
                for o in range(1, 4):
                    tile = jnp.where(lanes // 32 == o, turn(tiles[o], 32 * (o - k), 1), tile)
                coarse[q, 2 * p + k // 2, k % 2] = tile
    edges((fine0, fine1), coarse, up_out, down_out, outer_out, inner_out)


def signs_of(courant):
    goes_up = [[courant[d, s] >= 0.0 for s in range(SPECIES)] for d in range(3)]
    size = [[jnp.abs(courant[d, s]) for s in range(SPECIES)] for d in range(3)]
    return goes_up, size


def weights_of(size, reaction, factor):
    weights = [[factor * reaction[s, e] for e in range(SPECIES)] for s in range(SPECIES)]
    for s in range(SPECIES):
        weights[s][s] = weights[s][s] + (1.0 - size[0][s] - size[1][s] - size[2][s])
    return weights


def moved(values, upwind, size, weights, s):
    total = weights[s][0] * values[0]
    for e in range(1, SPECIES):
        total = total + weights[s][e] * values[e]
    for d in range(3):
        total = total + size[d][s] * upwind[d]
    return total


def ends(table, below, above, ghosts):
    _, lanes = iotas()
    m, _ = chunk()
    ghosts[:EDGE_COARSE, :] = below[:EDGE_COARSE, :]
    ghosts[EDGE_COARSE:, :] = above[:EDGE_COARSE, :]

    def replace(side, source, name, high):
        for i in range(BOXES):
            col, half, found = [table[STRIDE * i + f] for f in (COL, HALF, name)]
            inside = 32 * lax.rem(col, 4) + 8 * (lanes // 32) + lax.rem(lanes, 16) // 2
            for s in range(SPECIES):
                other = take(line(source, EDGE_COARSE + (2 * s + side) * QUADS + col // 4), inside, 1)
                other = jnp.where(half == high, other, 0.0)
                ghost = jnp.where(found >= 0, line(source, 8 * s + jnp.maximum(found, 0)), other)
                at = EDGE_COARSE * side + 8 * s + i
                ghosts[at : at + 1, :] = ghost[:1]

    @pl.when(m == 0)
    def _():
        replace(0, below, BOTTOM, 1)

    @pl.when(m == CHUNKS - 1)
    def _():
        replace(1, above, TOP, 0)


def fine_step(i, table, fine, coarse, ghosts, sides, goes_up, size, weights, write):
    rows, lanes = iotas()
    field = lambda f: table[STRIDE * i + f]
    col, half = field(COL), field(HALF)
    lower_col, upper_col = lax.rem(col + GY - 1, GY), lax.rem(col + 1, GY)
    y = lax.rem(lanes, 16)
    found = [field(f) for f in (WEST, EAST, SOUTH, NORTH)]
    there = [source >= 0 for source in found]
    at = [jnp.maximum(source, 0) for source in found]
    lane_x = [jnp.where(there[f], 16 * at[f] + y, 8 * col + y // 2) for f in range(2)]
    own_x, line_x = lanes - y, 8 * (lanes // 32)
    lane_y = [
        jnp.where(there[2], own_x + 15, 32 * lax.rem(lower_col, 4) + line_x + 7),
        jnp.where(there[3], own_x, 32 * lax.rem(upper_col, 4) + line_x),
    ]
    row_of = [[jnp.where(is_there, rows, 4 * r + rows // 2) for is_there in there] for r in range(2)]
    kind = [jnp.where(is_there, 0, 1) for is_there in there]
    values = [[fine[r][i, s] for s in range(SPECIES)] for r in range(2)]
    for s in range(SPECIES):
        up_x, up_y, up_z = [goes_up[d][s] for d in range(3)]
        shift_x, edge_x = jnp.where(up_x, 16, 112), lanes // 16 == jnp.where(up_x, 0, 7)
        shift_y, edge_y = jnp.where(up_y, 1, 127), y == jnp.where(up_y, 0, 15)
        shift_z, edge_z = jnp.where(up_z, 1, 7), rows == jnp.where(up_z, 0, 7)
        is_there = jnp.where(up_y, found[2], found[3]) >= 0
        box_y = jnp.where(up_y, at[2], at[3])
        quad_y = jnp.where(up_y, lower_col, upper_col) // 4
        coarse_y = coarse[quad_y, s, half]
        index_x = jnp.where(up_x, lane_x[0], lane_x[1])
        index_y = jnp.where(up_y, lane_y[0], lane_y[1])

        low, high = values[0][s], values[1][s]
        first = pltpu.roll(jnp.where(up_z, low, high), shift_z, 0)
        second = pltpu.roll(jnp.where(up_z, high, low), shift_z, 0)
        second = jnp.where(edge_z, first, second)
        first = jnp.where(edge_z, line(ghosts, jnp.where(up_z, 0, EDGE_COARSE) + 8 * s + i), first)
        from_z = (jnp.where(up_z, first, second), jnp.where(up_z, second, first))

        for r in range(2):
            value = values[r][s]
            west = sides(0, kind[0], s, jnp.where(there[0], r, half))
            east = sides(1, kind[1], s, jnp.where(there[1], r, half))
            ghost = take(jnp.where(up_x, west, east), jnp.where(up_x, row_of[r][0], row_of[r][1]), 0)
            ghost = take(ghost, index_x, 1)
            from_x = jnp.where(edge_x, ghost, pltpu.roll(value, shift_x, 1))
            ghost = take(
                jnp.where(is_there, fine[r][box_y, s], coarse_y), jnp.where(up_y, row_of[r][2], row_of[r][3]), 0
            )
            ghost = take(ghost, index_y, 1)
            from_y = jnp.where(edge_y, ghost, pltpu.roll(value, shift_y, 1))
            write(r, s, moved(values[r], (from_x, from_y, from_z[r]), size, weights, s))


def sides_of(outer, inner):
    _, part = chunk()

    def pick(side, kind, s, at):
        one, other = outer[kind, s, at], inner[kind, s, at]
        return jnp.where(part == side, one, other)

    return pick


def first_kernel(
    table, courant, reaction, fine0, fine1, coarse, below, above, outer, inner,
    new0, new1, middle, provisional, up_out, down_out, outer_out, inner_out, ghosts,
):
    rows, lanes = iotas()
    m, _ = chunk()
    goes_up, size = signs_of(courant)
    weights = weights_of(size, reaction, 1.0)
    x = lax.rem(lanes // 8, 4)
    y = lax.rem(lanes, 8)
    sides = sides_of(outer, inner)
    ends(table, below, above, ghosts)

    def coarse_quad(q, carry):
        before, after = lax.rem(q + QUADS - 1, QUADS), lax.rem(q + 1, QUADS)
        values = [[coarse[q, s, h] for s in range(SPECIES)] for h in range(2)]
        column = 8 * (4 * q + lanes // 32) + y
        for s in range(SPECIES):
            up_x, up_y, up_z = [goes_up[d][s] for d in range(3)]
            at = [EDGE_COARSE + (2 * s + h) * QUADS + q for h in range(2)]
            lows, highs = [line(below, k) for k in at], [line(above, k) for k in at]
            bottoms = (jnp.where(m > 0, lows[0], 0.0), jnp.where(m > 0, lows[1], lows[0]))
            tops = (
                jnp.where(m < CHUNKS - 1, highs[0], highs[1]),
                jnp.where(m < CHUNKS - 1, highs[1], 0.0),
            )
            for h in range(2):
                value = values[h][s]
                ghost = take(jnp.where(up_x, sides(0, 1, s, h), sides(1, 1, s, h)), column, 1)
                from_x = pltpu.roll(value, jnp.where(up_x, 8, 120), 1)
                from_x = jnp.where(x == jnp.where(up_x, 0, 3), ghost, from_x)

                beside = coarse[jnp.where(up_y, before, after), s, h]
                ghost = jnp.where(lanes // 32 == jnp.where(up_y, 3, 0), beside, value)
                ghost = pltpu.roll(ghost, jnp.where(up_y, 25, 103), 1)
                from_y = pltpu.roll(value, jnp.where(up_y, 1, 127), 1)
                from_y = jnp.where(y == jnp.where(up_y, 0, 7), ghost, from_y)

                ghost = jnp.where(up_z, bottoms[h], tops[h])
                from_z = pltpu.roll(value, jnp.where(up_z, 1, 7), 0)
                from_z = jnp.where(rows == jnp.where(up_z, 0, 7), ghost, from_z)

                result = moved(values[h], (from_x, from_y, from_z), size, weights, s)
                provisional[q, s, h] = result
                middle[q, s, h] = 0.5 * (value + result)
        return carry

    lax.fori_loop(0, QUADS, coarse_quad, 0)
    new = (new0, new1)
    weights = weights_of(size, reaction, 0.5)

    def box(i, carry):
        def write(r, s, result):
            new[r][i, s] = result

        fine_step(i, table, (fine0, fine1), coarse, ghosts, sides, goes_up, size, weights, write)
        return carry

    lax.fori_loop(0, BOXES, box, 0)
    edges(new, middle, up_out, down_out, outer_out, inner_out)


def second_kernel(
    table, courant, reaction, old0, old1, coarse, old_below, old_above, old_outer, old_inner,
    fine0, fine1, middle, below, above, outer, inner, provisional, out,
    coarse_new, ghosts, result0, result1, folded0, folded1,
):
    rows, lanes = iotas()
    m, part = chunk()
    goes_up, size = signs_of(courant)
    weights = weights_of(size, reaction, 0.5)
    up = [[jnp.maximum(courant[d, s], 0.0) for s in range(SPECIES)] for d in range(3)]
    down = [[jnp.minimum(courant[d, s], 0.0) for s in range(SPECIES)] for d in range(3)]
    x = lax.rem(lanes // 8, 4)
    y = lax.rem(lanes, 8)
    group = lanes // 32
    ends(table, below, above, ghosts)
    coarse_new[...] = provisional[...]

    def clear(j, carry):
        out[j, :FINE_ROWS, :] = jnp.zeros((FINE_ROWS, 128), F32)
        return carry

    lax.fori_loop(0, GY, clear, 0)
    sides = sides_of(outer, inner)

    def box_step(i, carry):
        t = table[STRIDE * i + SLOT]
        start = lax.rem(t, 2) * 80

        def write(r, s, result):
            out[t // 2, pl.ds(pl.multiple_of(start + (2 * s + r) * 8, 8), 8), :] = result
            (result0, result1)[r][i, s] = result

        fine_step(i, table, (fine0, fine1), middle, ghosts, sides, goes_up, size, weights, write)
        return carry

    lax.fori_loop(0, BOXES, box_step, 0)

    taken = lax.broadcasted_iota(jnp.int32, (128, 128), 0)
    given = lax.broadcasted_iota(jnp.int32, (128, 128), 1)
    given_y, fine_y = lax.rem(given, 8), lax.rem(taken, 16)
    same_x = lax.rem(given // 8, 4) == taken // 32

    def summing(rule):
        return jnp.where(same_x & rule, 1.0, 0.0).astype(F32)

    def product(values, matrix):
        return jnp.dot(values, matrix, precision=lax.Precision.HIGHEST, preferred_element_type=F32)

    def fold(tiles, matrix):
        for refs, folded in zip(tiles, (folded0, folded1)):
            pairs = sum(
                ref.reshape(BOXES * SPECIES * 8, 128)[pl.ds(odd, BOXES * SPECIES * 4, stride=2), :]
                for ref in refs
                for odd in range(2)
            )
            folded[...] = product(pairs, matrix)

    def folded_tile(i, s):
        at = pl.ds((i * SPECIES + s) * 4, 4)
        return jnp.concatenate([folded0[at, :], folded1[at, :]])

    def add(q, s, h, where, change):
        coarse_new[q, s, h] = coarse_new[q, s, h] + jnp.where(where, change, 0.0)

    def change_of(here, across, both, beside, rate_out, rate_in, sign):
        return sign * (rate_out * (here - 0.5 * both) + rate_in * (across - 0.125 * beside))

    edge_rule = ((fine_y == 0) & (given_y == 7)) | ((fine_y == 15) & (given_y == 0))
    fold(((old0, fine0), (old1, fine1)), summing(edge_rule))

    def open_y(i, carry):
        col, half, south, north = [table[STRIDE * i + f] for f in (COL, HALF, SOUTH, NORTH)]
        south_col, north_col = lax.rem(col + GY - 1, GY), lax.rem(col + 1, GY)
        south_quad, north_quad = south_col // 4, north_col // 4
        at_south = (group == lax.rem(south_col, 4)) & (y == 7) & (south < 0)
        at_north = (group == lax.rem(north_col, 4)) & (y == 0) & (north < 0)
        for s in range(SPECIES):
            beside = folded_tile(i, s)
            tile = coarse[col // 4, s, half]
            here = coarse[south_quad, s, half]
            both = here + middle[south_quad, s, half]
            change = change_of(here, turn(tile, -25, 1), both, beside, up[1][s], down[1][s], 1.0)
            add(south_quad, s, half, at_south, change)
            here = coarse[north_quad, s, half]
            both = here + middle[north_quad, s, half]
            change = change_of(here, turn(tile, 25, 1), both, beside, down[1][s], up[1][s], -1.0)
            add(north_quad, s, half, at_north, change)
        return carry

    lax.fori_loop(0, BOXES, open_y, 0)
    mean_matrix = summing(fine_y // 2 == given_y)

    def open_z(high, row, source, old_source, rate_out, rate_in, sign):
        folded0[:EDGE_COARSE, :] = product(source[:EDGE_COARSE, :] + old_source[:EDGE_COARSE, :], mean_matrix)
        for i in range(BOXES):
            col, half, is_open = [table[STRIDE * i + f] for f in (COL, HALF, OPEN_Z)]
            q = col // 4
            where = (rows == row) & (group == lax.rem(col, 4)) & (half == high) & (is_open > 0)
            for s in range(SPECIES):
                beside = jnp.broadcast_to(folded0[8 * s + i : 8 * s + i + 1, :], (8, 128))
                here = coarse[q, s, 1 - high]
                across = line(old_source, EDGE_COARSE + (2 * s + high) * QUADS + q)
                both = here + middle[q, s, 1 - high]
                change = change_of(here, across, both, beside, rate_out[s], rate_in[s], sign)
                add(q, s, 1 - high, where, change)

    @pl.when(m == CHUNKS - 1)
    def _():
        open_z(1, 7, above, old_above, up[2], down[2], 1.0)

    @pl.when(m == 0)
    def _():
        open_z(0, 0, below, old_below, down[2], up[2], -1.0)

    row_index = 2 * lax.rem(rows, 4)
    last = part > 0
    edge = jnp.where(last, 3, 0)
    sign = jnp.where(last, 1.0, -1.0)
    sums = []
    for s in range(SPECIES):
        totals = [old_outer[0, s, r] + outer[0, s, r] for r in range(2)]
        totals = [take(total + turn(total, -1, 0), row_index, 0) for total in totals]
        total = jnp.where(rows < 4, totals[0], totals[1])
        sums.append(total + turn(total, -1, 1))

    def open_x(q, carry):
        column = 8 * (4 * q + group) + y
        for h in range(2):
            box = table[BESIDE + 2 * (4 * q) + h]
            for o in range(1, 4):
                box = jnp.where(group == o, table[BESIDE + 2 * (4 * q + o) + h], box)
            where = (box >= 0) & (x == edge)
            index = 16 * jnp.maximum(box, 0) + 2 * y
            for s in range(SPECIES):
                rate_out = jnp.where(last, up[0][s], down[0][s])
                rate_in = jnp.where(last, down[0][s], up[0][s])
                here = coarse[q, s, h]
                across = take(old_outer[1, s, h], column, 1)
                both = here + middle[q, s, h]
                beside = take(sums[s], index, 1)
                add(q, s, h, where, change_of(here, across, both, beside, rate_out, rate_in, sign))
        return carry

    lax.fori_loop(0, QUADS, open_x, 0)
    fold(((result0,), (result1,)), mean_matrix)

    def cover(i, carry):
        col, half = [table[STRIDE * i + f] for f in (COL, HALF)]
        q = col // 4
        where = group == lax.rem(col, 4)
        for s in range(SPECIES):
            coarse_new[q, s, half] = jnp.where(where, 0.125 * folded_tile(i, s), coarse_new[q, s, half])
        return carry

    lax.fori_loop(0, BOXES, cover, 0)
    for q in range(QUADS):
        for p in range(3):
            at = FINE_ROWS + 8 * p
            tiles = [coarse_new[q, 2 * p + k // 2, k % 2] for k in range(4 if p < 2 else 2)]
            for o in range(4):
                tile = turn(tiles[0], -32 * o, 1)
                for k in range(1, len(tiles)):
                    tile = jnp.where(group == k, turn(tiles[k], 32 * (k - o), 1), tile)
                out[4 * q + o, at : at + 8, :] = tile


def call(kernel, out_shape, operands, smem, scratch=(), out_smem=False):
    many = isinstance(out_shape, (list, tuple))
    out_spec = SMEM if out_smem else VMEM
    return pl.pallas_call(
        kernel,
        out_shape=out_shape,
        in_specs=[SMEM] * smem + [VMEM] * (len(operands) - smem),
        out_specs=[out_spec] * len(out_shape) if many else out_spec,
        scratch_shapes=list(scratch),
        compiler_params=pltpu.CompilerParams(vmem_limit_bytes=40 * 1024 * 1024),
    )(*operands)


def exchange(up_edge, down_edge, outer_edge, inner_edge):
    device = lambda g, m, part: g % GX * GY + device_of(m % CHUNKS, part, g % GX)
    all_of = [(g, m, part) for g in range(GX) for m in range(CHUNKS) for part in range(2)]
    axes = ("gx", "gy")
    send = lambda value, target: lax.ppermute(value, axes, [(device(*d), device(*target(*d))) for d in all_of])
    outer = send(outer_edge, lambda g, m, part: (g + 2 * part - 1, m, 1 - part))
    below = send(up_edge, lambda g, m, part: (g, m + 1, part))
    above = send(down_edge, lambda g, m, part: (g, m - 1, part))
    inner = send(inner_edge, lambda g, m, part: (g, m, 1 - part))
    return below, above, outer, inner


def spread(pieces):
    return lax.all_to_all(pieces, "gy", 0, 0, tiled=True)


def shards(coarse, fine, corners, ghost_source, courant, reaction):
    shape = lambda *dims: jax.ShapeDtypeStruct(dims, F32)
    pieces = shape(GY, PIECE_ROWS, 128)
    boxes = shape(BOXES, SPECIES, 8, 128)
    grid = shape(QUADS, SPECIES, 2, 8, 128)
    sent = (shape(EDGE_ROWS, 128),) * 2 + (shape(2, SPECIES, 2, 8, 128),) * 2
    table = call(
        table_kernel,
        jax.ShapeDtypeStruct((TABLE,), jnp.int32),
        (corners.T, ghost_source.T),
        2,
        (pltpu.SMEM((3 * LIST_STRIDE,), jnp.int32), pltpu.SMEM((3 * ROW_SLOTS,), jnp.int32)),
        True,
    )
    received = spread(call(pack_kernel, pieces, (coarse, fine), 0))
    fine0, fine1, middle, *sending = call(compact_kernel, (boxes, boxes, grid) + sent, (table, received), 1)
    old = (fine0, fine1, middle, *exchange(*sending))
    ghosts = pltpu.VMEM((EDGE_ROWS, 128), F32)
    new0, new1, middle, provisional, *sending = call(
        first_kernel, (boxes, boxes, grid, grid) + sent, (table, courant, reaction) + old, 3, (ghosts,)
    )
    new = (new0, new1, middle, *exchange(*sending))
    scratch = (
        pltpu.VMEM((QUADS, SPECIES, 2, 8, 128), F32),
        ghosts,
        pltpu.VMEM((BOXES, SPECIES, 8, 128), F32),
        pltpu.VMEM((BOXES, SPECIES, 8, 128), F32),
        pltpu.VMEM((BOXES * SPECIES * 4, 128), F32),
        pltpu.VMEM((BOXES * SPECIES * 4, 128), F32),
    )
    back = call(second_kernel, pieces, (table, courant, reaction) + old + new + (provisional,), 3, scratch)
    return call(unpack_kernel, (shape(*coarse.shape), shape(*fine.shape)), (spread(back),), 0)


def solution(mesh):
    fine_spec = P(("gx", "gy"), None, None, None, None)
    coarse_spec = P(None, "gx", "gy", None)
    return jax.shard_map(
        shards,
        mesh=mesh,
        in_specs=(coarse_spec, fine_spec, P(), P(), P(), P()),
        out_specs=(coarse_spec, fine_spec),
        check_vma=False,
    )
```

```python
import jax
import jax.numpy as jnp
from jax import lax
from jax.experimental import pallas as pl
from jax.experimental.pallas import tpu as pltpu
from jax.sharding import PartitionSpec as P

CHIP_OF = (0, 1, 2, 3, 7, 6, 5, 4)
SPECIES = 5
GX = 16
GY = 16
BOXES = 8
CHUNKS = 8
QUADS = 4
ROW_SLOTS = 32
FINE_ROWS = 160
PIECE_ROWS = 184
EDGE_ROWS = 80
EDGE_COARSE = 40
STRIDE = 16
LIST_STRIDE = 40
F32 = jnp.float32
SLOT, COL, HALF, WEST, EAST, SOUTH, NORTH, BOTTOM, TOP, OPEN_Z = range(10)
BESIDE = BOXES * STRIDE
TABLE = BESIDE + 2 * GY

VMEM = pl.BlockSpec(memory_space=pltpu.VMEM)
SMEM = pl.BlockSpec(memory_space=pltpu.SMEM)
HBM = pl.BlockSpec(memory_space=pltpu.HBM)


def device_of(m, part, row):
    turned = (GY // 2) * (row % 2) if isinstance(row, int) else (GY // 2) * lax.rem(row, 2)
    place = 2 * CHIP_OF[m] + part + turned
    return place % GY if isinstance(row, int) else lax.rem(place, GY)


def chunk():
    turned = (GY // 2) * lax.rem(lax.axis_index("gx"), 2)
    j = lax.rem(lax.axis_index("gy") + turned, GY)
    q = j // 2
    return jnp.where(q < 4, q, 11 - q), lax.rem(j, 2)


def table_kernel(corners, sources, table, listed, ranks):
    row = lax.axis_index("gx")
    m, part = chunk()
    groups = [lax.rem(row + GX - 1 + r, GX) for r in range(3)]
    for r in range(3):

        def scan(t, count, r=r):
            live = corners[0, groups[r] * ROW_SLOTS + t] >= 0
            listed[r * LIST_STRIDE + count] = t
            ranks[r * ROW_SLOTS + t] = count
            return count + jnp.where(live, 1, 0)

        lax.fori_loop(0, ROW_SLOTS, scan, jnp.int32(0), unroll=8)

    def rank(r, source):
        found = ranks[r * ROW_SLOTS + lax.rem(jnp.maximum(source, 0), ROW_SLOTS)]
        return jnp.where(source >= 0, found, -1)

    for i in range(BOXES):
        t = listed[LIST_STRIDE + i]
        slot = groups[1] * ROW_SLOTS + t
        west, east, south, north, bottom, top = [sources[f, slot] for f in range(6)]
        half = corners[2, slot] // 128
        base = STRIDE * i
        table[base + SLOT] = t
        table[base + COL] = corners[1, slot] // 16
        table[base + HALF] = half
        table[base + WEST] = jnp.where(part > 0, i, rank(0, west))
        table[base + EAST] = jnp.where(part > 0, rank(2, east), i)
        table[base + SOUTH] = rank(1, south)
        table[base + NORTH] = rank(1, north)
        table[base + BOTTOM] = jnp.where(m > 0, i, rank(1, bottom))
        table[base + TOP] = jnp.where(m < CHUNKS - 1, i, rank(1, top))
        table[base + OPEN_Z] = jnp.where(jnp.where(half > 0, bottom, top) < 0, 1, 0)
        for field in range(10, STRIDE):
            table[base + field] = 0
    for k in range(2 * GY):
        table[BESIDE + k] = -1
    side = jnp.where(part > 0, 2, 0)
    face = jnp.where(part > 0, 0, 1)
    group = jnp.where(part > 0, groups[2], groups[0])
    for i in range(BOXES):
        beside = group * ROW_SLOTS + listed[side * LIST_STRIDE + i]
        spot = corners[1, beside] // 16 * 2 + corners[2, beside] // 128
        table[BESIDE + spot] = jnp.where(sources[face, beside] < 0, i, -1)


def pack_kernel(coarse_in, fine_in, out, coarse, fine, pieces, loaded, stored):
    row = lax.axis_index("gx")
    blocks = [(k, s) for k in range(2) for s in range(SPECIES)]
    loads = [pltpu.make_async_copy(fine_in.at[k, s], fine.at[k, s], loaded.at[n]) for n, (k, s) in enumerate(blocks)]
    loads.append(pltpu.make_async_copy(coarse_in, coarse, loaded.at[len(blocks)]))
    for load in loads:
        load.start()
    stores = []

    def send(low, high):
        piece = pl.ds(low, high - low)
        stores.append(
            pltpu.make_async_copy(pieces.at[:, piece, :], out.at[:, piece, :], stored.at[len(stores)])
        )
        stores[-1].start()

    for n, (k, s) in enumerate(blocks):
        loads[n].wait()
        turned = fine[k, s].reshape(256, 128).T
        at = (k * SPECIES + s) * 16
        for m in range(CHUNKS):
            for part in range(2):
                block = turned[16 * m : 16 * m + 16, 128 * part : 128 * part + 128]
                pieces[device_of(m, part, row), at : at + 16, :] = block
        send(at, at + 16)
    loads[len(blocks)].wait()
    for p in range(3):
        at = FINE_ROWS + 8 * p
        for part in range(2):
            blocks = []
            for s in (2 * p, 2 * p + 1):
                block = coarse[min(s, 4), 4 * part : 4 * part + 4].reshape(32, 128)
                blocks += [block, pltpu.roll(block, 64, 1)]
            turned = jnp.concatenate(blocks).T
            for m in range(CHUNKS):
                pieces[device_of(m, part, row), at : at + 8, :] = turned[8 * m : 8 * m + 8]
    send(FINE_ROWS, PIECE_ROWS)
    for store in stores:
        store.wait()


def unpack_kernel(received, coarse_out, fine_out, coarse, fine, stored):
    row = lax.axis_index("gx")
    stores = []

    def send(source, target):
        stores.append(pltpu.make_async_copy(source, target, stored.at[len(stores)]))
        stores[-1].start()

    for k in range(2):
        for s in range(SPECIES):
            at = (k * SPECIES + s) * 16
            for part in range(2):
                rows = [received[device_of(m, part, row), at : at + 16, :] for m in range(CHUNKS)]
                fine[k, s, 8 * part : 8 * part + 8] = jnp.concatenate(rows).T.reshape(8, 16, 128)
            send(fine.at[k, s], fine_out.at[k, s])
    left = lax.broadcasted_iota(jnp.int32, (32, 128), 1) < 64
    for p in range(3):
        at = FINE_ROWS + 8 * p
        rows = [received[device_of(m, part, row), at : at + 8, :] for part in range(2) for m in range(CHUNKS)]
        block = jnp.concatenate(rows).T
        for s in range(2 * p, min(2 * p + 2, SPECIES)):
            at_s = 64 * (s - 2 * p)
            low, high = block[at_s : at_s + 32], block[at_s + 32 : at_s + 64]
            coarse[s, 0:4] = jnp.where(left, low, pltpu.roll(high, 64, 1)).reshape(4, 8, 128)
            coarse[s, 4:8] = jnp.where(left, pltpu.roll(low, 64, 1), high).reshape(4, 8, 128)
    send(coarse, coarse_out)
    for store in stores:
        store.wait()


def iotas():
    return lax.broadcasted_iota(jnp.int32, (8, 128), 0), lax.broadcasted_iota(jnp.int32, (8, 128), 1)


def take(tile, index, axis):
    return jnp.take_along_axis(tile, index, axis=axis, mode="promise_in_bounds")


def turn(tile, shift, axis):
    return pltpu.roll(tile, shift % tile.shape[axis], axis)


def line(ref, index):
    return jnp.broadcast_to(ref[pl.ds(index, 1), :], (8, 128))


def edges(fine, coarse, up_out, down_out, outer_out, inner_out):
    _, lanes = iotas()
    _, part = chunk()
    last = part > 0
    for s in range(SPECIES):
        up_out[8 * s : 8 * s + 8, :] = fine[1][:, s, 7, :]
        down_out[8 * s : 8 * s + 8, :] = fine[0][:, s, 0, :]
        for h in range(2):
            at = EDGE_COARSE + (2 * s + h) * QUADS
            up_out[at : at + QUADS, :] = coarse[:, s, h, 7, :]
            down_out[at : at + QUADS, :] = coarse[:, s, h, 0, :]
        column = 32 * lax.rem(lanes // 8, 4) + lax.rem(lanes, 8)
        for r in range(2):
            faces = [jnp.zeros((8, 128), F32)] * 4
            for i in range(BOXES):
                here = lanes // 16 == i
                tile = fine[r][i, s]
                faces[0] = jnp.where(here, turn(tile, 16 * i, 1), faces[0])
                faces[1] = jnp.where(here, turn(tile, 16 * i + 16, 1), faces[1])
            for q in range(QUADS):
                here = lanes // 32 == q
                tile = coarse[q, s, r]
                faces[2] = jnp.where(here, take(tile, column, 1), faces[2])
                faces[3] = jnp.where(here, take(tile, column + 24, 1), faces[3])
            outer_out[0, s, r] = jnp.where(last, faces[1], faces[0])
            inner_out[0, s, r] = jnp.where(last, faces[0], faces[1])
            outer_out[1, s, r] = jnp.where(last, faces[3], faces[2])
            inner_out[1, s, r] = jnp.where(last, faces[2], faces[3])


def compact_kernel(table, received, fine0, fine1, coarse, up_out, down_out, outer_out, inner_out):
    _, lanes = iotas()
    for i in range(BOXES):
        t = table[STRIDE * i + SLOT]
        start = pl.multiple_of(lax.rem(t, 2) * 80, 8)
        box = received[t // 2, pl.ds(start, 80), :].reshape(SPECIES, 2, 8, 128)
        fine0[i] = box[:, 0]
        fine1[i] = box[:, 1]
    for q in range(QUADS):
        for p in range(3):
            at = FINE_ROWS + 8 * p
            tiles = [received[4 * q + o, at : at + 8, :] for o in range(4)]
            for k in range(4 if p < 2 else 2):
                tile = turn(tiles[0], -32 * k, 1)
                for o in range(1, 4):
                    tile = jnp.where(lanes // 32 == o, turn(tiles[o], 32 * (o - k), 1), tile)
                coarse[q, 2 * p + k // 2, k % 2] = tile
    edges((fine0, fine1), coarse, up_out, down_out, outer_out, inner_out)


def signs_of(courant):
    goes_up = [[courant[d, s] >= 0.0 for s in range(SPECIES)] for d in range(3)]
    size = [[jnp.abs(courant[d, s]) for s in range(SPECIES)] for d in range(3)]
    return goes_up, size


def weights_of(size, reaction, factor):
    weights = [[factor * reaction[s, e] for e in range(SPECIES)] for s in range(SPECIES)]
    for s in range(SPECIES):
        weights[s][s] = weights[s][s] + (1.0 - size[0][s] - size[1][s] - size[2][s])
    return weights


def moved(values, upwind, size, weights, s):
    total = weights[s][0] * values[0]
    for e in range(1, SPECIES):
        total = total + weights[s][e] * values[e]
    for d in range(3):
        total = total + size[d][s] * upwind[d]
    return total


def ends(table, below, above, ghosts):
    _, lanes = iotas()
    m, _ = chunk()
    ghosts[:EDGE_COARSE, :] = below[:EDGE_COARSE, :]
    ghosts[EDGE_COARSE:, :] = above[:EDGE_COARSE, :]

    def replace(side, source, name, high):
        for i in range(BOXES):
            col, half, found = [table[STRIDE * i + f] for f in (COL, HALF, name)]
            inside = 32 * lax.rem(col, 4) + 8 * (lanes // 32) + lax.rem(lanes, 16) // 2
            for s in range(SPECIES):
                other = take(line(source, EDGE_COARSE + (2 * s + side) * QUADS + col // 4), inside, 1)
                other = jnp.where(half == high, other, 0.0)
                ghost = jnp.where(found >= 0, line(source, 8 * s + jnp.maximum(found, 0)), other)
                at = EDGE_COARSE * side + 8 * s + i
                ghosts[at : at + 1, :] = ghost[:1]

    @pl.when(m == 0)
    def _():
        replace(0, below, BOTTOM, 1)

    @pl.when(m == CHUNKS - 1)
    def _():
        replace(1, above, TOP, 0)


def fine_step(i, table, fine, coarse, ghosts, sides, goes_up, size, weights, write):
    rows, lanes = iotas()
    field = lambda f: table[STRIDE * i + f]
    col, half = field(COL), field(HALF)
    lower_col, upper_col = lax.rem(col + GY - 1, GY), lax.rem(col + 1, GY)
    y = lax.rem(lanes, 16)
    found = [field(f) for f in (WEST, EAST, SOUTH, NORTH)]
    there = [source >= 0 for source in found]
    at = [jnp.maximum(source, 0) for source in found]
    lane_x = [jnp.where(there[f], 16 * at[f] + y, 8 * col + y // 2) for f in range(2)]
    own_x, line_x = lanes - y, 8 * (lanes // 32)
    lane_y = [
        jnp.where(there[2], own_x + 15, 32 * lax.rem(lower_col, 4) + line_x + 7),
        jnp.where(there[3], own_x, 32 * lax.rem(upper_col, 4) + line_x),
    ]
    row_of = [[jnp.where(is_there, rows, 4 * r + rows // 2) for is_there in there] for r in range(2)]
    kind = [jnp.where(is_there, 0, 1) for is_there in there]
    values = [[fine[r][i, s] for s in range(SPECIES)] for r in range(2)]
    for s in range(SPECIES):
        up_x, up_y, up_z = [goes_up[d][s] for d in range(3)]
        shift_x, edge_x = jnp.where(up_x, 16, 112), lanes // 16 == jnp.where(up_x, 0, 7)
        shift_y, edge_y = jnp.where(up_y, 1, 127), y == jnp.where(up_y, 0, 15)
        shift_z, edge_z = jnp.where(up_z, 1, 7), rows == jnp.where(up_z, 0, 7)
        is_there = jnp.where(up_y, found[2], found[3]) >= 0
        box_y = jnp.where(up_y, at[2], at[3])
        quad_y = jnp.where(up_y, lower_col, upper_col) // 4
        coarse_y = coarse[quad_y, s, half]
        index_x = jnp.where(up_x, lane_x[0], lane_x[1])
        index_y = jnp.where(up_y, lane_y[0], lane_y[1])

        low, high = values[0][s], values[1][s]
        first = pltpu.roll(jnp.where(up_z, low, high), shift_z, 0)
        second = pltpu.roll(jnp.where(up_z, high, low), shift_z, 0)
        second = jnp.where(edge_z, first, second)
        first = jnp.where(edge_z, line(ghosts, jnp.where(up_z, 0, EDGE_COARSE) + 8 * s + i), first)
        from_z = (jnp.where(up_z, first, second), jnp.where(up_z, second, first))

        for r in range(2):
            value = values[r][s]
            west = sides(0, kind[0], s, jnp.where(there[0], r, half))
            east = sides(1, kind[1], s, jnp.where(there[1], r, half))
            ghost = take(jnp.where(up_x, west, east), jnp.where(up_x, row_of[r][0], row_of[r][1]), 0)
            ghost = take(ghost, index_x, 1)
            from_x = jnp.where(edge_x, ghost, pltpu.roll(value, shift_x, 1))
            ghost = take(
                jnp.where(is_there, fine[r][box_y, s], coarse_y), jnp.where(up_y, row_of[r][2], row_of[r][3]), 0
            )
            ghost = take(ghost, index_y, 1)
            from_y = jnp.where(edge_y, ghost, pltpu.roll(value, shift_y, 1))
            write(r, s, moved(values[r], (from_x, from_y, from_z[r]), size, weights, s))


def sides_of(outer, inner):
    _, part = chunk()

    def pick(side, kind, s, at):
        one, other = outer[kind, s, at], inner[kind, s, at]
        return jnp.where(part == side, one, other)

    return pick


def first_kernel(
    table, courant, reaction, fine0, fine1, coarse, below, above, outer, inner,
    new0, new1, middle, provisional, up_out, down_out, outer_out, inner_out, ghosts,
):
    rows, lanes = iotas()
    m, _ = chunk()
    goes_up, size = signs_of(courant)
    weights = weights_of(size, reaction, 1.0)
    x = lax.rem(lanes // 8, 4)
    y = lax.rem(lanes, 8)
    sides = sides_of(outer, inner)
    ends(table, below, above, ghosts)

    def coarse_quad(q, carry):
        before, after = lax.rem(q + QUADS - 1, QUADS), lax.rem(q + 1, QUADS)
        values = [[coarse[q, s, h] for s in range(SPECIES)] for h in range(2)]
        column = 8 * (4 * q + lanes // 32) + y
        for s in range(SPECIES):
            up_x, up_y, up_z = [goes_up[d][s] for d in range(3)]
            at = [EDGE_COARSE + (2 * s + h) * QUADS + q for h in range(2)]
            lows, highs = [line(below, k) for k in at], [line(above, k) for k in at]
            bottoms = (jnp.where(m > 0, lows[0], 0.0), jnp.where(m > 0, lows[1], lows[0]))
            tops = (
                jnp.where(m < CHUNKS - 1, highs[0], highs[1]),
                jnp.where(m < CHUNKS - 1, highs[1], 0.0),
            )
            for h in range(2):
                value = values[h][s]
                ghost = take(jnp.where(up_x, sides(0, 1, s, h), sides(1, 1, s, h)), column, 1)
                from_x = pltpu.roll(value, jnp.where(up_x, 8, 120), 1)
                from_x = jnp.where(x == jnp.where(up_x, 0, 3), ghost, from_x)

                beside = coarse[jnp.where(up_y, before, after), s, h]
                ghost = jnp.where(lanes // 32 == jnp.where(up_y, 3, 0), beside, value)
                ghost = pltpu.roll(ghost, jnp.where(up_y, 25, 103), 1)
                from_y = pltpu.roll(value, jnp.where(up_y, 1, 127), 1)
                from_y = jnp.where(y == jnp.where(up_y, 0, 7), ghost, from_y)

                ghost = jnp.where(up_z, bottoms[h], tops[h])
                from_z = pltpu.roll(value, jnp.where(up_z, 1, 7), 0)
                from_z = jnp.where(rows == jnp.where(up_z, 0, 7), ghost, from_z)

                result = moved(values[h], (from_x, from_y, from_z), size, weights, s)
                provisional[q, s, h] = result
                middle[q, s, h] = 0.5 * (value + result)
        return carry

    lax.fori_loop(0, QUADS, coarse_quad, 0)
    new = (new0, new1)
    weights = weights_of(size, reaction, 0.5)

    def box(i, carry):
        def write(r, s, result):
            new[r][i, s] = result

        fine_step(i, table, (fine0, fine1), coarse, ghosts, sides, goes_up, size, weights, write)
        return carry

    lax.fori_loop(0, BOXES, box, 0)
    edges(new, middle, up_out, down_out, outer_out, inner_out)


def tools_of(courant, coarse_new, folded0, folded1):
    up = [[jnp.maximum(courant[d, s], 0.0) for s in range(SPECIES)] for d in range(3)]
    down = [[jnp.minimum(courant[d, s], 0.0) for s in range(SPECIES)] for d in range(3)]
    taken = lax.broadcasted_iota(jnp.int32, (128, 128), 0)
    given = lax.broadcasted_iota(jnp.int32, (128, 128), 1)
    given_y, fine_y = lax.rem(given, 8), lax.rem(taken, 16)
    same_x = lax.rem(given // 8, 4) == taken // 32

    def summing(rule):
        return jnp.where(same_x & rule(given_y, fine_y), 1.0, 0.0).astype(F32)

    def product(values, matrix):
        return jnp.dot(values, matrix, precision=lax.Precision.HIGHEST, preferred_element_type=F32)

    def fold(tiles, matrix):
        for refs, folded in zip(tiles, (folded0, folded1)):
            pairs = sum(
                ref.reshape(BOXES * SPECIES * 8, 128)[pl.ds(odd, BOXES * SPECIES * 4, stride=2), :]
                for ref in refs
                for odd in range(2)
            )
            folded[...] = product(pairs, matrix)

    def folded_tile(i, s):
        at = pl.ds((i * SPECIES + s) * 4, 4)
        return jnp.concatenate([folded0[at, :], folded1[at, :]])

    def add(q, s, h, where, change):
        coarse_new[q, s, h] = coarse_new[q, s, h] + jnp.where(where, change, 0.0)

    def change_of(here, across, both, beside, rate_out, rate_in, sign):
        return sign * (rate_out * (here - 0.5 * both) + rate_in * (across - 0.125 * beside))

    return up, down, summing, product, fold, folded_tile, add, change_of


def beside_kernel(table, courant, old0, old1, coarse, fine0, fine1, middle, provisional, coarse_new, folded0, folded1):
    _, lanes = iotas()
    y = lax.rem(lanes, 8)
    group = lanes // 32
    up, down, summing, _, fold, folded_tile, add, change_of = tools_of(courant, coarse_new, folded0, folded1)
    coarse_new[...] = provisional[...]

    def rule(given_y, fine_y):
        return ((fine_y == 0) & (given_y == 7)) | ((fine_y == 15) & (given_y == 0))

    fold(((old0, fine0), (old1, fine1)), summing(rule))

    def open_y(i, carry):
        col, half, south, north = [table[STRIDE * i + f] for f in (COL, HALF, SOUTH, NORTH)]
        south_col, north_col = lax.rem(col + GY - 1, GY), lax.rem(col + 1, GY)
        south_quad, north_quad = south_col // 4, north_col // 4
        at_south = (group == lax.rem(south_col, 4)) & (y == 7) & (south < 0)
        at_north = (group == lax.rem(north_col, 4)) & (y == 0) & (north < 0)
        for s in range(SPECIES):
            beside = folded_tile(i, s)
            tile = coarse[col // 4, s, half]
            here = coarse[south_quad, s, half]
            both = here + middle[south_quad, s, half]
            change = change_of(here, turn(tile, -25, 1), both, beside, up[1][s], down[1][s], 1.0)
            add(south_quad, s, half, at_south, change)
            here = coarse[north_quad, s, half]
            both = here + middle[north_quad, s, half]
            change = change_of(here, turn(tile, 25, 1), both, beside, down[1][s], up[1][s], -1.0)
            add(north_quad, s, half, at_north, change)
        return carry

    lax.fori_loop(0, BOXES, open_y, 0)


def second_kernel(
    table, courant, reaction, old0, old1, coarse, old_below, old_above, old_outer, old_inner,
    fine0, fine1, middle, below, above, outer, inner, corrected, out,
    coarse_new, ghosts, result0, result1, folded0, folded1,
):
    rows, lanes = iotas()
    m, part = chunk()
    goes_up, size = signs_of(courant)
    weights = weights_of(size, reaction, 0.5)
    up, down, summing, product, fold, folded_tile, add, change_of = tools_of(courant, coarse_new, folded0, folded1)
    x = lax.rem(lanes // 8, 4)
    y = lax.rem(lanes, 8)
    group = lanes // 32
    ends(table, below, above, ghosts)
    coarse_new[...] = corrected[...]

    def clear(j, carry):
        out[j, :FINE_ROWS, :] = jnp.zeros((FINE_ROWS, 128), F32)
        return carry

    lax.fori_loop(0, GY, clear, 0)
    sides = sides_of(outer, inner)

    def box_step(i, carry):
        t = table[STRIDE * i + SLOT]
        start = lax.rem(t, 2) * 80

        def write(r, s, result):
            out[t // 2, pl.ds(pl.multiple_of(start + (2 * s + r) * 8, 8), 8), :] = result
            (result0, result1)[r][i, s] = result

        fine_step(i, table, (fine0, fine1), middle, ghosts, sides, goes_up, size, weights, write)
        return carry

    lax.fori_loop(0, BOXES, box_step, 0)

    mean_matrix = summing(lambda given_y, fine_y: fine_y // 2 == given_y)

    def open_z(high, row, source, old_source, rate_out, rate_in, sign):
        folded0[:EDGE_COARSE, :] = product(source[:EDGE_COARSE, :] + old_source[:EDGE_COARSE, :], mean_matrix)
        for i in range(BOXES):
            col, half, is_open = [table[STRIDE * i + f] for f in (COL, HALF, OPEN_Z)]
            q = col // 4
            where = (rows == row) & (group == lax.rem(col, 4)) & (half == high) & (is_open > 0)
            for s in range(SPECIES):
                beside = jnp.broadcast_to(folded0[8 * s + i : 8 * s + i + 1, :], (8, 128))
                here = coarse[q, s, 1 - high]
                across = line(old_source, EDGE_COARSE + (2 * s + high) * QUADS + q)
                both = here + middle[q, s, 1 - high]
                change = change_of(here, across, both, beside, rate_out[s], rate_in[s], sign)
                add(q, s, 1 - high, where, change)

    @pl.when(m == CHUNKS - 1)
    def _():
        open_z(1, 7, above, old_above, up[2], down[2], 1.0)

    @pl.when(m == 0)
    def _():
        open_z(0, 0, below, old_below, down[2], up[2], -1.0)

    row_index = 2 * lax.rem(rows, 4)
    last = part > 0
    edge = jnp.where(last, 3, 0)
    sign = jnp.where(last, 1.0, -1.0)
    sums = []
    for s in range(SPECIES):
        totals = [old_outer[0, s, r] + outer[0, s, r] for r in range(2)]
        totals = [take(total + turn(total, -1, 0), row_index, 0) for total in totals]
        total = jnp.where(rows < 4, totals[0], totals[1])
        sums.append(total + turn(total, -1, 1))

    def open_x(q, carry):
        column = 8 * (4 * q + group) + y
        for h in range(2):
            box = table[BESIDE + 2 * (4 * q) + h]
            for o in range(1, 4):
                box = jnp.where(group == o, table[BESIDE + 2 * (4 * q + o) + h], box)
            where = (box >= 0) & (x == edge)
            index = 16 * jnp.maximum(box, 0) + 2 * y
            for s in range(SPECIES):
                rate_out = jnp.where(last, up[0][s], down[0][s])
                rate_in = jnp.where(last, down[0][s], up[0][s])
                here = coarse[q, s, h]
                across = take(old_outer[1, s, h], column, 1)
                both = here + middle[q, s, h]
                beside = take(sums[s], index, 1)
                add(q, s, h, where, change_of(here, across, both, beside, rate_out, rate_in, sign))
        return carry

    lax.fori_loop(0, QUADS, open_x, 0)
    fold(((result0,), (result1,)), mean_matrix)

    def cover(i, carry):
        col, half = [table[STRIDE * i + f] for f in (COL, HALF)]
        q = col // 4
        where = group == lax.rem(col, 4)
        for s in range(SPECIES):
            coarse_new[q, s, half] = jnp.where(where, 0.125 * folded_tile(i, s), coarse_new[q, s, half])
        return carry

    lax.fori_loop(0, BOXES, cover, 0)
    for q in range(QUADS):
        for p in range(3):
            at = FINE_ROWS + 8 * p
            tiles = [coarse_new[q, 2 * p + k // 2, k % 2] for k in range(4 if p < 2 else 2)]
            for o in range(4):
                tile = turn(tiles[0], -32 * o, 1)
                for k in range(1, len(tiles)):
                    tile = jnp.where(group == k, turn(tiles[k], 32 * (k - o), 1), tile)
                out[4 * q + o, at : at + 8, :] = tile


def call(kernel, out_shape, operands, smem, scratch=(), in_spec=VMEM, out_spec=VMEM):
    many = isinstance(out_shape, (list, tuple))
    return pl.pallas_call(
        kernel,
        out_shape=out_shape,
        in_specs=[SMEM] * smem + [in_spec] * (len(operands) - smem),
        out_specs=[out_spec] * len(out_shape) if many else out_spec,
        scratch_shapes=list(scratch),
        compiler_params=pltpu.CompilerParams(vmem_limit_bytes=40 * 1024 * 1024),
    )(*operands)


def exchange(up_edge, down_edge, outer_edge, inner_edge):
    device = lambda g, m, part: g % GX * GY + device_of(m % CHUNKS, part, g % GX)
    all_of = [(g, m, part) for g in range(GX) for m in range(CHUNKS) for part in range(2)]
    axes = ("gx", "gy")
    send = lambda value, target: lax.ppermute(value, axes, [(device(*d), device(*target(*d))) for d in all_of])
    outer = send(outer_edge, lambda g, m, part: (g + 2 * part - 1, m, 1 - part))
    below = send(up_edge, lambda g, m, part: (g, m + 1, part))
    above = send(down_edge, lambda g, m, part: (g, m - 1, part))
    inner = send(inner_edge, lambda g, m, part: (g, m, 1 - part))
    return below, above, outer, inner


def spread(pieces):
    return lax.all_to_all(pieces, "gy", 0, 0, tiled=True)


def shards(coarse, fine, corners, ghost_source, courant, reaction):
    shape = lambda *dims: jax.ShapeDtypeStruct(dims, F32)
    pieces = shape(GY, PIECE_ROWS, 128)
    boxes = shape(BOXES, SPECIES, 8, 128)
    grid = shape(QUADS, SPECIES, 2, 8, 128)
    sent = (shape(EDGE_ROWS, 128),) * 2 + (shape(2, SPECIES, 2, 8, 128),) * 2
    table = call(
        table_kernel,
        jax.ShapeDtypeStruct((TABLE,), jnp.int32),
        (corners.T, ghost_source.T),
        2,
        (pltpu.SMEM((3 * LIST_STRIDE,), jnp.int32), pltpu.SMEM((3 * ROW_SLOTS,), jnp.int32)),
        out_spec=SMEM,
    )
    whole = (pltpu.VMEM(coarse.shape, F32), pltpu.VMEM(fine.shape, F32))
    copies = pltpu.SemaphoreType.DMA((2 * SPECIES + 1,))
    scratch = (*whole, pltpu.VMEM(pieces.shape, F32), copies, copies)
    placed = [pltpu.with_memory_space_constraint(value, pltpu.HBM) for value in (coarse, fine)]
    received = spread(call(pack_kernel, pieces, placed, 0, scratch, HBM, HBM))
    fine0, fine1, middle, *sending = call(compact_kernel, (boxes, boxes, grid) + sent, (table, received), 1)
    old = (fine0, fine1, middle, *exchange(*sending))
    ghosts = pltpu.VMEM((EDGE_ROWS, 128), F32)
    new0, new1, middle, provisional, *sending = call(
        first_kernel, (boxes, boxes, grid, grid) + sent, (table, courant, reaction) + old, 3, (ghosts,)
    )
    new = (new0, new1, middle, *exchange(*sending))
    folded = (pltpu.VMEM((BOXES * SPECIES * 4, 128), F32),) * 2
    operands = (table, courant) + old[:3] + new[:3] + (provisional,)
    corrected = call(beside_kernel, grid, operands, 2, folded)
    scratch = (
        pltpu.VMEM(grid.shape, F32),
        ghosts,
        pltpu.VMEM(boxes.shape, F32),
        pltpu.VMEM(boxes.shape, F32),
        *folded,
    )
    back = call(second_kernel, pieces, (table, courant, reaction) + old + new + (corrected,), 3, scratch)
    outputs = (shape(*coarse.shape), shape(*fine.shape))
    return call(unpack_kernel, outputs, (spread(back),), 0, (*whole, copies), VMEM, HBM)


def solution(mesh):
    fine_spec = P(("gx", "gy"), None, None, None, None)
    coarse_spec = P(None, "gx", "gy", None)
    return jax.shard_map(
        shards,
        mesh=mesh,
        in_specs=(coarse_spec, fine_spec, P(), P(), P(), P()),
        out_specs=(coarse_spec, fine_spec),
        check_vma=False,
    )
```

```python
import jax
import jax.numpy as jnp
from jax import lax
from jax.experimental import pallas as pl
from jax.experimental.pallas import tpu as pltpu
from jax.sharding import PartitionSpec as P

CHIP_OF = (0, 1, 2, 3, 7, 6, 5, 4)
SPECIES = 5
GX = 16
GY = 16
BOXES = 8
CHUNKS = 8
QUADS = 4
ROW_SLOTS = 32
FINE_ROWS = 160
PIECE_ROWS = 184
EDGE_ROWS = 80
EDGE_COARSE = 40
STRIDE = 16
LIST_STRIDE = 40
F32 = jnp.float32
SLOT, COL, HALF, WEST, EAST, SOUTH, NORTH, BOTTOM, TOP, OPEN_Z = range(10)
BESIDE = BOXES * STRIDE
TABLE = BESIDE + 2 * GY

VMEM = pl.BlockSpec(memory_space=pltpu.VMEM)
SMEM = pl.BlockSpec(memory_space=pltpu.SMEM)
HBM = pl.BlockSpec(memory_space=pltpu.HBM)


def device_of(m, part, row):
    turned = (GY // 2) * (row % 2) if isinstance(row, int) else (GY // 2) * lax.rem(row, 2)
    place = 2 * CHIP_OF[m] + part + turned
    return place % GY if isinstance(row, int) else lax.rem(place, GY)


def chunk():
    turned = (GY // 2) * lax.rem(lax.axis_index("gx"), 2)
    j = lax.rem(lax.axis_index("gy") + turned, GY)
    q = j // 2
    return jnp.where(q < 4, q, 11 - q), lax.rem(j, 2)


def fill_table(corners, sources, table, listed, ranks):
    row = lax.axis_index("gx")
    m, part = chunk()
    groups = (row, lax.rem(row + jnp.where(part > 0, 1, GX - 1), GX))

    def scan(t, counts):
        new_counts = []
        for r in range(2):
            live = corners[0, groups[r] * ROW_SLOTS + t] >= 0
            listed[r * LIST_STRIDE + counts[r]] = t
            ranks[r * ROW_SLOTS + t] = counts[r]
            new_counts.append(counts[r] + jnp.where(live, 1, 0))
        return tuple(new_counts)

    lax.fori_loop(0, ROW_SLOTS, scan, (jnp.int32(0), jnp.int32(0)), unroll=True)

    def rank(r, source):
        found = ranks[r * ROW_SLOTS + lax.rem(jnp.maximum(source, 0), ROW_SLOTS)]
        return jnp.where(source >= 0, found, -1)

    for k in range(2 * GY):
        table[BESIDE + k] = -1
    face = jnp.where(part > 0, 0, 1)
    for i in range(BOXES):
        t = listed[i]
        slot = groups[0] * ROW_SLOTS + t
        south, north, bottom, top = [sources[f, slot] for f in range(2, 6)]
        beside = rank(1, sources[1 - face, slot])
        half = corners[2, slot] // 128
        base = STRIDE * i
        table[base + SLOT] = t
        table[base + COL] = corners[1, slot] // 16
        table[base + HALF] = half
        table[base + WEST] = jnp.where(part > 0, i, beside)
        table[base + EAST] = jnp.where(part > 0, beside, i)
        table[base + SOUTH] = rank(0, south)
        table[base + NORTH] = rank(0, north)
        table[base + BOTTOM] = jnp.where(m > 0, i, rank(0, bottom))
        table[base + TOP] = jnp.where(m < CHUNKS - 1, i, rank(0, top))
        table[base + OPEN_Z] = jnp.where(jnp.where(half > 0, bottom, top) < 0, 1, 0)
        other = groups[1] * ROW_SLOTS + listed[LIST_STRIDE + i]
        spot = corners[1, other] // 16 * 2 + corners[2, other] // 128
        table[BESIDE + spot] = jnp.where(sources[face, other] < 0, i, -1)


def pack_kernel(
    corners_in, sources_in, coarse_in, fine_in, out, table, coarse, fine, loaded, listed, ranks, corners, sources,
    around,
):
    row, column = lax.axis_index("gx"), lax.axis_index("gy")
    blocks = [(k, s) for k in range(2) for s in range(SPECIES)]
    loads = [pltpu.make_async_copy(fine_in.at[k, s], fine.at[k, s], loaded.at[n]) for n, (k, s) in enumerate(blocks)]
    loads.append(pltpu.make_async_copy(coarse_in, coarse, loaded.at[len(blocks)]))
    integers = (
        pltpu.make_async_copy(corners_in, corners, loaded.at[len(blocks) + 1]),
        pltpu.make_async_copy(sources_in, sources, loaded.at[len(blocks) + 2]),
    )
    for load in (*integers, *loads):
        load.start()
    for load in (*integers, *loads):
        load.wait()
    fill_table(corners, sources, table, listed, ranks)
    for n, (k, s) in enumerate(blocks):
        turned = fine[k, s].reshape(256, 128).T
        at = (k * SPECIES + s) * 16
        for m in range(CHUNKS):
            for part in range(2):
                block = turned[16 * m : 16 * m + 16, 128 * part : 128 * part + 128]
                out[device_of(m, part, row), at : at + 16, :] = block
    for p in range(3):
        at = FINE_ROWS + 8 * p
        for part in range(2):
            blocks = []
            for s in (2 * p, 2 * p + 1):
                block = coarse[min(s, 4), 4 * part : 4 * part + 4].reshape(32, 128)
                blocks += [block, pltpu.roll(block, 64, 1)]
            for n, block in enumerate(blocks):
                around[pl.ds(pl.multiple_of(32 * lax.rem(column + n, 4), 32), 32), :] = block
            turned = around[...].T
            for m in range(CHUNKS):
                out[device_of(m, part, row), at : at + 8, :] = turned[8 * m : 8 * m + 8]


def unpack_kernel(received, coarse_out, fine_out, coarse, fine, stored, around):
    row, column = lax.axis_index("gx"), lax.axis_index("gy")
    stores = []

    def send(source, target):
        stores.append(pltpu.make_async_copy(source, target, stored.at[len(stores)]))
        stores[-1].start()

    for k in range(2):
        for s in range(SPECIES):
            at = (k * SPECIES + s) * 16
            for part in range(2):
                rows = [received[device_of(m, part, row), at : at + 16, :] for m in range(CHUNKS)]
                fine[k, s, 8 * part : 8 * part + 8] = jnp.concatenate(rows).T.reshape(8, 16, 128)
            send(fine.at[k, s], fine_out.at[k, s])
    left = lax.broadcasted_iota(jnp.int32, (32, 128), 1) < 64
    for p in range(3):
        at = FINE_ROWS + 8 * p
        rows = [received[device_of(m, part, row), at : at + 8, :] for part in range(2) for m in range(CHUNKS)]
        around[...] = jnp.concatenate(rows).T
        for s in range(2 * p, min(2 * p + 2, SPECIES)):
            low, high = [
                around[pl.ds(pl.multiple_of(32 * lax.rem(column + 2 * (s - 2 * p) + h, 4), 32), 32), :] for h in range(2)
            ]
            coarse[s, 0:4] = jnp.where(left, low, pltpu.roll(high, 64, 1)).reshape(4, 8, 128)
            coarse[s, 4:8] = jnp.where(left, pltpu.roll(low, 64, 1), high).reshape(4, 8, 128)
    send(coarse, coarse_out)
    for store in stores:
        store.wait()


def iotas():
    return lax.broadcasted_iota(jnp.int32, (8, 128), 0), lax.broadcasted_iota(jnp.int32, (8, 128), 1)


def take(tile, index, axis):
    return jnp.take_along_axis(tile, index, axis=axis, mode="promise_in_bounds")


def turn(tile, shift, axis):
    return pltpu.roll(tile, shift % tile.shape[axis], axis)


def line(ref, index):
    return jnp.broadcast_to(ref[pl.ds(index, 1), :], (8, 128))


def edges(fine, coarse, up_out, down_out, outer_out, inner_out):
    _, lanes = iotas()
    _, part = chunk()
    last = part > 0
    for s in range(SPECIES):
        up_out[8 * s : 8 * s + 8, :] = fine[1][:, s, 7, :]
        down_out[8 * s : 8 * s + 8, :] = fine[0][:, s, 0, :]
        for h in range(2):
            at = EDGE_COARSE + (2 * s + h) * QUADS
            up_out[at : at + QUADS, :] = coarse[:, s, h, 7, :]
            down_out[at : at + QUADS, :] = coarse[:, s, h, 0, :]
        for r in range(2):
            low = high = coarse_low = coarse_high = jnp.zeros((8, 128), F32)
            for i in range(BOXES):
                here = lanes // 16 == i
                low = jnp.where(here, turn(fine[r][i, s], 16 * i, 1), low)
                high = jnp.where(here, turn(fine[r][i, s], 16 * i + 16, 1), high)
            for q in range(QUADS):
                here = lax.rem(lanes // 8, 4) == q
                coarse_low = jnp.where(here, turn(coarse[q, s, r], 8 * q, 1), coarse_low)
                coarse_high = jnp.where(here, turn(coarse[q, s, r], 8 * q - 24, 1), coarse_high)
            outer_out[0, s, r] = jnp.where(last, high, low)
            inner_out[0, s, r] = jnp.where(last, low, high)
            outer_out[1, s, r] = jnp.where(last, coarse_high, coarse_low)
            inner_out[1, s, r] = jnp.where(last, coarse_low, coarse_high)


def compact_kernel(table, received, fine0, fine1, coarse, up_out, down_out, outer_out, inner_out):
    _, lanes = iotas()
    for i in range(BOXES):
        t = table[STRIDE * i + SLOT]
        start = pl.multiple_of(lax.rem(t, 2) * 80, 8)
        box = received[t // 2, pl.ds(start, 80), :].reshape(SPECIES, 2, 8, 128)
        fine0[i] = box[:, 0]
        fine1[i] = box[:, 1]
    for q in range(QUADS):
        for p in range(3):
            at = FINE_ROWS + 8 * p
            tiles = [received[4 * q + o, at : at + 8, :] for o in range(4)]
            for k in range(4 if p < 2 else 2):
                tile = tiles[0]
                for o in range(1, 4):
                    tile = jnp.where(lanes // 32 == (o + k) % 4, tiles[o], tile)
                coarse[q, 2 * p + k // 2, k % 2] = turn(tile, -32 * k, 1)
    edges((fine0, fine1), coarse, up_out, down_out, outer_out, inner_out)


def signs_of(courant):
    goes_up = [[courant[d, s] >= 0.0 for s in range(SPECIES)] for d in range(3)]
    size = [[jnp.abs(courant[d, s]) for s in range(SPECIES)] for d in range(3)]
    return goes_up, size


def weights_of(size, reaction, factor):
    weights = [[factor * reaction[s, e] for e in range(SPECIES)] for s in range(SPECIES)]
    for s in range(SPECIES):
        weights[s][s] = weights[s][s] + (1.0 - size[0][s] - size[1][s] - size[2][s])
    return weights


def moved(values, upwind, size, weights, s):
    total = weights[s][0] * values[0]
    for e in range(1, SPECIES):
        total = total + weights[s][e] * values[e]
    for d in range(3):
        total = total + size[d][s] * upwind[d]
    return total


def ends(table, below, above, ghosts):
    _, lanes = iotas()
    m, _ = chunk()
    ghosts[:EDGE_COARSE, :] = below[:EDGE_COARSE, :]
    ghosts[EDGE_COARSE:, :] = above[:EDGE_COARSE, :]

    def replace(side, source, name, high):
        for i in range(BOXES):
            col, half, found = [table[STRIDE * i + f] for f in (COL, HALF, name)]
            inside = 32 * lax.rem(col, 4) + 8 * (lanes // 32) + lax.rem(lanes, 16) // 2
            for s in range(SPECIES):
                other = take(line(source, EDGE_COARSE + (2 * s + side) * QUADS + col // 4), inside, 1)
                other = jnp.where(half == high, other, 0.0)
                ghost = jnp.where(found >= 0, line(source, 8 * s + jnp.maximum(found, 0)), other)
                at = EDGE_COARSE * side + 8 * s + i
                ghosts[at : at + 1, :] = ghost[:1]

    @pl.when(m == 0)
    def _():
        replace(0, below, BOTTOM, 1)

    @pl.when(m == CHUNKS - 1)
    def _():
        replace(1, above, TOP, 0)


def fine_step(i, table, fine, coarse, ghosts, sides, goes_up, size, weights, write):
    rows, lanes = iotas()
    field = lambda f: table[STRIDE * i + f]
    col, half = field(COL), field(HALF)
    lower_col, upper_col = lax.rem(col + GY - 1, GY), lax.rem(col + 1, GY)
    y = lax.rem(lanes, 16)
    found = [field(f) for f in (WEST, EAST, SOUTH, NORTH)]
    there = [source >= 0 for source in found]
    at = [jnp.maximum(source, 0) for source in found]
    beside = 32 * lax.rem(col, 4) + 8 * (col // 4) + y // 2
    lane_x = [jnp.where(there[f], 16 * at[f] + y, beside) for f in range(2)]
    own_x, line_x = lanes - y, 8 * (lanes // 32)
    lane_y = [
        jnp.where(there[2], own_x + 15, 32 * lax.rem(lower_col, 4) + line_x + 7),
        jnp.where(there[3], own_x, 32 * lax.rem(upper_col, 4) + line_x),
    ]
    row_of = [[jnp.where(is_there, rows, 4 * r + rows // 2) for is_there in there] for r in range(2)]
    kind = [jnp.where(is_there, 0, 1) for is_there in there]
    values = [[fine[r][i, s] for s in range(SPECIES)] for r in range(2)]
    for s in range(SPECIES):
        up_x, up_y, up_z = [goes_up[d][s] for d in range(3)]
        shift_x, edge_x = jnp.where(up_x, 16, 112), lanes // 16 == jnp.where(up_x, 0, 7)
        shift_y, edge_y = jnp.where(up_y, 1, 127), y == jnp.where(up_y, 0, 15)
        shift_z, edge_z = jnp.where(up_z, 1, 7), rows == jnp.where(up_z, 0, 7)
        is_there = jnp.where(up_y, found[2], found[3]) >= 0
        box_y = jnp.where(up_y, at[2], at[3])
        quad_y = jnp.where(up_y, lower_col, upper_col) // 4
        coarse_y = coarse[quad_y, s, half]
        index_x = jnp.where(up_x, lane_x[0], lane_x[1])
        index_y = jnp.where(up_y, lane_y[0], lane_y[1])

        low, high = values[0][s], values[1][s]
        first = pltpu.roll(jnp.where(up_z, low, high), shift_z, 0)
        second = pltpu.roll(jnp.where(up_z, high, low), shift_z, 0)
        second = jnp.where(edge_z, first, second)
        first = jnp.where(edge_z, line(ghosts, jnp.where(up_z, 0, EDGE_COARSE) + 8 * s + i), first)
        from_z = (jnp.where(up_z, first, second), jnp.where(up_z, second, first))

        for r in range(2):
            value = values[r][s]
            west = sides(0, kind[0], s, jnp.where(there[0], r, half))
            east = sides(1, kind[1], s, jnp.where(there[1], r, half))
            ghost = take(jnp.where(up_x, west, east), jnp.where(up_x, row_of[r][0], row_of[r][1]), 0)
            ghost = take(ghost, index_x, 1)
            from_x = jnp.where(edge_x, ghost, pltpu.roll(value, shift_x, 1))
            ghost = take(
                jnp.where(is_there, fine[r][box_y, s], coarse_y), jnp.where(up_y, row_of[r][2], row_of[r][3]), 0
            )
            ghost = take(ghost, index_y, 1)
            from_y = jnp.where(edge_y, ghost, pltpu.roll(value, shift_y, 1))
            write(r, s, moved(values[r], (from_x, from_y, from_z[r]), size, weights, s))


def sides_of(outer, inner):
    _, part = chunk()

    def pick(side, kind, s, at):
        one, other = outer[kind, s, at], inner[kind, s, at]
        return jnp.where(part == side, one, other)

    return pick


def first_kernel(
    table, courant, reaction, fine0, fine1, coarse, below, above, outer, inner,
    new0, new1, middle, provisional, up_out, down_out, outer_out, inner_out, ghosts,
):
    rows, lanes = iotas()
    m, _ = chunk()
    goes_up, size = signs_of(courant)
    weights = weights_of(size, reaction, 1.0)
    x = lax.rem(lanes // 8, 4)
    y = lax.rem(lanes, 8)
    sides = sides_of(outer, inner)
    ends(table, below, above, ghosts)

    def coarse_quad(q, carry):
        before, after = lax.rem(q + QUADS - 1, QUADS), lax.rem(q + 1, QUADS)
        values = [[coarse[q, s, h] for s in range(SPECIES)] for h in range(2)]
        column = 32 * (lanes // 32) + 8 * q + y
        for s in range(SPECIES):
            up_x, up_y, up_z = [goes_up[d][s] for d in range(3)]
            at = [EDGE_COARSE + (2 * s + h) * QUADS + q for h in range(2)]
            lows, highs = [line(below, k) for k in at], [line(above, k) for k in at]
            bottoms = (jnp.where(m > 0, lows[0], 0.0), jnp.where(m > 0, lows[1], lows[0]))
            tops = (
                jnp.where(m < CHUNKS - 1, highs[0], highs[1]),
                jnp.where(m < CHUNKS - 1, highs[1], 0.0),
            )
            for h in range(2):
                value = values[h][s]
                ghost = take(jnp.where(up_x, sides(0, 1, s, h), sides(1, 1, s, h)), column, 1)
                from_x = pltpu.roll(value, jnp.where(up_x, 8, 120), 1)
                from_x = jnp.where(x == jnp.where(up_x, 0, 3), ghost, from_x)

                beside = coarse[jnp.where(up_y, before, after), s, h]
                ghost = jnp.where(lanes // 32 == jnp.where(up_y, 3, 0), beside, value)
                ghost = pltpu.roll(ghost, jnp.where(up_y, 25, 103), 1)
                from_y = pltpu.roll(value, jnp.where(up_y, 1, 127), 1)
                from_y = jnp.where(y == jnp.where(up_y, 0, 7), ghost, from_y)

                ghost = jnp.where(up_z, bottoms[h], tops[h])
                from_z = pltpu.roll(value, jnp.where(up_z, 1, 7), 0)
                from_z = jnp.where(rows == jnp.where(up_z, 0, 7), ghost, from_z)

                result = moved(values[h], (from_x, from_y, from_z), size, weights, s)
                provisional[q, s, h] = result
                middle[q, s, h] = 0.5 * (value + result)
        return carry

    lax.fori_loop(0, QUADS, coarse_quad, 0, unroll=4)
    new = (new0, new1)
    weights = weights_of(size, reaction, 0.5)

    def box(i, carry):
        def write(r, s, result):
            new[r][i, s] = result

        fine_step(i, table, (fine0, fine1), coarse, ghosts, sides, goes_up, size, weights, write)
        return carry

    lax.fori_loop(0, BOXES, box, 0, unroll=8)
    edges(new, middle, up_out, down_out, outer_out, inner_out)


def tools_of(courant, coarse_new, folded0, folded1):
    up = [[jnp.maximum(courant[d, s], 0.0) for s in range(SPECIES)] for d in range(3)]
    down = [[jnp.minimum(courant[d, s], 0.0) for s in range(SPECIES)] for d in range(3)]
    taken = lax.broadcasted_iota(jnp.int32, (128, 128), 0)
    given = lax.broadcasted_iota(jnp.int32, (128, 128), 1)
    given_y, fine_y = lax.rem(given, 8), lax.rem(taken, 16)
    same_x = lax.rem(given // 8, 4) == taken // 32

    def summing(rule):
        return jnp.where(same_x & rule(given_y, fine_y), 1.0, 0.0).astype(F32)

    def product(values, matrix):
        return jnp.dot(values, matrix, precision=lax.Precision.HIGHEST, preferred_element_type=F32)

    def fold(tiles, matrix):
        for refs, folded in zip(tiles, (folded0, folded1)):
            pairs = sum(
                ref.reshape(BOXES * SPECIES * 8, 128)[pl.ds(odd, BOXES * SPECIES * 4, stride=2), :]
                for ref in refs
                for odd in range(2)
            )
            folded[...] = product(pairs, matrix)

    def folded_tile(i, s):
        at = pl.ds((i * SPECIES + s) * 4, 4)
        return jnp.concatenate([folded0[at, :], folded1[at, :]])

    def add(q, s, h, where, change):
        coarse_new[q, s, h] = coarse_new[q, s, h] + jnp.where(where, change, 0.0)

    def change_of(here, across, both, beside, rate_out, rate_in, sign):
        return sign * (rate_out * (here - 0.5 * both) + rate_in * (across - 0.125 * beside))

    return up, down, summing, product, fold, folded_tile, add, change_of


def beside_kernel(table, courant, old0, old1, coarse, fine0, fine1, middle, provisional, coarse_new, folded0, folded1):
    _, lanes = iotas()
    y = lax.rem(lanes, 8)
    group = lanes // 32
    up, down, summing, _, fold, folded_tile, add, change_of = tools_of(courant, coarse_new, folded0, folded1)
    coarse_new[...] = provisional[...]

    def rule(given_y, fine_y):
        return ((fine_y == 0) & (given_y == 7)) | ((fine_y == 15) & (given_y == 0))

    fold(((old0, fine0), (old1, fine1)), summing(rule))

    def open_y(i, carry):
        col, half, south, north = [table[STRIDE * i + f] for f in (COL, HALF, SOUTH, NORTH)]
        south_col, north_col = lax.rem(col + GY - 1, GY), lax.rem(col + 1, GY)
        south_quad, north_quad = south_col // 4, north_col // 4
        at_south = (group == lax.rem(south_col, 4)) & (y == 7) & (south < 0)
        at_north = (group == lax.rem(north_col, 4)) & (y == 0) & (north < 0)
        for s in range(SPECIES):
            beside = folded_tile(i, s)
            tile = coarse[col // 4, s, half]
            here = coarse[south_quad, s, half]
            both = here + middle[south_quad, s, half]
            change = change_of(here, turn(tile, -25, 1), both, beside, up[1][s], down[1][s], 1.0)
            add(south_quad, s, half, at_south, change)
            here = coarse[north_quad, s, half]
            both = here + middle[north_quad, s, half]
            change = change_of(here, turn(tile, 25, 1), both, beside, down[1][s], up[1][s], -1.0)
            add(north_quad, s, half, at_north, change)
        return carry

    lax.fori_loop(0, BOXES, open_y, 0, unroll=8)


def second_kernel(
    table, courant, reaction, old0, old1, coarse, old_below, old_above, old_outer, old_inner,
    fine0, fine1, middle, below, above, outer, inner, corrected, out,
    coarse_new, ghosts, result0, result1, folded0, folded1,
):
    rows, lanes = iotas()
    m, part = chunk()
    goes_up, size = signs_of(courant)
    weights = weights_of(size, reaction, 0.5)
    up, down, summing, product, fold, folded_tile, add, change_of = tools_of(courant, coarse_new, folded0, folded1)
    x = lax.rem(lanes // 8, 4)
    y = lax.rem(lanes, 8)
    group = lanes // 32
    ends(table, below, above, ghosts)
    coarse_new[...] = corrected[...]

    def clear(j, carry):
        out[j, :FINE_ROWS, :] = jnp.zeros((FINE_ROWS, 128), F32)
        return carry

    lax.fori_loop(0, GY, clear, 0, unroll=4)
    sides = sides_of(outer, inner)

    def box_step(i, carry):
        t = table[STRIDE * i + SLOT]
        start = lax.rem(t, 2) * 80

        def write(r, s, result):
            out[t // 2, pl.ds(pl.multiple_of(start + (2 * s + r) * 8, 8), 8), :] = result
            (result0, result1)[r][i, s] = result

        fine_step(i, table, (fine0, fine1), middle, ghosts, sides, goes_up, size, weights, write)
        return carry

    lax.fori_loop(0, BOXES, box_step, 0, unroll=8)

    mean_matrix = summing(lambda given_y, fine_y: fine_y // 2 == given_y)

    def open_z(high, row, source, old_source, rate_out, rate_in, sign):
        folded0[:EDGE_COARSE, :] = product(source[:EDGE_COARSE, :] + old_source[:EDGE_COARSE, :], mean_matrix)
        for i in range(BOXES):
            col, half, is_open = [table[STRIDE * i + f] for f in (COL, HALF, OPEN_Z)]
            q = col // 4
            where = (rows == row) & (group == lax.rem(col, 4)) & (half == high) & (is_open > 0)
            for s in range(SPECIES):
                beside = jnp.broadcast_to(folded0[8 * s + i : 8 * s + i + 1, :], (8, 128))
                here = coarse[q, s, 1 - high]
                across = line(old_source, EDGE_COARSE + (2 * s + high) * QUADS + q)
                both = here + middle[q, s, 1 - high]
                change = change_of(here, across, both, beside, rate_out[s], rate_in[s], sign)
                add(q, s, 1 - high, where, change)

    @pl.when(m == CHUNKS - 1)
    def _():
        open_z(1, 7, above, old_above, up[2], down[2], 1.0)

    @pl.when(m == 0)
    def _():
        open_z(0, 0, below, old_below, down[2], up[2], -1.0)

    row_index = 2 * lax.rem(rows, 4)
    last = part > 0
    edge = jnp.where(last, 3, 0)
    sign = jnp.where(last, 1.0, -1.0)
    sums = []
    for s in range(SPECIES):
        totals = [old_outer[0, s, r] + outer[0, s, r] for r in range(2)]
        totals = [take(total + turn(total, -1, 0), row_index, 0) for total in totals]
        total = jnp.where(rows < 4, totals[0], totals[1])
        sums.append(total + turn(total, -1, 1))

    def open_x(q, carry):
        column = 32 * group + 8 * q + y
        for h in range(2):
            box = table[BESIDE + 2 * (4 * q) + h]
            for o in range(1, 4):
                box = jnp.where(group == o, table[BESIDE + 2 * (4 * q + o) + h], box)
            where = (box >= 0) & (x == edge)
            index = 16 * jnp.maximum(box, 0) + 2 * y
            for s in range(SPECIES):
                rate_out = jnp.where(last, up[0][s], down[0][s])
                rate_in = jnp.where(last, down[0][s], up[0][s])
                here = coarse[q, s, h]
                across = take(old_outer[1, s, h], column, 1)
                both = here + middle[q, s, h]
                beside = take(sums[s], index, 1)
                add(q, s, h, where, change_of(here, across, both, beside, rate_out, rate_in, sign))
        return carry

    lax.fori_loop(0, QUADS, open_x, 0, unroll=4)
    fold(((result0,), (result1,)), mean_matrix)

    def cover(i, carry):
        col, half = [table[STRIDE * i + f] for f in (COL, HALF)]
        q = col // 4
        where = group == lax.rem(col, 4)
        for s in range(SPECIES):
            coarse_new[q, s, half] = jnp.where(where, 0.125 * folded_tile(i, s), coarse_new[q, s, half])
        return carry

    lax.fori_loop(0, BOXES, cover, 0, unroll=8)
    for q in range(QUADS):
        for p in range(3):
            at = FINE_ROWS + 8 * p
            tiles = [turn(coarse_new[q, 2 * p + k // 2, k % 2], 32 * k, 1) for k in range(4 if p < 2 else 2)]
            for o in range(4):
                tile = tiles[0]
                for k in range(1, len(tiles)):
                    tile = jnp.where(group == (o + k) % 4, tiles[k], tile)
                out[4 * q + o, at : at + 8, :] = tile


def call(kernel, out_shape, operands, smem, scratch=(), in_spec=VMEM, out_spec=VMEM):
    many = isinstance(out_shape, (list, tuple))
    specs = [out_spec] * len(out_shape) if many and not isinstance(out_spec, list) else out_spec
    return pl.pallas_call(
        kernel,
        out_shape=out_shape,
        in_specs=[SMEM] * smem + [in_spec] * (len(operands) - smem),
        out_specs=specs,
        scratch_shapes=list(scratch),
        compiler_params=pltpu.CompilerParams(vmem_limit_bytes=40 * 1024 * 1024),
    )(*operands)


def exchange(up_edge, down_edge, outer_edge, inner_edge):
    device = lambda g, m, part: g % GX * GY + device_of(m % CHUNKS, part, g % GX)
    all_of = [(g, m, part) for g in range(GX) for m in range(CHUNKS) for part in range(2)]
    axes = ("gx", "gy")
    send = lambda value, target: lax.ppermute(value, axes, [(device(*d), device(*target(*d))) for d in all_of])
    outer = send(outer_edge, lambda g, m, part: (g + 2 * part - 1, m, 1 - part))
    below = send(up_edge, lambda g, m, part: (g, m + 1, part))
    above = send(down_edge, lambda g, m, part: (g, m - 1, part))
    inner = send(inner_edge, lambda g, m, part: (g, m, 1 - part))
    return below, above, outer, inner


def spread(pieces):
    return lax.all_to_all(pieces, "gy", 0, 0, tiled=True)


def shards(coarse, fine, corners, ghost_source, courant, reaction):
    shape = lambda *dims: jax.ShapeDtypeStruct(dims, F32)
    pieces = shape(GY, PIECE_ROWS, 128)
    boxes = shape(BOXES, SPECIES, 8, 128)
    grid = shape(QUADS, SPECIES, 2, 8, 128)
    sent = (shape(EDGE_ROWS, 128),) * 2 + (shape(2, SPECIES, 2, 8, 128),) * 2
    whole = (pltpu.VMEM(coarse.shape, F32), pltpu.VMEM(fine.shape, F32))
    copies = pltpu.SemaphoreType.DMA((2 * SPECIES + 1,))
    integers = lambda *dims: pltpu.SMEM(dims, jnp.int32)
    placed = [pltpu.with_memory_space_constraint(value, pltpu.HBM) for value in (corners.T, ghost_source.T, coarse, fine)]
    sending, table = call(
        pack_kernel,
        [pltpu.VMEM(pieces.shape, F32), jax.ShapeDtypeStruct((TABLE,), jnp.int32)],
        placed,
        0,
        (
            *whole,
            pltpu.SemaphoreType.DMA((2 * SPECIES + 3,)),
            integers(2 * LIST_STRIDE),
            integers(2 * ROW_SLOTS),
            integers(3, 512),
            integers(6, 512),
            pltpu.VMEM((128, 128), F32),
        ),
        HBM,
        [VMEM, SMEM],
    )
    received = spread(sending)
    fine0, fine1, middle, *sending = call(compact_kernel, (boxes, boxes, grid) + sent, (table, received), 1)
    old = (fine0, fine1, middle, *exchange(*sending))
    ghosts = pltpu.VMEM((EDGE_ROWS, 128), F32)
    new0, new1, middle, provisional, *sending = call(
        first_kernel, (boxes, boxes, grid, grid) + sent, (table, courant, reaction) + old, 3, (ghosts,)
    )
    new = (new0, new1, middle, *exchange(*sending))
    folded = (pltpu.VMEM((BOXES * SPECIES * 4, 128), F32),) * 2
    operands = (table, courant) + old[:3] + new[:3] + (provisional,)
    corrected = call(beside_kernel, grid, operands, 2, folded)
    scratch = (
        pltpu.VMEM(grid.shape, F32),
        ghosts,
        pltpu.VMEM(boxes.shape, F32),
        pltpu.VMEM(boxes.shape, F32),
        *folded,
    )
    back = call(second_kernel, pieces, (table, courant, reaction) + old + new + (corrected,), 3, scratch)
    outputs = (shape(*coarse.shape), shape(*fine.shape))
    return call(unpack_kernel, outputs, (spread(back),), 0, (*whole, copies, pltpu.VMEM((128, 128), F32)), VMEM, HBM)


def solution(mesh):
    fine_spec = P(("gx", "gy"), None, None, None, None)
    coarse_spec = P(None, "gx", "gy", None)
    return jax.shard_map(
        shards,
        mesh=mesh,
        in_specs=(coarse_spec, fine_spec, P(), P(), P(), P()),
        out_specs=(coarse_spec, fine_spec),
        check_vma=False,
    )
```

```python
import jax
import jax.numpy as jnp
from jax import lax
from jax.experimental import pallas as pl
from jax.experimental.pallas import tpu as pltpu
from jax.sharding import PartitionSpec as P

CHIP_OF = (0, 1, 2, 3, 7, 6, 5, 4)
SPECIES = 5
GX = 16
GY = 16
BOXES = 8
CHUNKS = 8
QUADS = 4
ROW_SLOTS = 32
FINE_ROWS = 160
PIECE_ROWS = 184
EDGE_ROWS = 80
EDGE_COARSE = 40
STRIDE = 16
LIST_STRIDE = 40
F32 = jnp.float32
SLOT, COL, HALF, WEST, EAST, SOUTH, NORTH, BOTTOM, TOP, OPEN_Z = range(10)
BESIDE = BOXES * STRIDE
OWN = BESIDE + 2 * GY
TABLE = OWN + 4
SHELL_ROWS = 80
PLANE_ROWS = 104
BACK_ROWS = 128

VMEM = pl.BlockSpec(memory_space=pltpu.VMEM)
SMEM = pl.BlockSpec(memory_space=pltpu.SMEM)
HBM = pl.BlockSpec(memory_space=pltpu.HBM)


def device_of(m, part, row):
    turned = (GY // 2) * (row % 2) if isinstance(row, int) else (GY // 2) * lax.rem(row, 2)
    place = 2 * CHIP_OF[m] + part + turned
    return place % GY if isinstance(row, int) else lax.rem(place, GY)


def chunk():
    turned = (GY // 2) * lax.rem(lax.axis_index("gx"), 2)
    j = lax.rem(lax.axis_index("gy") + turned, GY)
    q = j // 2
    return jnp.where(q < 4, q, 11 - q), lax.rem(j, 2)


def fill_table(corners, sources, table, listed, ranks):
    row = lax.axis_index("gx")
    m, part = chunk()
    groups = (row, lax.rem(row + jnp.where(part > 0, 1, GX - 1), GX))

    def scan(t, counts):
        new_counts = []
        for r in range(2):
            live = corners[0, groups[r] * ROW_SLOTS + t] >= 0
            listed[r * LIST_STRIDE + counts[r]] = t
            ranks[r * ROW_SLOTS + t] = counts[r]
            new_counts.append(counts[r] + jnp.where(live, 1, 0))
        return tuple(new_counts)

    lax.fori_loop(0, ROW_SLOTS, scan, (jnp.int32(0), jnp.int32(0)), unroll=True)

    def rank(r, source):
        found = ranks[r * ROW_SLOTS + lax.rem(jnp.maximum(source, 0), ROW_SLOTS)]
        return jnp.where(source >= 0, found, -1)

    for k in range(2 * GY):
        table[BESIDE + k] = -1
    for k in range(2):
        slot = row * ROW_SLOTS + 2 * lax.axis_index("gy") + k
        table[OWN + 2 * k] = jnp.where(corners[0, slot] >= 0, 1, 0)
        table[OWN + 2 * k + 1] = corners[2, slot] // 128
    face = jnp.where(part > 0, 0, 1)
    for i in range(BOXES):
        t = listed[i]
        slot = groups[0] * ROW_SLOTS + t
        south, north, bottom, top = [sources[f, slot] for f in range(2, 6)]
        beside = rank(1, sources[1 - face, slot])
        half = corners[2, slot] // 128
        base = STRIDE * i
        table[base + SLOT] = t
        table[base + COL] = corners[1, slot] // 16
        table[base + HALF] = half
        table[base + WEST] = jnp.where(part > 0, i, beside)
        table[base + EAST] = jnp.where(part > 0, beside, i)
        table[base + SOUTH] = rank(0, south)
        table[base + NORTH] = rank(0, north)
        table[base + BOTTOM] = jnp.where(m > 0, i, rank(0, bottom))
        table[base + TOP] = jnp.where(m < CHUNKS - 1, i, rank(0, top))
        table[base + OPEN_Z] = jnp.where(jnp.where(half > 0, bottom, top) < 0, 1, 0)
        other = groups[1] * ROW_SLOTS + listed[LIST_STRIDE + i]
        spot = corners[1, other] // 16 * 2 + corners[2, other] // 128
        table[BESIDE + spot] = jnp.where(sources[face, other] < 0, i, -1)


def pack_kernel(
    corners_in, sources_in, coarse_in, fine_in, out, table, coarse, fine, loaded, listed, ranks, corners, sources,
    around,
):
    row, column = lax.axis_index("gx"), lax.axis_index("gy")
    blocks = [(k, s) for k in range(2) for s in range(SPECIES)]
    loads = [pltpu.make_async_copy(fine_in.at[k, s], fine.at[k, s], loaded.at[n]) for n, (k, s) in enumerate(blocks)]
    loads.append(pltpu.make_async_copy(coarse_in, coarse, loaded.at[len(blocks)]))
    integers = (
        pltpu.make_async_copy(corners_in, corners, loaded.at[len(blocks) + 1]),
        pltpu.make_async_copy(sources_in, sources, loaded.at[len(blocks) + 2]),
    )
    for load in (*integers, *loads):
        load.start()
    for load in (*integers, *loads):
        load.wait()
    fill_table(corners, sources, table, listed, ranks)
    for n, (k, s) in enumerate(blocks):
        turned = fine[k, s].reshape(256, 128).T
        at = (k * SPECIES + s) * 16
        for m in range(CHUNKS):
            for part in range(2):
                block = turned[16 * m : 16 * m + 16, 128 * part : 128 * part + 128]
                out[device_of(m, part, row), at : at + 16, :] = block
    for p in range(3):
        at = FINE_ROWS + 8 * p
        for part in range(2):
            blocks = []
            for s in (2 * p, 2 * p + 1):
                block = coarse[min(s, 4), 4 * part : 4 * part + 4].reshape(32, 128)
                blocks += [block, pltpu.roll(block, 64, 1)]
            for n, block in enumerate(blocks):
                around[pl.ds(pl.multiple_of(32 * lax.rem(column + n, 4), 32), 32), :] = block
            turned = around[...].T
            for m in range(CHUNKS):
                out[device_of(m, part, row), at : at + 8, :] = turned[8 * m : 8 * m + 8]


def unpack_kernel(table, received, interior, coarse_out, fine_out, coarse, fine, stored, around, shells, planes):
    row, column = lax.axis_index("gx"), lax.axis_index("gy")
    rows, lanes = iotas()
    stores = []

    def send(source, target):
        stores.append(pltpu.make_async_copy(source, target, stored.at[len(stores)]))
        stores[-1].start()

    live = [table[OWN + 2 * k] > 0 for k in range(2)]
    high = [table[OWN + 2 * k + 1] > 0 for k in range(2)]
    in_plane = [jnp.where(high[k], lanes, 127 - lanes) < 2 for k in range(2)]
    for part in range(2):
        parts = []
        for k in range(2):
            source = jnp.where(high[k], device_of(0, part, row), device_of(CHUNKS - 1, part, row))
            parts.append(received[source, PLANE_ROWS + 10 * k : PLANE_ROWS + 10 * k + 10, :])
        planes[part] = jnp.concatenate([*parts, jnp.zeros((108, 128), F32)]).T
    for s in range(SPECIES):
        for part in range(2):
            pieces = [received[device_of(m, part, row), 16 * s : 16 * s + 16, :] for m in range(CHUNKS)]
            shells[part] = jnp.concatenate(pieces).T
        for k in range(2):
            shift = lax.rem(jnp.where(high[k], 128, 254) - (10 * k + 2 * s), 128)
            for x in range(16):
                part, at_x = x // 8, x % 8
                depth = at_x if part == 0 else 7 - at_x
                if depth < 2:
                    at = 64 * k + 16 * depth
                    tiles = [shells[part, at + 8 * j : at + 8 * j + 8, :] for j in range(2)]
                else:
                    at = 64 * k + 32 + 8 * ((depth - 2) // 2)
                    tile = shells[part, at : at + 8, :]
                    sides = (tile, tile) if depth % 2 == 0 else (turn(tile, -2, 0), turn(tile, 2, 0))
                    tiles = []
                    for j in range(2):
                        at = 16 * at_x + 8 * j
                        plane = pltpu.roll(planes[part, at : at + 8, :], shift, 1)
                        inner = jnp.where(in_plane[k], plane, interior[k, s, x, 8 * j : 8 * j + 8, :])
                        tiles.append(jnp.where(rows >= 6 if j else rows < 2, sides[j], inner))
                for j in range(2):
                    fine[k, s, x, 8 * j : 8 * j + 8, :] = jnp.where(live[k], tiles[j], 0.0)
            send(fine.at[k, s], fine_out.at[k, s])
    left = lax.broadcasted_iota(jnp.int32, (32, 128), 1) < 64
    for p in range(3):
        at = SHELL_ROWS + 8 * p
        pieces = [received[device_of(m, part, row), at : at + 8, :] for part in range(2) for m in range(CHUNKS)]
        around[...] = jnp.concatenate(pieces).T
        for s in range(2 * p, min(2 * p + 2, SPECIES)):
            low, high = [
                around[pl.ds(pl.multiple_of(32 * lax.rem(column + 2 * (s - 2 * p) + h, 4), 32), 32), :] for h in range(2)
            ]
            coarse[s, 0:4] = jnp.where(left, low, pltpu.roll(high, 64, 1)).reshape(4, 8, 128)
            coarse[s, 4:8] = jnp.where(left, pltpu.roll(low, 64, 1), high).reshape(4, 8, 128)
    send(coarse, coarse_out)
    for store in stores:
        store.wait()


def interior_kernel(courant, reaction, fine, out, between):
    rows, lanes = iotas()
    goes_up, size = signs_of(courant)
    weights = weights_of(size, reaction, 0.5)

    def step(load, store, first, last):
        def plane(x, carry):
            values = [[load(s, x, j) for s in range(SPECIES)] for j in range(2)]
            for s in range(SPECIES):
                up_x, up_y, up_z = [goes_up[d][s] for d in range(3)]
                before = x + jnp.where(up_x, -1, 1)
                low, high = [pltpu.roll(values[j][s], jnp.where(up_y, 1, 7), 0) for j in range(2)]
                from_y = (
                    jnp.where((rows == 7) & jnp.logical_not(up_y), high, low),
                    jnp.where((rows == 0) & up_y, low, high),
                )
                for j in range(2):
                    from_z = pltpu.roll(values[j][s], jnp.where(up_z, 1, 127), 1)
                    from_z = jnp.where(lanes == jnp.where(up_z, 0, 127), 0.0, from_z)
                    upwind = (load(s, before, j), from_y[j], from_z)
                    store(s, x, j, moved(values[j], upwind, size, weights, s))
            return carry

        lax.fori_loop(first, last, plane, 0, unroll=2)

    for k in range(2):

        def put(ref):
            def store(s, x, j, tile):
                ref[s, x, 8 * j : 8 * j + 8, :] = tile

            return store

        def get(ref):
            return lambda s, x, j: ref[s, x, 8 * j : 8 * j + 8, :]

        step(get(fine.at[k]), put(between), 1, 15)
        step(get(between), put(out.at[k]), 2, 14)


def iotas():
    return lax.broadcasted_iota(jnp.int32, (8, 128), 0), lax.broadcasted_iota(jnp.int32, (8, 128), 1)


def take(tile, index, axis):
    return jnp.take_along_axis(tile, index, axis=axis, mode="promise_in_bounds")


def turn(tile, shift, axis):
    return pltpu.roll(tile, shift % tile.shape[axis], axis)


def line(ref, index):
    return jnp.broadcast_to(ref[pl.ds(index, 1), :], (8, 128))


def edges(fine, coarse, up_out, down_out, outer_out, inner_out):
    _, lanes = iotas()
    _, part = chunk()
    last = part > 0
    for s in range(SPECIES):
        up_out[8 * s : 8 * s + 8, :] = fine[1][:, s, 7, :]
        down_out[8 * s : 8 * s + 8, :] = fine[0][:, s, 0, :]
        for h in range(2):
            at = EDGE_COARSE + (2 * s + h) * QUADS
            up_out[at : at + QUADS, :] = coarse[:, s, h, 7, :]
            down_out[at : at + QUADS, :] = coarse[:, s, h, 0, :]
        for r in range(2):
            low = high = coarse_low = coarse_high = jnp.zeros((8, 128), F32)
            for i in range(BOXES):
                here = lanes // 16 == i
                low = jnp.where(here, turn(fine[r][i, s], 16 * i, 1), low)
                high = jnp.where(here, turn(fine[r][i, s], 16 * i + 16, 1), high)
            for q in range(QUADS):
                here = lax.rem(lanes // 8, 4) == q
                coarse_low = jnp.where(here, turn(coarse[q, s, r], 8 * q, 1), coarse_low)
                coarse_high = jnp.where(here, turn(coarse[q, s, r], 8 * q - 24, 1), coarse_high)
            outer_out[0, s, r] = jnp.where(last, high, low)
            inner_out[0, s, r] = jnp.where(last, low, high)
            outer_out[1, s, r] = jnp.where(last, coarse_high, coarse_low)
            inner_out[1, s, r] = jnp.where(last, coarse_low, coarse_high)


def compact_kernel(table, received, fine0, fine1, coarse, up_out, down_out, outer_out, inner_out):
    _, lanes = iotas()
    for i in range(BOXES):
        t = table[STRIDE * i + SLOT]
        start = pl.multiple_of(lax.rem(t, 2) * 80, 8)
        box = received[t // 2, pl.ds(start, 80), :].reshape(SPECIES, 2, 8, 128)
        fine0[i] = box[:, 0]
        fine1[i] = box[:, 1]
    for q in range(QUADS):
        for p in range(3):
            at = FINE_ROWS + 8 * p
            tiles = [received[4 * q + o, at : at + 8, :] for o in range(4)]
            for k in range(4 if p < 2 else 2):
                tile = tiles[0]
                for o in range(1, 4):
                    tile = jnp.where(lanes // 32 == (o + k) % 4, tiles[o], tile)
                coarse[q, 2 * p + k // 2, k % 2] = turn(tile, -32 * k, 1)
    edges((fine0, fine1), coarse, up_out, down_out, outer_out, inner_out)


def signs_of(courant):
    goes_up = [[courant[d, s] >= 0.0 for s in range(SPECIES)] for d in range(3)]
    size = [[jnp.abs(courant[d, s]) for s in range(SPECIES)] for d in range(3)]
    return goes_up, size


def weights_of(size, reaction, factor):
    weights = [[factor * reaction[s, e] for e in range(SPECIES)] for s in range(SPECIES)]
    for s in range(SPECIES):
        weights[s][s] = weights[s][s] + (1.0 - size[0][s] - size[1][s] - size[2][s])
    return weights


def moved(values, upwind, size, weights, s):
    total = weights[s][0] * values[0]
    for e in range(1, SPECIES):
        total = total + weights[s][e] * values[e]
    for d in range(3):
        total = total + size[d][s] * upwind[d]
    return total


def ends(table, below, above, ghosts):
    _, lanes = iotas()
    m, _ = chunk()
    ghosts[:EDGE_COARSE, :] = below[:EDGE_COARSE, :]
    ghosts[EDGE_COARSE:, :] = above[:EDGE_COARSE, :]

    def replace(side, source, name, high):
        for i in range(BOXES):
            col, half, found = [table[STRIDE * i + f] for f in (COL, HALF, name)]
            inside = 32 * lax.rem(col, 4) + 8 * (lanes // 32) + lax.rem(lanes, 16) // 2
            for s in range(SPECIES):
                other = take(line(source, EDGE_COARSE + (2 * s + side) * QUADS + col // 4), inside, 1)
                other = jnp.where(half == high, other, 0.0)
                ghost = jnp.where(found >= 0, line(source, 8 * s + jnp.maximum(found, 0)), other)
                at = EDGE_COARSE * side + 8 * s + i
                ghosts[at : at + 1, :] = ghost[:1]

    @pl.when(m == 0)
    def _():
        replace(0, below, BOTTOM, 1)

    @pl.when(m == CHUNKS - 1)
    def _():
        replace(1, above, TOP, 0)


def fine_step(i, table, fine, coarse, ghosts, sides, goes_up, size, weights, write):
    rows, lanes = iotas()
    field = lambda f: table[STRIDE * i + f]
    col, half = field(COL), field(HALF)
    lower_col, upper_col = lax.rem(col + GY - 1, GY), lax.rem(col + 1, GY)
    y = lax.rem(lanes, 16)
    found = [field(f) for f in (WEST, EAST, SOUTH, NORTH)]
    there = [source >= 0 for source in found]
    at = [jnp.maximum(source, 0) for source in found]
    beside = 32 * lax.rem(col, 4) + 8 * (col // 4) + y // 2
    lane_x = [jnp.where(there[f], 16 * at[f] + y, beside) for f in range(2)]
    own_x, line_x = lanes - y, 8 * (lanes // 32)
    lane_y = [
        jnp.where(there[2], own_x + 15, 32 * lax.rem(lower_col, 4) + line_x + 7),
        jnp.where(there[3], own_x, 32 * lax.rem(upper_col, 4) + line_x),
    ]
    row_of = [[jnp.where(is_there, rows, 4 * r + rows // 2) for is_there in there] for r in range(2)]
    kind = [jnp.where(is_there, 0, 1) for is_there in there]
    values = [[fine[r][i, s] for s in range(SPECIES)] for r in range(2)]
    for s in range(SPECIES):
        up_x, up_y, up_z = [goes_up[d][s] for d in range(3)]
        shift_x, edge_x = jnp.where(up_x, 16, 112), lanes // 16 == jnp.where(up_x, 0, 7)
        shift_y, edge_y = jnp.where(up_y, 1, 127), y == jnp.where(up_y, 0, 15)
        shift_z, edge_z = jnp.where(up_z, 1, 7), rows == jnp.where(up_z, 0, 7)
        is_there = jnp.where(up_y, found[2], found[3]) >= 0
        box_y = jnp.where(up_y, at[2], at[3])
        quad_y = jnp.where(up_y, lower_col, upper_col) // 4
        coarse_y = coarse[quad_y, s, half]
        index_x = jnp.where(up_x, lane_x[0], lane_x[1])
        index_y = jnp.where(up_y, lane_y[0], lane_y[1])

        low, high = values[0][s], values[1][s]
        first = pltpu.roll(jnp.where(up_z, low, high), shift_z, 0)
        second = pltpu.roll(jnp.where(up_z, high, low), shift_z, 0)
        second = jnp.where(edge_z, first, second)
        first = jnp.where(edge_z, line(ghosts, jnp.where(up_z, 0, EDGE_COARSE) + 8 * s + i), first)
        from_z = (jnp.where(up_z, first, second), jnp.where(up_z, second, first))

        for r in range(2):
            value = values[r][s]
            west = sides(0, kind[0], s, jnp.where(there[0], r, half))
            east = sides(1, kind[1], s, jnp.where(there[1], r, half))
            ghost = take(jnp.where(up_x, west, east), jnp.where(up_x, row_of[r][0], row_of[r][1]), 0)
            ghost = take(ghost, index_x, 1)
            from_x = jnp.where(edge_x, ghost, pltpu.roll(value, shift_x, 1))
            ghost = take(
                jnp.where(is_there, fine[r][box_y, s], coarse_y), jnp.where(up_y, row_of[r][2], row_of[r][3]), 0
            )
            ghost = take(ghost, index_y, 1)
            from_y = jnp.where(edge_y, ghost, pltpu.roll(value, shift_y, 1))
            write(r, s, moved(values[r], (from_x, from_y, from_z[r]), size, weights, s))


def sides_of(outer, inner):
    _, part = chunk()

    def pick(side, kind, s, at):
        one, other = outer[kind, s, at], inner[kind, s, at]
        return jnp.where(part == side, one, other)

    return pick


def first_kernel(
    table, courant, reaction, fine0, fine1, coarse, below, above, outer, inner,
    new0, new1, middle, provisional, up_out, down_out, outer_out, inner_out, ghosts,
):
    rows, lanes = iotas()
    m, _ = chunk()
    goes_up, size = signs_of(courant)
    weights = weights_of(size, reaction, 1.0)
    x = lax.rem(lanes // 8, 4)
    y = lax.rem(lanes, 8)
    sides = sides_of(outer, inner)
    ends(table, below, above, ghosts)

    def coarse_quad(q, carry):
        before, after = lax.rem(q + QUADS - 1, QUADS), lax.rem(q + 1, QUADS)
        values = [[coarse[q, s, h] for s in range(SPECIES)] for h in range(2)]
        column = 32 * (lanes // 32) + 8 * q + y
        for s in range(SPECIES):
            up_x, up_y, up_z = [goes_up[d][s] for d in range(3)]
            at = [EDGE_COARSE + (2 * s + h) * QUADS + q for h in range(2)]
            lows, highs = [line(below, k) for k in at], [line(above, k) for k in at]
            bottoms = (jnp.where(m > 0, lows[0], 0.0), jnp.where(m > 0, lows[1], lows[0]))
            tops = (
                jnp.where(m < CHUNKS - 1, highs[0], highs[1]),
                jnp.where(m < CHUNKS - 1, highs[1], 0.0),
            )
            for h in range(2):
                value = values[h][s]
                ghost = take(jnp.where(up_x, sides(0, 1, s, h), sides(1, 1, s, h)), column, 1)
                from_x = pltpu.roll(value, jnp.where(up_x, 8, 120), 1)
                from_x = jnp.where(x == jnp.where(up_x, 0, 3), ghost, from_x)

                beside = coarse[jnp.where(up_y, before, after), s, h]
                ghost = jnp.where(lanes // 32 == jnp.where(up_y, 3, 0), beside, value)
                ghost = pltpu.roll(ghost, jnp.where(up_y, 25, 103), 1)
                from_y = pltpu.roll(value, jnp.where(up_y, 1, 127), 1)
                from_y = jnp.where(y == jnp.where(up_y, 0, 7), ghost, from_y)

                ghost = jnp.where(up_z, bottoms[h], tops[h])
                from_z = pltpu.roll(value, jnp.where(up_z, 1, 7), 0)
                from_z = jnp.where(rows == jnp.where(up_z, 0, 7), ghost, from_z)

                result = moved(values[h], (from_x, from_y, from_z), size, weights, s)
                provisional[q, s, h] = result
                middle[q, s, h] = 0.5 * (value + result)
        return carry

    lax.fori_loop(0, QUADS, coarse_quad, 0, unroll=4)
    new = (new0, new1)
    weights = weights_of(size, reaction, 0.5)

    def box(i, carry):
        def write(r, s, result):
            new[r][i, s] = result

        fine_step(i, table, (fine0, fine1), coarse, ghosts, sides, goes_up, size, weights, write)
        return carry

    lax.fori_loop(0, BOXES, box, 0, unroll=8)
    edges(new, middle, up_out, down_out, outer_out, inner_out)


def tools_of(courant, coarse_new, folded0, folded1):
    up = [[jnp.maximum(courant[d, s], 0.0) for s in range(SPECIES)] for d in range(3)]
    down = [[jnp.minimum(courant[d, s], 0.0) for s in range(SPECIES)] for d in range(3)]
    taken = lax.broadcasted_iota(jnp.int32, (128, 128), 0)
    given = lax.broadcasted_iota(jnp.int32, (128, 128), 1)
    given_y, fine_y = lax.rem(given, 8), lax.rem(taken, 16)
    same_x = lax.rem(given // 8, 4) == taken // 32

    def summing(rule):
        return jnp.where(same_x & rule(given_y, fine_y), 1.0, 0.0).astype(F32)

    def product(values, matrix):
        return jnp.dot(values, matrix, precision=lax.Precision.HIGHEST, preferred_element_type=F32)

    def fold(tiles, matrix):
        for refs, folded in zip(tiles, (folded0, folded1)):
            pairs = sum(
                ref.reshape(BOXES * SPECIES * 8, 128)[pl.ds(odd, BOXES * SPECIES * 4, stride=2), :]
                for ref in refs
                for odd in range(2)
            )
            folded[...] = product(pairs, matrix)

    def folded_tile(i, s):
        at = pl.ds((i * SPECIES + s) * 4, 4)
        return jnp.concatenate([folded0[at, :], folded1[at, :]])

    def add(q, s, h, where, change):
        coarse_new[q, s, h] = coarse_new[q, s, h] + jnp.where(where, change, 0.0)

    def change_of(here, across, both, beside, rate_out, rate_in, sign):
        return sign * (rate_out * (here - 0.5 * both) + rate_in * (across - 0.125 * beside))

    return up, down, summing, product, fold, folded_tile, add, change_of


def beside_kernel(table, courant, old0, old1, coarse, fine0, fine1, middle, provisional, coarse_new, folded0, folded1):
    _, lanes = iotas()
    y = lax.rem(lanes, 8)
    group = lanes // 32
    up, down, summing, _, fold, folded_tile, add, change_of = tools_of(courant, coarse_new, folded0, folded1)
    coarse_new[...] = provisional[...]

    def rule(given_y, fine_y):
        return ((fine_y == 0) & (given_y == 7)) | ((fine_y == 15) & (given_y == 0))

    fold(((old0, fine0), (old1, fine1)), summing(rule))

    def open_y(i, carry):
        col, half, south, north = [table[STRIDE * i + f] for f in (COL, HALF, SOUTH, NORTH)]
        south_col, north_col = lax.rem(col + GY - 1, GY), lax.rem(col + 1, GY)
        south_quad, north_quad = south_col // 4, north_col // 4
        at_south = (group == lax.rem(south_col, 4)) & (y == 7) & (south < 0)
        at_north = (group == lax.rem(north_col, 4)) & (y == 0) & (north < 0)
        for s in range(SPECIES):
            beside = folded_tile(i, s)
            tile = coarse[col // 4, s, half]
            here = coarse[south_quad, s, half]
            both = here + middle[south_quad, s, half]
            change = change_of(here, turn(tile, -25, 1), both, beside, up[1][s], down[1][s], 1.0)
            add(south_quad, s, half, at_south, change)
            here = coarse[north_quad, s, half]
            both = here + middle[north_quad, s, half]
            change = change_of(here, turn(tile, 25, 1), both, beside, down[1][s], up[1][s], -1.0)
            add(north_quad, s, half, at_north, change)
        return carry

    lax.fori_loop(0, BOXES, open_y, 0, unroll=8)


def second_kernel(
    table, courant, reaction, old0, old1, coarse, old_below, old_above, old_outer, old_inner,
    fine0, fine1, middle, below, above, outer, inner, corrected, out,
    coarse_new, ghosts, result0, result1, folded0, folded1,
):
    rows, lanes = iotas()
    m, part = chunk()
    goes_up, size = signs_of(courant)
    weights = weights_of(size, reaction, 0.5)
    up, down, summing, product, fold, folded_tile, add, change_of = tools_of(courant, coarse_new, folded0, folded1)
    x = lax.rem(lanes // 8, 4)
    y = lax.rem(lanes, 8)
    group = lanes // 32
    ends(table, below, above, ghosts)
    coarse_new[...] = corrected[...]

    sides = sides_of(outer, inner)

    def box_step(i, carry):
        def write(r, s, result):
            (result0, result1)[r][i, s] = result

        fine_step(i, table, (fine0, fine1), middle, ghosts, sides, goes_up, size, weights, write)
        return carry

    lax.fori_loop(0, BOXES, box_step, 0, unroll=8)

    place = lax.rem(lanes, 64)
    rest = jnp.maximum(place - 32, 0)
    slot = lax.rem(rest, 8)
    is_second = (slot >= 2) & (slot < 6)
    depth = jnp.where(place < 32, place // 16, 2 + 2 * (rest // 8) + jnp.where(is_second, 1, 0))
    depth = jnp.minimum(depth, 7)
    rest_y = jnp.where(is_second, slot - 2, slot)
    rest_y = jnp.where(slot >= 4, jnp.where(is_second, slot + 10, slot + 8), rest_y)
    shell_y = jnp.where(place < 32, lax.rem(place, 16), rest_y)
    shell_index = 16 * jnp.where(part > 0, 7 - depth, depth) + shell_y

    def pack_box(i, carry):
        t = table[STRIDE * i + SLOT]
        k = lax.rem(t, 2)
        mine = lanes // 64 == k
        for s in range(SPECIES):
            for r, result in enumerate((result0, result1)):
                at = (2 * s + r) * 8
                packed = take(result[i, s], shell_index, 1)
                out[t // 2, at : at + 8, :] = jnp.where(mine, packed, out[t // 2, at : at + 8, :])
            plane = jnp.where(m == 0, result0[i, s, 0:2, :], result1[i, s, 6:8, :])
            out[t // 2, pl.ds(PLANE_ROWS + 10 * k + 2 * s, 2), :] = plane
        return carry

    lax.fori_loop(0, BOXES, pack_box, 0, unroll=4)
    mean_matrix = summing(lambda given_y, fine_y: fine_y // 2 == given_y)

    def open_z(high, row, source, old_source, rate_out, rate_in, sign):
        folded0[:EDGE_COARSE, :] = product(source[:EDGE_COARSE, :] + old_source[:EDGE_COARSE, :], mean_matrix)
        for i in range(BOXES):
            col, half, is_open = [table[STRIDE * i + f] for f in (COL, HALF, OPEN_Z)]
            q = col // 4
            where = (rows == row) & (group == lax.rem(col, 4)) & (half == high) & (is_open > 0)
            for s in range(SPECIES):
                beside = jnp.broadcast_to(folded0[8 * s + i : 8 * s + i + 1, :], (8, 128))
                here = coarse[q, s, 1 - high]
                across = line(old_source, EDGE_COARSE + (2 * s + high) * QUADS + q)
                both = here + middle[q, s, 1 - high]
                change = change_of(here, across, both, beside, rate_out[s], rate_in[s], sign)
                add(q, s, 1 - high, where, change)

    @pl.when(m == CHUNKS - 1)
    def _():
        open_z(1, 7, above, old_above, up[2], down[2], 1.0)

    @pl.when(m == 0)
    def _():
        open_z(0, 0, below, old_below, down[2], up[2], -1.0)

    row_index = 2 * lax.rem(rows, 4)
    last = part > 0
    edge = jnp.where(last, 3, 0)
    sign = jnp.where(last, 1.0, -1.0)
    sums = []
    for s in range(SPECIES):
        totals = [old_outer[0, s, r] + outer[0, s, r] for r in range(2)]
        totals = [take(total + turn(total, -1, 0), row_index, 0) for total in totals]
        total = jnp.where(rows < 4, totals[0], totals[1])
        sums.append(total + turn(total, -1, 1))

    def open_x(q, carry):
        column = 32 * group + 8 * q + y
        for h in range(2):
            box = table[BESIDE + 2 * (4 * q) + h]
            for o in range(1, 4):
                box = jnp.where(group == o, table[BESIDE + 2 * (4 * q + o) + h], box)
            where = (box >= 0) & (x == edge)
            index = 16 * jnp.maximum(box, 0) + 2 * y
            for s in range(SPECIES):
                rate_out = jnp.where(last, up[0][s], down[0][s])
                rate_in = jnp.where(last, down[0][s], up[0][s])
                here = coarse[q, s, h]
                across = take(old_outer[1, s, h], column, 1)
                both = here + middle[q, s, h]
                beside = take(sums[s], index, 1)
                add(q, s, h, where, change_of(here, across, both, beside, rate_out, rate_in, sign))
        return carry

    lax.fori_loop(0, QUADS, open_x, 0, unroll=4)
    fold(((result0,), (result1,)), mean_matrix)

    def cover(i, carry):
        col, half = [table[STRIDE * i + f] for f in (COL, HALF)]
        q = col // 4
        where = group == lax.rem(col, 4)
        for s in range(SPECIES):
            coarse_new[q, s, half] = jnp.where(where, 0.125 * folded_tile(i, s), coarse_new[q, s, half])
        return carry

    lax.fori_loop(0, BOXES, cover, 0, unroll=8)
    for q in range(QUADS):
        for p in range(3):
            at = SHELL_ROWS + 8 * p
            tiles = [turn(coarse_new[q, 2 * p + k // 2, k % 2], 32 * k, 1) for k in range(4 if p < 2 else 2)]
            for o in range(4):
                tile = tiles[0]
                for k in range(1, len(tiles)):
                    tile = jnp.where(group == (o + k) % 4, tiles[k], tile)
                out[4 * q + o, at : at + 8, :] = tile


def call(kernel, out_shape, operands, smem, scratch=(), in_spec=VMEM, out_spec=VMEM):
    many = isinstance(out_shape, (list, tuple))
    specs = [out_spec] * len(out_shape) if many and not isinstance(out_spec, list) else out_spec
    return pl.pallas_call(
        kernel,
        out_shape=out_shape,
        in_specs=[SMEM] * smem + [in_spec] * (len(operands) - smem),
        out_specs=specs,
        scratch_shapes=list(scratch),
        compiler_params=pltpu.CompilerParams(vmem_limit_bytes=40 * 1024 * 1024),
    )(*operands)


def exchange(up_edge, down_edge, outer_edge, inner_edge):
    device = lambda g, m, part: g % GX * GY + device_of(m % CHUNKS, part, g % GX)
    all_of = [(g, m, part) for g in range(GX) for m in range(CHUNKS) for part in range(2)]
    axes = ("gx", "gy")
    send = lambda value, target: lax.ppermute(value, axes, [(device(*d), device(*target(*d))) for d in all_of])
    outer = send(outer_edge, lambda g, m, part: (g + 2 * part - 1, m, 1 - part))
    below = send(up_edge, lambda g, m, part: (g, m + 1, part))
    above = send(down_edge, lambda g, m, part: (g, m - 1, part))
    inner = send(inner_edge, lambda g, m, part: (g, m, 1 - part))
    return below, above, outer, inner


def spread(pieces):
    return lax.all_to_all(pieces, "gy", 0, 0, tiled=True)


def shards(coarse, fine, corners, ghost_source, courant, reaction):
    shape = lambda *dims: jax.ShapeDtypeStruct(dims, F32)
    pieces = shape(GY, PIECE_ROWS, 128)
    boxes = shape(BOXES, SPECIES, 8, 128)
    grid = shape(QUADS, SPECIES, 2, 8, 128)
    sent = (shape(EDGE_ROWS, 128),) * 2 + (shape(2, SPECIES, 2, 8, 128),) * 2
    whole = (pltpu.VMEM(coarse.shape, F32), pltpu.VMEM(fine.shape, F32))
    copies = pltpu.SemaphoreType.DMA((2 * SPECIES + 1,))
    integers = lambda *dims: pltpu.SMEM(dims, jnp.int32)
    placed = [pltpu.with_memory_space_constraint(value, pltpu.HBM) for value in (corners.T, ghost_source.T, coarse, fine)]
    sending, table = call(
        pack_kernel,
        [pltpu.VMEM(pieces.shape, F32), jax.ShapeDtypeStruct((TABLE,), jnp.int32)],
        placed,
        0,
        (
            *whole,
            pltpu.SemaphoreType.DMA((2 * SPECIES + 3,)),
            integers(2 * LIST_STRIDE),
            integers(2 * ROW_SLOTS),
            integers(3, 512),
            integers(6, 512),
            pltpu.VMEM((128, 128), F32),
        ),
        HBM,
        [VMEM, SMEM],
    )
    received = spread(sending)
    fine0, fine1, middle, *sending = call(compact_kernel, (boxes, boxes, grid) + sent, (table, received), 1)
    old = (fine0, fine1, middle, *exchange(*sending))
    between = (pltpu.VMEM(fine.shape[1:], F32),)
    held, _ = lax.optimization_barrier((fine, old[0]))
    interior = call(interior_kernel, shape(*fine.shape), (courant, reaction, held), 2, between)
    interior, *old = lax.optimization_barrier((interior, *old))
    old = tuple(old)
    ghosts = pltpu.VMEM((EDGE_ROWS, 128), F32)
    new0, new1, middle, provisional, *sending = call(
        first_kernel, (boxes, boxes, grid, grid) + sent, (table, courant, reaction) + old, 3, (ghosts,)
    )
    new = (new0, new1, middle, *exchange(*sending))
    folded = (pltpu.VMEM((BOXES * SPECIES * 4, 128), F32),) * 2
    operands = (table, courant) + old[:3] + new[:3] + (provisional,)
    corrected = call(beside_kernel, grid, operands, 2, folded)
    scratch = (
        pltpu.VMEM(grid.shape, F32),
        ghosts,
        pltpu.VMEM(boxes.shape, F32),
        pltpu.VMEM(boxes.shape, F32),
        *folded,
    )
    back = call(
        second_kernel, shape(GY, BACK_ROWS, 128), (table, courant, reaction) + old + new + (corrected,), 3, scratch
    )
    outputs = (shape(*coarse.shape), shape(*fine.shape))
    scratch = (
        *whole,
        copies,
        pltpu.VMEM((128, 128), F32),
        pltpu.VMEM((2, 128, 128), F32),
        pltpu.VMEM((2, 128, 128), F32),
    )
    return call(unpack_kernel, outputs, (table, spread(back), interior), 1, scratch, VMEM, HBM)


def solution(mesh):
    fine_spec = P(("gx", "gy"), None, None, None, None)
    coarse_spec = P(None, "gx", "gy", None)
    return jax.shard_map(
        shards,
        mesh=mesh,
        in_specs=(coarse_spec, fine_spec, P(), P(), P(), P()),
        out_specs=(coarse_spec, fine_spec),
        check_vma=False,
    )
```

```python
import jax
import jax.numpy as jnp
from jax import lax
from jax.experimental import pallas as pl
from jax.experimental.pallas import tpu as pltpu
from jax.sharding import PartitionSpec as P

CHIP_OF = (0, 1, 2, 3, 7, 6, 5, 4)
SPECIES = 5
GX = 16
GY = 16
BOXES = 8
CHUNKS = 8
QUADS = 4
ROW_SLOTS = 32
FINE_ROWS = 160
PIECE_ROWS = 184
EDGE_ROWS = 80
EDGE_COARSE = 40
STRIDE = 16
LIST_STRIDE = 40
F32 = jnp.float32
SLOT, COL, HALF, WEST, EAST, SOUTH, NORTH, BOTTOM, TOP, OPEN_Z = range(10)
BESIDE = BOXES * STRIDE
OWN = BESIDE + 2 * GY
TABLE = OWN + 4
SHELL_ROWS = 80
PLANE_ROWS = 104
BACK_ROWS = 128

VMEM = pl.BlockSpec(memory_space=pltpu.VMEM)
SMEM = pl.BlockSpec(memory_space=pltpu.SMEM)
HBM = pl.BlockSpec(memory_space=pltpu.HBM)


def device_of(m, part, row):
    turned = (GY // 2) * (row % 2) if isinstance(row, int) else (GY // 2) * lax.rem(row, 2)
    place = 2 * CHIP_OF[m] + part + turned
    return place % GY if isinstance(row, int) else lax.rem(place, GY)


def chunk():
    turned = (GY // 2) * lax.rem(lax.axis_index("gx"), 2)
    j = lax.rem(lax.axis_index("gy") + turned, GY)
    q = j // 2
    return jnp.where(q < 4, q, 11 - q), lax.rem(j, 2)


def fill_table(corners, sources, table, listed, ranks):
    row = lax.axis_index("gx")
    m, part = chunk()
    groups = (row, lax.rem(row + jnp.where(part > 0, 1, GX - 1), GX))

    def scan(t, counts):
        new_counts = []
        for r in range(2):
            live = corners[0, groups[r] * ROW_SLOTS + t] >= 0
            listed[r * LIST_STRIDE + counts[r]] = t
            ranks[r * ROW_SLOTS + t] = counts[r]
            new_counts.append(counts[r] + jnp.where(live, 1, 0))
        return tuple(new_counts)

    lax.fori_loop(0, ROW_SLOTS, scan, (jnp.int32(0), jnp.int32(0)), unroll=True)

    def rank(r, source):
        found = ranks[r * ROW_SLOTS + lax.rem(jnp.maximum(source, 0), ROW_SLOTS)]
        return jnp.where(source >= 0, found, -1)

    for k in range(2 * GY):
        table[BESIDE + k] = -1
    for k in range(2):
        slot = row * ROW_SLOTS + 2 * lax.axis_index("gy") + k
        table[OWN + 2 * k] = jnp.where(corners[0, slot] >= 0, 1, 0)
        table[OWN + 2 * k + 1] = corners[2, slot] // 128
    face = jnp.where(part > 0, 0, 1)
    for i in range(BOXES):
        t = listed[i]
        slot = groups[0] * ROW_SLOTS + t
        south, north, bottom, top = [sources[f, slot] for f in range(2, 6)]
        beside = rank(1, sources[1 - face, slot])
        half = corners[2, slot] // 128
        base = STRIDE * i
        table[base + SLOT] = t
        table[base + COL] = corners[1, slot] // 16
        table[base + HALF] = half
        table[base + WEST] = jnp.where(part > 0, i, beside)
        table[base + EAST] = jnp.where(part > 0, beside, i)
        table[base + SOUTH] = rank(0, south)
        table[base + NORTH] = rank(0, north)
        table[base + BOTTOM] = jnp.where(m > 0, i, rank(0, bottom))
        table[base + TOP] = jnp.where(m < CHUNKS - 1, i, rank(0, top))
        table[base + OPEN_Z] = jnp.where(jnp.where(half > 0, bottom, top) < 0, 1, 0)
        other = groups[1] * ROW_SLOTS + listed[LIST_STRIDE + i]
        spot = corners[1, other] // 16 * 2 + corners[2, other] // 128
        table[BESIDE + spot] = jnp.where(sources[face, other] < 0, i, -1)


def pack_kernel(
    corners_in, sources_in, coarse_in, fine_in, out, table, coarse, fine, loaded, listed, ranks, corners, sources,
    around,
):
    row, column = lax.axis_index("gx"), lax.axis_index("gy")
    blocks = [(k, s) for k in range(2) for s in range(SPECIES)]
    loads = [pltpu.make_async_copy(fine_in.at[k, s], fine.at[k, s], loaded.at[n]) for n, (k, s) in enumerate(blocks)]
    loads.append(pltpu.make_async_copy(coarse_in, coarse, loaded.at[len(blocks)]))
    integers = (
        pltpu.make_async_copy(corners_in, corners, loaded.at[len(blocks) + 1]),
        pltpu.make_async_copy(sources_in, sources, loaded.at[len(blocks) + 2]),
    )
    for load in (*integers, *loads):
        load.start()
    for load in (*integers, *loads[:SPECIES]):
        load.wait()
    fill_table(corners, sources, table, listed, ranks)
    for n, (k, s) in enumerate(blocks):
        if n == SPECIES:
            for load in loads[SPECIES:]:
                load.wait()
        turned = fine[k, s].reshape(256, 128).T
        at = (k * SPECIES + s) * 16
        for m in range(CHUNKS):
            for part in range(2):
                block = turned[16 * m : 16 * m + 16, 128 * part : 128 * part + 128]
                out[device_of(m, part, row), at : at + 16, :] = block
    for p in range(3):
        at = FINE_ROWS + 8 * p
        for part in range(2):
            blocks = []
            for s in (2 * p, 2 * p + 1):
                block = coarse[min(s, 4), 4 * part : 4 * part + 4].reshape(32, 128)
                blocks += [block, pltpu.roll(block, 64, 1)]
            for n, block in enumerate(blocks):
                around[pl.ds(pl.multiple_of(32 * lax.rem(column + n, 4), 32), 32), :] = block
            turned = around[...].T
            for m in range(CHUNKS):
                out[device_of(m, part, row), at : at + 8, :] = turned[8 * m : 8 * m + 8]


def unpack_kernel(table, received, interior, coarse_out, fine_out, coarse, fine, stored, around, shells, planes):
    row, column = lax.axis_index("gx"), lax.axis_index("gy")
    rows, lanes = iotas()
    stores = []

    def send(source, target):
        stores.append(pltpu.make_async_copy(source, target, stored.at[len(stores)]))
        stores[-1].start()

    live = [table[OWN + 2 * k] > 0 for k in range(2)]
    high = [table[OWN + 2 * k + 1] > 0 for k in range(2)]
    in_plane = [jnp.where(high[k], lanes, 127 - lanes) < 2 for k in range(2)]
    for part in range(2):
        parts = []
        for k in range(2):
            source = jnp.where(high[k], device_of(0, part, row), device_of(CHUNKS - 1, part, row))
            parts.append(received[source, PLANE_ROWS + 10 * k : PLANE_ROWS + 10 * k + 10, :])
        planes[part] = jnp.concatenate([*parts, jnp.zeros((108, 128), F32)]).T
    for s in range(SPECIES):
        for part in range(2):
            pieces = [received[device_of(m, part, row), 16 * s : 16 * s + 16, :] for m in range(CHUNKS)]
            shells[part] = jnp.concatenate(pieces).T
        for k in range(2):
            shift = lax.rem(jnp.where(high[k], 128, 254) - (10 * k + 2 * s), 128)
            for x in range(16):
                part, at_x = x // 8, x % 8
                depth = at_x if part == 0 else 7 - at_x
                if depth < 2:
                    at = 64 * k + 16 * depth
                    tiles = [shells[part, at + 8 * j : at + 8 * j + 8, :] for j in range(2)]
                else:
                    at = 64 * k + 32 + 8 * ((depth - 2) // 2)
                    tile = shells[part, at : at + 8, :]
                    sides = (tile, tile) if depth % 2 == 0 else (turn(tile, -2, 0), turn(tile, 2, 0))
                    tiles = []
                    for j in range(2):
                        at = 16 * at_x + 8 * j
                        plane = pltpu.roll(planes[part, at : at + 8, :], shift, 1)
                        inner = jnp.where(in_plane[k], plane, interior[k, s, x, 8 * j : 8 * j + 8, :])
                        tiles.append(jnp.where(rows >= 6 if j else rows < 2, sides[j], inner))
                for j in range(2):
                    fine[k, s, x, 8 * j : 8 * j + 8, :] = jnp.where(live[k], tiles[j], 0.0)
            send(fine.at[k, s], fine_out.at[k, s])
    left = lax.broadcasted_iota(jnp.int32, (32, 128), 1) < 64
    for p in range(3):
        at = SHELL_ROWS + 8 * p
        pieces = [received[device_of(m, part, row), at : at + 8, :] for part in range(2) for m in range(CHUNKS)]
        around[...] = jnp.concatenate(pieces).T
        for s in range(2 * p, min(2 * p + 2, SPECIES)):
            low, high = [
                around[pl.ds(pl.multiple_of(32 * lax.rem(column + 2 * (s - 2 * p) + h, 4), 32), 32), :] for h in range(2)
            ]
            coarse[s, 0:4] = jnp.where(left, low, pltpu.roll(high, 64, 1)).reshape(4, 8, 128)
            coarse[s, 4:8] = jnp.where(left, pltpu.roll(low, 64, 1), high).reshape(4, 8, 128)
    send(coarse, coarse_out)
    for store in stores:
        store.wait()


def interior_kernel(courant, reaction, fine, out, between):
    rows, lanes = iotas()
    goes_up, size = signs_of(courant)
    weights = weights_of(size, reaction, 0.5)

    def step(load, store, first, last):
        def plane(x, carry):
            values = [[load(s, x, j) for s in range(SPECIES)] for j in range(2)]
            for s in range(SPECIES):
                up_x, up_y, up_z = [goes_up[d][s] for d in range(3)]
                before = x + jnp.where(up_x, -1, 1)
                low, high = [pltpu.roll(values[j][s], jnp.where(up_y, 1, 7), 0) for j in range(2)]
                from_y = (
                    jnp.where((rows == 7) & jnp.logical_not(up_y), high, low),
                    jnp.where((rows == 0) & up_y, low, high),
                )
                for j in range(2):
                    from_z = pltpu.roll(values[j][s], jnp.where(up_z, 1, 127), 1)
                    from_z = jnp.where(lanes == jnp.where(up_z, 0, 127), 0.0, from_z)
                    upwind = (load(s, before, j), from_y[j], from_z)
                    store(s, x, j, moved(values[j], upwind, size, weights, s))
            return carry

        lax.fori_loop(first, last, plane, 0, unroll=True)

    for k in range(2):

        def put(ref):
            def store(s, x, j, tile):
                ref[s, x, 8 * j : 8 * j + 8, :] = tile

            return store

        def get(ref):
            return lambda s, x, j: ref[s, x, 8 * j : 8 * j + 8, :]

        step(get(fine.at[k]), put(between), 1, 15)
        step(get(between), put(out.at[k]), 2, 14)


def iotas():
    return lax.broadcasted_iota(jnp.int32, (8, 128), 0), lax.broadcasted_iota(jnp.int32, (8, 128), 1)


def take(tile, index, axis):
    return jnp.take_along_axis(tile, index, axis=axis, mode="promise_in_bounds")


def turn(tile, shift, axis):
    return pltpu.roll(tile, shift % tile.shape[axis], axis)


def line(ref, index):
    return jnp.broadcast_to(ref[pl.ds(index, 1), :], (8, 128))


def edges(fine, coarse, up_out, down_out, outer_out, inner_out):
    _, lanes = iotas()
    _, part = chunk()
    last = part > 0
    for s in range(SPECIES):
        up_out[8 * s : 8 * s + 8, :] = fine[1][:, s, 7, :]
        down_out[8 * s : 8 * s + 8, :] = fine[0][:, s, 0, :]
        for h in range(2):
            at = EDGE_COARSE + (2 * s + h) * QUADS
            up_out[at : at + QUADS, :] = coarse[:, s, h, 7, :]
            down_out[at : at + QUADS, :] = coarse[:, s, h, 0, :]
        for r in range(2):
            low = high = coarse_low = coarse_high = jnp.zeros((8, 128), F32)
            for i in range(BOXES):
                here = lanes // 16 == i
                low = jnp.where(here, turn(fine[r][i, s], 16 * i, 1), low)
                high = jnp.where(here, turn(fine[r][i, s], 16 * i + 16, 1), high)
            for q in range(QUADS):
                here = lax.rem(lanes // 8, 4) == q
                coarse_low = jnp.where(here, turn(coarse[q, s, r], 8 * q, 1), coarse_low)
                coarse_high = jnp.where(here, turn(coarse[q, s, r], 8 * q - 24, 1), coarse_high)
            outer_out[0, s, r] = jnp.where(last, high, low)
            inner_out[0, s, r] = jnp.where(last, low, high)
            outer_out[1, s, r] = jnp.where(last, coarse_high, coarse_low)
            inner_out[1, s, r] = jnp.where(last, coarse_low, coarse_high)


def compact_kernel(table, received, fine0, fine1, coarse, up_out, down_out, outer_out, inner_out):
    _, lanes = iotas()
    for i in range(BOXES):
        t = table[STRIDE * i + SLOT]
        start = pl.multiple_of(lax.rem(t, 2) * 80, 8)
        box = received[t // 2, pl.ds(start, 80), :].reshape(SPECIES, 2, 8, 128)
        fine0[i] = box[:, 0]
        fine1[i] = box[:, 1]
    for q in range(QUADS):
        for p in range(3):
            at = FINE_ROWS + 8 * p
            tiles = [received[4 * q + o, at : at + 8, :] for o in range(4)]
            for k in range(4 if p < 2 else 2):
                tile = tiles[0]
                for o in range(1, 4):
                    tile = jnp.where(lanes // 32 == (o + k) % 4, tiles[o], tile)
                coarse[q, 2 * p + k // 2, k % 2] = turn(tile, -32 * k, 1)
    edges((fine0, fine1), coarse, up_out, down_out, outer_out, inner_out)


def signs_of(courant):
    goes_up = [[courant[d, s] >= 0.0 for s in range(SPECIES)] for d in range(3)]
    size = [[jnp.abs(courant[d, s]) for s in range(SPECIES)] for d in range(3)]
    return goes_up, size


def weights_of(size, reaction, factor):
    weights = [[factor * reaction[s, e] for e in range(SPECIES)] for s in range(SPECIES)]
    for s in range(SPECIES):
        weights[s][s] = weights[s][s] + (1.0 - size[0][s] - size[1][s] - size[2][s])
    return weights


def moved(values, upwind, size, weights, s):
    total = weights[s][0] * values[0]
    for e in range(1, SPECIES):
        total = total + weights[s][e] * values[e]
    for d in range(3):
        total = total + size[d][s] * upwind[d]
    return total


def ends(table, below, above, ghosts):
    _, lanes = iotas()
    m, _ = chunk()
    ghosts[:EDGE_COARSE, :] = below[:EDGE_COARSE, :]
    ghosts[EDGE_COARSE:, :] = above[:EDGE_COARSE, :]

    def replace(side, source, name, high):
        for i in range(BOXES):
            col, half, found = [table[STRIDE * i + f] for f in (COL, HALF, name)]
            inside = 32 * lax.rem(col, 4) + 8 * (lanes // 32) + lax.rem(lanes, 16) // 2
            for s in range(SPECIES):
                other = take(line(source, EDGE_COARSE + (2 * s + side) * QUADS + col // 4), inside, 1)
                other = jnp.where(half == high, other, 0.0)
                ghost = jnp.where(found >= 0, line(source, 8 * s + jnp.maximum(found, 0)), other)
                at = EDGE_COARSE * side + 8 * s + i
                ghosts[at : at + 1, :] = ghost[:1]

    @pl.when(m == 0)
    def _():
        replace(0, below, BOTTOM, 1)

    @pl.when(m == CHUNKS - 1)
    def _():
        replace(1, above, TOP, 0)


def fine_step(i, table, fine, coarse, ghosts, sides, goes_up, size, weights, write):
    rows, lanes = iotas()
    field = lambda f: table[STRIDE * i + f]
    col, half = field(COL), field(HALF)
    lower_col, upper_col = lax.rem(col + GY - 1, GY), lax.rem(col + 1, GY)
    y = lax.rem(lanes, 16)
    found = [field(f) for f in (WEST, EAST, SOUTH, NORTH)]
    there = [source >= 0 for source in found]
    at = [jnp.maximum(source, 0) for source in found]
    beside = 32 * lax.rem(col, 4) + 8 * (col // 4) + y // 2
    lane_x = [jnp.where(there[f], 16 * at[f] + y, beside) for f in range(2)]
    own_x, line_x = lanes - y, 8 * (lanes // 32)
    lane_y = [
        jnp.where(there[2], own_x + 15, 32 * lax.rem(lower_col, 4) + line_x + 7),
        jnp.where(there[3], own_x, 32 * lax.rem(upper_col, 4) + line_x),
    ]
    row_of = [[jnp.where(is_there, rows, 4 * r + rows // 2) for is_there in there] for r in range(2)]
    kind = [jnp.where(is_there, 0, 1) for is_there in there]
    values = [[fine[r][i, s] for s in range(SPECIES)] for r in range(2)]
    for s in range(SPECIES):
        up_x, up_y, up_z = [goes_up[d][s] for d in range(3)]
        shift_x, edge_x = jnp.where(up_x, 16, 112), lanes // 16 == jnp.where(up_x, 0, 7)
        shift_y, edge_y = jnp.where(up_y, 1, 127), y == jnp.where(up_y, 0, 15)
        shift_z, edge_z = jnp.where(up_z, 1, 7), rows == jnp.where(up_z, 0, 7)
        is_there = jnp.where(up_y, found[2], found[3]) >= 0
        box_y = jnp.where(up_y, at[2], at[3])
        quad_y = jnp.where(up_y, lower_col, upper_col) // 4
        coarse_y = coarse[quad_y, s, half]
        index_x = jnp.where(up_x, lane_x[0], lane_x[1])
        index_y = jnp.where(up_y, lane_y[0], lane_y[1])

        low, high = values[0][s], values[1][s]
        first = pltpu.roll(jnp.where(up_z, low, high), shift_z, 0)
        second = pltpu.roll(jnp.where(up_z, high, low), shift_z, 0)
        second = jnp.where(edge_z, first, second)
        first = jnp.where(edge_z, line(ghosts, jnp.where(up_z, 0, EDGE_COARSE) + 8 * s + i), first)
        from_z = (jnp.where(up_z, first, second), jnp.where(up_z, second, first))

        for r in range(2):
            value = values[r][s]
            west = sides(0, kind[0], s, jnp.where(there[0], r, half))
            east = sides(1, kind[1], s, jnp.where(there[1], r, half))
            ghost = take(jnp.where(up_x, west, east), jnp.where(up_x, row_of[r][0], row_of[r][1]), 0)
            ghost = take(ghost, index_x, 1)
            from_x = jnp.where(edge_x, ghost, pltpu.roll(value, shift_x, 1))
            ghost = take(
                jnp.where(is_there, fine[r][box_y, s], coarse_y), jnp.where(up_y, row_of[r][2], row_of[r][3]), 0
            )
            ghost = take(ghost, index_y, 1)
            from_y = jnp.where(edge_y, ghost, pltpu.roll(value, shift_y, 1))
            write(r, s, moved(values[r], (from_x, from_y, from_z[r]), size, weights, s))


def sides_of(outer, inner):
    _, part = chunk()

    def pick(side, kind, s, at):
        one, other = outer[kind, s, at], inner[kind, s, at]
        return jnp.where(part == side, one, other)

    return pick


def first_kernel(
    table, courant, reaction, fine0, fine1, coarse, below, above, outer, inner,
    new0, new1, middle, provisional, up_out, down_out, outer_out, inner_out, ghosts,
):
    rows, lanes = iotas()
    m, _ = chunk()
    goes_up, size = signs_of(courant)
    weights = weights_of(size, reaction, 1.0)
    x = lax.rem(lanes // 8, 4)
    y = lax.rem(lanes, 8)
    sides = sides_of(outer, inner)
    ends(table, below, above, ghosts)

    def coarse_quad(q, carry):
        before, after = lax.rem(q + QUADS - 1, QUADS), lax.rem(q + 1, QUADS)
        values = [[coarse[q, s, h] for s in range(SPECIES)] for h in range(2)]
        column = 32 * (lanes // 32) + 8 * q + y
        for s in range(SPECIES):
            up_x, up_y, up_z = [goes_up[d][s] for d in range(3)]
            at = [EDGE_COARSE + (2 * s + h) * QUADS + q for h in range(2)]
            lows, highs = [line(below, k) for k in at], [line(above, k) for k in at]
            bottoms = (jnp.where(m > 0, lows[0], 0.0), jnp.where(m > 0, lows[1], lows[0]))
            tops = (
                jnp.where(m < CHUNKS - 1, highs[0], highs[1]),
                jnp.where(m < CHUNKS - 1, highs[1], 0.0),
            )
            for h in range(2):
                value = values[h][s]
                ghost = take(jnp.where(up_x, sides(0, 1, s, h), sides(1, 1, s, h)), column, 1)
                from_x = pltpu.roll(value, jnp.where(up_x, 8, 120), 1)
                from_x = jnp.where(x == jnp.where(up_x, 0, 3), ghost, from_x)

                beside = coarse[jnp.where(up_y, before, after), s, h]
                ghost = jnp.where(lanes // 32 == jnp.where(up_y, 3, 0), beside, value)
                ghost = pltpu.roll(ghost, jnp.where(up_y, 25, 103), 1)
                from_y = pltpu.roll(value, jnp.where(up_y, 1, 127), 1)
                from_y = jnp.where(y == jnp.where(up_y, 0, 7), ghost, from_y)

                ghost = jnp.where(up_z, bottoms[h], tops[h])
                from_z = pltpu.roll(value, jnp.where(up_z, 1, 7), 0)
                from_z = jnp.where(rows == jnp.where(up_z, 0, 7), ghost, from_z)

                result = moved(values[h], (from_x, from_y, from_z), size, weights, s)
                provisional[q, s, h] = result
                middle[q, s, h] = 0.5 * (value + result)
        return carry

    lax.fori_loop(0, QUADS, coarse_quad, 0, unroll=4)
    new = (new0, new1)
    weights = weights_of(size, reaction, 0.5)

    def box(i, carry):
        def write(r, s, result):
            new[r][i, s] = result

        fine_step(i, table, (fine0, fine1), coarse, ghosts, sides, goes_up, size, weights, write)
        return carry

    lax.fori_loop(0, BOXES, box, 0, unroll=8)
    edges(new, middle, up_out, down_out, outer_out, inner_out)


def tools_of(courant, coarse_new, folded0, folded1):
    up = [[jnp.maximum(courant[d, s], 0.0) for s in range(SPECIES)] for d in range(3)]
    down = [[jnp.minimum(courant[d, s], 0.0) for s in range(SPECIES)] for d in range(3)]
    taken = lax.broadcasted_iota(jnp.int32, (128, 128), 0)
    given = lax.broadcasted_iota(jnp.int32, (128, 128), 1)
    given_y, fine_y = lax.rem(given, 8), lax.rem(taken, 16)
    same_x = lax.rem(given // 8, 4) == taken // 32

    def summing(rule):
        return jnp.where(same_x & rule(given_y, fine_y), 1.0, 0.0).astype(F32)

    def product(values, matrix):
        return jnp.dot(values, matrix, precision=lax.Precision.HIGHEST, preferred_element_type=F32)

    def fold(tiles, matrix):
        for refs, folded in zip(tiles, (folded0, folded1)):
            pairs = sum(
                ref.reshape(BOXES * SPECIES * 8, 128)[pl.ds(odd, BOXES * SPECIES * 4, stride=2), :]
                for ref in refs
                for odd in range(2)
            )
            folded[...] = product(pairs, matrix)

    def folded_tile(i, s):
        at = pl.ds((i * SPECIES + s) * 4, 4)
        return jnp.concatenate([folded0[at, :], folded1[at, :]])

    def add(q, s, h, where, change):
        coarse_new[q, s, h] = coarse_new[q, s, h] + jnp.where(where, change, 0.0)

    def change_of(here, across, both, beside, rate_out, rate_in, sign):
        return sign * (rate_out * (here - 0.5 * both) + rate_in * (across - 0.125 * beside))

    return up, down, summing, product, fold, folded_tile, add, change_of


def beside_kernel(table, courant, old0, old1, coarse, fine0, fine1, middle, provisional, coarse_new, folded0, folded1):
    _, lanes = iotas()
    y = lax.rem(lanes, 8)
    group = lanes // 32
    up, down, summing, _, fold, folded_tile, add, change_of = tools_of(courant, coarse_new, folded0, folded1)
    coarse_new[...] = provisional[...]

    def rule(given_y, fine_y):
        return ((fine_y == 0) & (given_y == 7)) | ((fine_y == 15) & (given_y == 0))

    fold(((old0, fine0), (old1, fine1)), summing(rule))

    def open_y(i, carry):
        col, half, south, north = [table[STRIDE * i + f] for f in (COL, HALF, SOUTH, NORTH)]
        south_col, north_col = lax.rem(col + GY - 1, GY), lax.rem(col + 1, GY)
        south_quad, north_quad = south_col // 4, north_col // 4
        at_south = (group == lax.rem(south_col, 4)) & (y == 7) & (south < 0)
        at_north = (group == lax.rem(north_col, 4)) & (y == 0) & (north < 0)
        for s in range(SPECIES):
            beside = folded_tile(i, s)
            tile = coarse[col // 4, s, half]
            here = coarse[south_quad, s, half]
            both = here + middle[south_quad, s, half]
            change = change_of(here, turn(tile, -25, 1), both, beside, up[1][s], down[1][s], 1.0)
            add(south_quad, s, half, at_south, change)
            here = coarse[north_quad, s, half]
            both = here + middle[north_quad, s, half]
            change = change_of(here, turn(tile, 25, 1), both, beside, down[1][s], up[1][s], -1.0)
            add(north_quad, s, half, at_north, change)
        return carry

    lax.fori_loop(0, BOXES, open_y, 0, unroll=8)


def second_kernel(
    table, courant, reaction, old0, old1, coarse, old_below, old_above, old_outer, old_inner,
    fine0, fine1, middle, below, above, outer, inner, corrected, out,
    coarse_new, ghosts, result0, result1, folded0, folded1,
):
    rows, lanes = iotas()
    m, part = chunk()
    goes_up, size = signs_of(courant)
    weights = weights_of(size, reaction, 0.5)
    up, down, summing, product, fold, folded_tile, add, change_of = tools_of(courant, coarse_new, folded0, folded1)
    x = lax.rem(lanes // 8, 4)
    y = lax.rem(lanes, 8)
    group = lanes // 32
    ends(table, below, above, ghosts)
    coarse_new[...] = corrected[...]

    sides = sides_of(outer, inner)

    def box_step(i, carry):
        def write(r, s, result):
            (result0, result1)[r][i, s] = result

        fine_step(i, table, (fine0, fine1), middle, ghosts, sides, goes_up, size, weights, write)
        return carry

    lax.fori_loop(0, BOXES, box_step, 0, unroll=8)

    place = lax.rem(lanes, 64)
    rest = jnp.maximum(place - 32, 0)
    slot = lax.rem(rest, 8)
    is_second = (slot >= 2) & (slot < 6)
    depth = jnp.where(place < 32, place // 16, 2 + 2 * (rest // 8) + jnp.where(is_second, 1, 0))
    depth = jnp.minimum(depth, 7)
    rest_y = jnp.where(is_second, slot - 2, slot)
    rest_y = jnp.where(slot >= 4, jnp.where(is_second, slot + 10, slot + 8), rest_y)
    shell_y = jnp.where(place < 32, lax.rem(place, 16), rest_y)
    shell_index = 16 * jnp.where(part > 0, 7 - depth, depth) + shell_y

    def pack_box(i, carry):
        t = table[STRIDE * i + SLOT]
        k = lax.rem(t, 2)
        mine = lanes // 64 == k
        for s in range(SPECIES):
            for r, result in enumerate((result0, result1)):
                at = (2 * s + r) * 8
                packed = take(result[i, s], shell_index, 1)
                out[t // 2, at : at + 8, :] = jnp.where(mine, packed, out[t // 2, at : at + 8, :])
            plane = jnp.where(m == 0, result0[i, s, 0:2, :], result1[i, s, 6:8, :])
            out[t // 2, pl.ds(PLANE_ROWS + 10 * k + 2 * s, 2), :] = plane
        return carry

    lax.fori_loop(0, BOXES, pack_box, 0, unroll=4)
    mean_matrix = summing(lambda given_y, fine_y: fine_y // 2 == given_y)

    def open_z(high, row, source, old_source, rate_out, rate_in, sign):
        folded0[:EDGE_COARSE, :] = product(source[:EDGE_COARSE, :] + old_source[:EDGE_COARSE, :], mean_matrix)
        for i in range(BOXES):
            col, half, is_open = [table[STRIDE * i + f] for f in (COL, HALF, OPEN_Z)]
            q = col // 4
            where = (rows == row) & (group == lax.rem(col, 4)) & (half == high) & (is_open > 0)
            for s in range(SPECIES):
                beside = jnp.broadcast_to(folded0[8 * s + i : 8 * s + i + 1, :], (8, 128))
                here = coarse[q, s, 1 - high]
                across = line(old_source, EDGE_COARSE + (2 * s + high) * QUADS + q)
                both = here + middle[q, s, 1 - high]
                change = change_of(here, across, both, beside, rate_out[s], rate_in[s], sign)
                add(q, s, 1 - high, where, change)

    @pl.when(m == CHUNKS - 1)
    def _():
        open_z(1, 7, above, old_above, up[2], down[2], 1.0)

    @pl.when(m == 0)
    def _():
        open_z(0, 0, below, old_below, down[2], up[2], -1.0)

    row_index = 2 * lax.rem(rows, 4)
    last = part > 0
    edge = jnp.where(last, 3, 0)
    sign = jnp.where(last, 1.0, -1.0)
    sums = []
    for s in range(SPECIES):
        totals = [old_outer[0, s, r] + outer[0, s, r] for r in range(2)]
        totals = [take(total + turn(total, -1, 0), row_index, 0) for total in totals]
        total = jnp.where(rows < 4, totals[0], totals[1])
        sums.append(total + turn(total, -1, 1))

    def open_x(q, carry):
        column = 32 * group + 8 * q + y
        for h in range(2):
            box = table[BESIDE + 2 * (4 * q) + h]
            for o in range(1, 4):
                box = jnp.where(group == o, table[BESIDE + 2 * (4 * q + o) + h], box)
            where = (box >= 0) & (x == edge)
            index = 16 * jnp.maximum(box, 0) + 2 * y
            for s in range(SPECIES):
                rate_out = jnp.where(last, up[0][s], down[0][s])
                rate_in = jnp.where(last, down[0][s], up[0][s])
                here = coarse[q, s, h]
                across = take(old_outer[1, s, h], column, 1)
                both = here + middle[q, s, h]
                beside = take(sums[s], index, 1)
                add(q, s, h, where, change_of(here, across, both, beside, rate_out, rate_in, sign))
        return carry

    lax.fori_loop(0, QUADS, open_x, 0, unroll=4)
    fold(((result0,), (result1,)), mean_matrix)

    def cover(i, carry):
        col, half = [table[STRIDE * i + f] for f in (COL, HALF)]
        q = col // 4
        where = group == lax.rem(col, 4)
        for s in range(SPECIES):
            coarse_new[q, s, half] = jnp.where(where, 0.125 * folded_tile(i, s), coarse_new[q, s, half])
        return carry

    lax.fori_loop(0, BOXES, cover, 0, unroll=8)
    for q in range(QUADS):
        for p in range(3):
            at = SHELL_ROWS + 8 * p
            tiles = [turn(coarse_new[q, 2 * p + k // 2, k % 2], 32 * k, 1) for k in range(4 if p < 2 else 2)]
            for o in range(4):
                tile = tiles[0]
                for k in range(1, len(tiles)):
                    tile = jnp.where(group == (o + k) % 4, tiles[k], tile)
                out[4 * q + o, at : at + 8, :] = tile


def call(kernel, out_shape, operands, smem, scratch=(), in_spec=VMEM, out_spec=VMEM):
    many = isinstance(out_shape, (list, tuple))
    specs = [out_spec] * len(out_shape) if many and not isinstance(out_spec, list) else out_spec
    return pl.pallas_call(
        kernel,
        out_shape=out_shape,
        in_specs=[SMEM] * smem + [in_spec] * (len(operands) - smem),
        out_specs=specs,
        scratch_shapes=list(scratch),
        compiler_params=pltpu.CompilerParams(vmem_limit_bytes=40 * 1024 * 1024),
    )(*operands)


def exchange(up_edge, down_edge, outer_edge, inner_edge):
    device = lambda g, m, part: g % GX * GY + device_of(m % CHUNKS, part, g % GX)
    all_of = [(g, m, part) for g in range(GX) for m in range(CHUNKS) for part in range(2)]
    axes = ("gx", "gy")
    send = lambda value, target: lax.ppermute(value, axes, [(device(*d), device(*target(*d))) for d in all_of])
    outer = send(outer_edge, lambda g, m, part: (g + 2 * part - 1, m, 1 - part))
    below = send(up_edge, lambda g, m, part: (g, m + 1, part))
    above = send(down_edge, lambda g, m, part: (g, m - 1, part))
    inner = send(inner_edge, lambda g, m, part: (g, m, 1 - part))
    return below, above, outer, inner


def spread(pieces):
    return lax.all_to_all(pieces, "gy", 0, 0, tiled=True)


def shards(coarse, fine, corners, ghost_source, courant, reaction):
    shape = lambda *dims: jax.ShapeDtypeStruct(dims, F32)
    pieces = shape(GY, PIECE_ROWS, 128)
    boxes = shape(BOXES, SPECIES, 8, 128)
    grid = shape(QUADS, SPECIES, 2, 8, 128)
    sent = (shape(EDGE_ROWS, 128),) * 2 + (shape(2, SPECIES, 2, 8, 128),) * 2
    whole = (pltpu.VMEM(coarse.shape, F32), pltpu.VMEM(fine.shape, F32))
    copies = pltpu.SemaphoreType.DMA((2 * SPECIES + 1,))
    integers = lambda *dims: pltpu.SMEM(dims, jnp.int32)
    placed = [pltpu.with_memory_space_constraint(value, pltpu.HBM) for value in (corners.T, ghost_source.T, coarse, fine)]
    sending, table = call(
        pack_kernel,
        [pltpu.VMEM(pieces.shape, F32), jax.ShapeDtypeStruct((TABLE,), jnp.int32)],
        placed,
        0,
        (
            *whole,
            pltpu.SemaphoreType.DMA((2 * SPECIES + 3,)),
            integers(2 * LIST_STRIDE),
            integers(2 * ROW_SLOTS),
            integers(3, 512),
            integers(6, 512),
            pltpu.VMEM((128, 128), F32),
        ),
        HBM,
        [VMEM, SMEM],
    )
    received = spread(sending)
    fine0, fine1, middle, *sending = call(compact_kernel, (boxes, boxes, grid) + sent, (table, received), 1)
    old = (fine0, fine1, middle, *exchange(*sending))
    between = (pltpu.VMEM(fine.shape[1:], F32),)
    held, _ = lax.optimization_barrier((fine, old[0]))
    interior = call(interior_kernel, shape(*fine.shape), (courant, reaction, held), 2, between)
    interior, *old = lax.optimization_barrier((interior, *old))
    old = tuple(old)
    ghosts = pltpu.VMEM((EDGE_ROWS, 128), F32)
    new0, new1, middle, provisional, *sending = call(
        first_kernel, (boxes, boxes, grid, grid) + sent, (table, courant, reaction) + old, 3, (ghosts,)
    )
    new = (new0, new1, middle, *exchange(*sending))
    folded = (pltpu.VMEM((BOXES * SPECIES * 4, 128), F32),) * 2
    operands = (table, courant) + old[:3] + new[:3] + (provisional,)
    corrected = call(beside_kernel, grid, operands, 2, folded)
    scratch = (
        pltpu.VMEM(grid.shape, F32),
        ghosts,
        pltpu.VMEM(boxes.shape, F32),
        pltpu.VMEM(boxes.shape, F32),
        *folded,
    )
    back = call(
        second_kernel, shape(GY, BACK_ROWS, 128), (table, courant, reaction) + old + new + (corrected,), 3, scratch
    )
    outputs = (shape(*coarse.shape), shape(*fine.shape))
    scratch = (
        *whole,
        copies,
        pltpu.VMEM((128, 128), F32),
        pltpu.VMEM((2, 128, 128), F32),
        pltpu.VMEM((2, 128, 128), F32),
    )
    return call(unpack_kernel, outputs, (table, spread(back), interior), 1, scratch, VMEM, HBM)


def solution(mesh):
    fine_spec = P(("gx", "gy"), None, None, None, None)
    coarse_spec = P(None, "gx", "gy", None)
    return jax.shard_map(
        shards,
        mesh=mesh,
        in_specs=(coarse_spec, fine_spec, P(), P(), P(), P()),
        out_specs=(coarse_spec, fine_spec),
        check_vma=False,
    )
```

```python
import jax
import jax.numpy as jnp
from jax import lax
from jax.experimental import pallas as pl
from jax.experimental.pallas import tpu as pltpu
from jax.sharding import PartitionSpec as P

CHIP_OF = (0, 1, 2, 3, 7, 6, 5, 4)
SPECIES = 5
GX = 16
GY = 16
BOXES = 8
CHUNKS = 8
QUADS = 4
ROW_SLOTS = 32
FINE_ROWS = 160
PIECE_ROWS = 184
EDGE_ROWS = 80
EDGE_COARSE = 40
STRIDE = 16
LIST_STRIDE = 40
F32 = jnp.float32
SLOT, COL, HALF, WEST, EAST, SOUTH, NORTH, BOTTOM, TOP, OPEN_Z = range(10)
BESIDE = BOXES * STRIDE
OWN = BESIDE + 2 * GY
TABLE = OWN + 4
SHELL_ROWS = 80
PLANE_ROWS = 104
BACK_ROWS = 120

VMEM = pl.BlockSpec(memory_space=pltpu.VMEM)
SMEM = pl.BlockSpec(memory_space=pltpu.SMEM)
HBM = pl.BlockSpec(memory_space=pltpu.HBM)


def device_of(m, part, row):
    turned = (GY // 2) * (row % 2) if isinstance(row, int) else (GY // 2) * lax.rem(row, 2)
    place = 2 * CHIP_OF[m] + part + turned
    return place % GY if isinstance(row, int) else lax.rem(place, GY)


def chunk():
    turned = (GY // 2) * lax.rem(lax.axis_index("gx"), 2)
    j = lax.rem(lax.axis_index("gy") + turned, GY)
    q = j // 2
    return jnp.where(q < 4, q, 11 - q), lax.rem(j, 2)


def fill_table(corners, sources, table, listed, ranks):
    row = lax.axis_index("gx")
    m, part = chunk()
    groups = (row, lax.rem(row + jnp.where(part > 0, 1, GX - 1), GX))

    def scan(t, counts):
        new_counts = []
        for r in range(2):
            live = corners[0, groups[r] * ROW_SLOTS + t] >= 0
            listed[r * LIST_STRIDE + counts[r]] = t
            ranks[r * ROW_SLOTS + t] = counts[r]
            new_counts.append(counts[r] + jnp.where(live, 1, 0))
        return tuple(new_counts)

    lax.fori_loop(0, ROW_SLOTS, scan, (jnp.int32(0), jnp.int32(0)), unroll=True)

    def rank(r, source):
        found = ranks[r * ROW_SLOTS + lax.rem(jnp.maximum(source, 0), ROW_SLOTS)]
        return jnp.where(source >= 0, found, -1)

    for k in range(2 * GY):
        table[BESIDE + k] = -1
    for k in range(2):
        slot = row * ROW_SLOTS + 2 * lax.axis_index("gy") + k
        table[OWN + 2 * k] = jnp.where(corners[0, slot] >= 0, 1, 0)
        table[OWN + 2 * k + 1] = corners[2, slot] // 128
    face = jnp.where(part > 0, 0, 1)
    for i in range(BOXES):
        t = listed[i]
        slot = groups[0] * ROW_SLOTS + t
        south, north, bottom, top = [sources[f, slot] for f in range(2, 6)]
        beside = rank(1, sources[1 - face, slot])
        half = corners[2, slot] // 128
        base = STRIDE * i
        table[base + SLOT] = t
        table[base + COL] = corners[1, slot] // 16
        table[base + HALF] = half
        table[base + WEST] = jnp.where(part > 0, i, beside)
        table[base + EAST] = jnp.where(part > 0, beside, i)
        table[base + SOUTH] = rank(0, south)
        table[base + NORTH] = rank(0, north)
        table[base + BOTTOM] = jnp.where(m > 0, i, rank(0, bottom))
        table[base + TOP] = jnp.where(m < CHUNKS - 1, i, rank(0, top))
        table[base + OPEN_Z] = jnp.where(jnp.where(half > 0, bottom, top) < 0, 1, 0)
        other = groups[1] * ROW_SLOTS + listed[LIST_STRIDE + i]
        spot = corners[1, other] // 16 * 2 + corners[2, other] // 128
        table[BESIDE + spot] = jnp.where(sources[face, other] < 0, i, -1)


def pack_kernel(
    corners_in, sources_in, coarse_in, fine_in, out, table, coarse, fine, loaded, listed, ranks, corners, sources,
    around,
):
    row, column = lax.axis_index("gx"), lax.axis_index("gy")
    blocks = [(k, s) for k in range(2) for s in range(SPECIES)]
    loads = [pltpu.make_async_copy(fine_in.at[k, s], fine.at[k, s], loaded.at[n]) for n, (k, s) in enumerate(blocks)]
    loads.append(pltpu.make_async_copy(coarse_in, coarse, loaded.at[len(blocks)]))
    integers = (
        pltpu.make_async_copy(corners_in, corners, loaded.at[len(blocks) + 1]),
        pltpu.make_async_copy(sources_in, sources, loaded.at[len(blocks) + 2]),
    )
    for load in (*integers, *loads):
        load.start()
    for load in (*integers, *loads[:SPECIES]):
        load.wait()
    fill_table(corners, sources, table, listed, ranks)
    for n, (k, s) in enumerate(blocks):
        if n == SPECIES:
            for load in loads[SPECIES:]:
                load.wait()
        turned = fine[k, s].reshape(256, 128).T
        at = (k * SPECIES + s) * 16
        for m in range(CHUNKS):
            for part in range(2):
                block = turned[16 * m : 16 * m + 16, 128 * part : 128 * part + 128]
                out[device_of(m, part, row), at : at + 16, :] = block
    for p in range(3):
        at = FINE_ROWS + 8 * p
        for part in range(2):
            blocks = []
            for s in (2 * p, 2 * p + 1):
                block = coarse[min(s, 4), 4 * part : 4 * part + 4].reshape(32, 128)
                blocks += [block, pltpu.roll(block, 64, 1)]
            for n, block in enumerate(blocks):
                around[pl.ds(pl.multiple_of(32 * lax.rem(column + n, 4), 32), 32), :] = block
            turned = around[...].T
            for m in range(CHUNKS):
                out[device_of(m, part, row), at : at + 8, :] = turned[8 * m : 8 * m + 8]


def unpack_kernel(table, received, interior, coarse_out, fine_out, coarse, fine, stored, around, shells, planes):
    row, column = lax.axis_index("gx"), lax.axis_index("gy")
    rows, lanes = iotas()
    stores = []

    def send(source, target):
        stores.append(pltpu.make_async_copy(source, target, stored.at[len(stores)]))
        stores[-1].start()

    live = [table[OWN + 2 * k] > 0 for k in range(2)]
    high = [table[OWN + 2 * k + 1] > 0 for k in range(2)]
    in_plane = [jnp.where(high[k], lanes, 127 - lanes) < 2 for k in range(2)]
    turned = lax.rem(column, 4)
    for part in range(2):
        parts, last = [], []
        for k in range(2):
            source = jnp.where(high[k], device_of(0, part, row), device_of(CHUNKS - 1, part, row))
            parts.append(received[source, PLANE_ROWS + 8 * k : PLANE_ROWS + 8 * k + 8, :])
            tile = received[source, PLANE_ROWS - 8 : PLANE_ROWS, :]
            low = pltpu.roll(tile, lax.rem(192 - 32 * turned, 128), 1)
            rest = pltpu.roll(turn(tile, -2, 0), lax.rem(128 - 32 * turned, 128), 1)
            last.append(jnp.where(lanes < 64, low, rest))
        parts.append(jnp.where(rows < 4, last[0], last[1]))
        planes[part] = jnp.concatenate([*parts, jnp.zeros((104, 128), F32)]).T
    for s in range(SPECIES):
        for part in range(2):
            pieces = [received[device_of(m, part, row), 16 * s : 16 * s + 16, :] for m in range(CHUNKS)]
            shells[part] = jnp.concatenate(pieces).T
        for k in range(2):
            first = 8 * k + 2 * s if s < SPECIES - 1 else 16 + 4 * k
            shift = lax.rem(jnp.where(high[k], 128, 254) - first, 128)
            for x in range(16):
                part, at_x = x // 8, x % 8
                depth = at_x if part == 0 else 7 - at_x
                if depth < 2:
                    at = 64 * k + 16 * depth
                    tiles = [shells[part, at + 8 * j : at + 8 * j + 8, :] for j in range(2)]
                else:
                    at = 64 * k + 32 + 8 * ((depth - 2) // 2)
                    tile = shells[part, at : at + 8, :]
                    sides = (tile, tile) if depth % 2 == 0 else (turn(tile, -2, 0), turn(tile, 2, 0))
                    tiles = []
                    for j in range(2):
                        at = 16 * at_x + 8 * j
                        plane = pltpu.roll(planes[part, at : at + 8, :], shift, 1)
                        inner = jnp.where(in_plane[k], plane, interior[k, s, x, 8 * j : 8 * j + 8, :])
                        tiles.append(jnp.where(rows >= 6 if j else rows < 2, sides[j], inner))
                for j in range(2):
                    fine[k, s, x, 8 * j : 8 * j + 8, :] = jnp.where(live[k], tiles[j], 0.0)
            send(fine.at[k, s], fine_out.at[k, s])
    left = lax.broadcasted_iota(jnp.int32, (32, 128), 1) < 64
    for p in range(3):
        at = SHELL_ROWS + 8 * p
        pieces = [received[device_of(m, part, row), at : at + 8, :] for part in range(2) for m in range(CHUNKS)]
        around[...] = jnp.concatenate(pieces).T
        for s in range(2 * p, min(2 * p + 2, SPECIES)):
            low, high = [
                around[pl.ds(pl.multiple_of(32 * lax.rem(column + 2 * (s - 2 * p) + h, 4), 32), 32), :] for h in range(2)
            ]
            coarse[s, 0:4] = jnp.where(left, low, pltpu.roll(high, 64, 1)).reshape(4, 8, 128)
            coarse[s, 4:8] = jnp.where(left, pltpu.roll(low, 64, 1), high).reshape(4, 8, 128)
    send(coarse, coarse_out)
    for store in stores:
        store.wait()


def interior_kernel(courant, reaction, fine, out, between):
    rows, lanes = iotas()
    goes_up, size = signs_of(courant)
    weights = weights_of(size, reaction, 0.5)

    def step(load, store, first, last):
        def plane(x, carry):
            values = [[load(s, x, j) for s in range(SPECIES)] for j in range(2)]
            for s in range(SPECIES):
                up_x, up_y, up_z = [goes_up[d][s] for d in range(3)]
                before = x + jnp.where(up_x, -1, 1)
                low, high = [pltpu.roll(values[j][s], jnp.where(up_y, 1, 7), 0) for j in range(2)]
                from_y = (
                    jnp.where((rows == 7) & jnp.logical_not(up_y), high, low),
                    jnp.where((rows == 0) & up_y, low, high),
                )
                for j in range(2):
                    from_z = pltpu.roll(values[j][s], jnp.where(up_z, 1, 127), 1)
                    from_z = jnp.where(lanes == jnp.where(up_z, 0, 127), 0.0, from_z)
                    upwind = (load(s, before, j), from_y[j], from_z)
                    store(s, x, j, moved(values[j], upwind, size, weights, s))
            return carry

        lax.fori_loop(first, last, plane, 0, unroll=True)

    for k in range(2):

        def put(ref):
            def store(s, x, j, tile):
                ref[s, x, 8 * j : 8 * j + 8, :] = tile

            return store

        def get(ref):
            return lambda s, x, j: ref[s, x, 8 * j : 8 * j + 8, :]

        step(get(fine.at[k]), put(between), 1, 15)
        step(get(between), put(out.at[k]), 2, 14)


def iotas():
    return lax.broadcasted_iota(jnp.int32, (8, 128), 0), lax.broadcasted_iota(jnp.int32, (8, 128), 1)


def take(tile, index, axis):
    return jnp.take_along_axis(tile, index, axis=axis, mode="promise_in_bounds")


def turn(tile, shift, axis):
    return pltpu.roll(tile, shift % tile.shape[axis], axis)


def line(ref, index):
    return jnp.broadcast_to(ref[pl.ds(index, 1), :], (8, 128))


def edges(fine, coarse, up_out, down_out, outer_out, inner_out):
    _, lanes = iotas()
    _, part = chunk()
    last = part > 0
    for s in range(SPECIES):
        up_out[8 * s : 8 * s + 8, :] = fine[1][:, s, 7, :]
        down_out[8 * s : 8 * s + 8, :] = fine[0][:, s, 0, :]
        for h in range(2):
            at = EDGE_COARSE + (2 * s + h) * QUADS
            up_out[at : at + QUADS, :] = coarse[:, s, h, 7, :]
            down_out[at : at + QUADS, :] = coarse[:, s, h, 0, :]
        for r in range(2):
            low = high = coarse_low = coarse_high = jnp.zeros((8, 128), F32)
            for i in range(BOXES):
                here = lanes // 16 == i
                low = jnp.where(here, turn(fine[r][i, s], 16 * i, 1), low)
                high = jnp.where(here, turn(fine[r][i, s], 16 * i + 16, 1), high)
            for q in range(QUADS):
                here = lax.rem(lanes // 8, 4) == q
                coarse_low = jnp.where(here, turn(coarse[q, s, r], 8 * q, 1), coarse_low)
                coarse_high = jnp.where(here, turn(coarse[q, s, r], 8 * q - 24, 1), coarse_high)
            outer_out[0, s, r] = jnp.where(last, high, low)
            inner_out[0, s, r] = jnp.where(last, low, high)
            outer_out[1, s, r] = jnp.where(last, coarse_high, coarse_low)
            inner_out[1, s, r] = jnp.where(last, coarse_low, coarse_high)


def compact_kernel(table, received, fine0, fine1, coarse, up_out, down_out, outer_out, inner_out):
    _, lanes = iotas()
    for i in range(BOXES):
        t = table[STRIDE * i + SLOT]
        start = pl.multiple_of(lax.rem(t, 2) * 80, 8)
        box = received[t // 2, pl.ds(start, 80), :].reshape(SPECIES, 2, 8, 128)
        fine0[i] = box[:, 0]
        fine1[i] = box[:, 1]
    for q in range(QUADS):
        for p in range(3):
            at = FINE_ROWS + 8 * p
            tiles = [received[4 * q + o, at : at + 8, :] for o in range(4)]
            for k in range(4 if p < 2 else 2):
                tile = tiles[0]
                for o in range(1, 4):
                    tile = jnp.where(lanes // 32 == (o + k) % 4, tiles[o], tile)
                coarse[q, 2 * p + k // 2, k % 2] = turn(tile, -32 * k, 1)
    edges((fine0, fine1), coarse, up_out, down_out, outer_out, inner_out)


def signs_of(courant):
    goes_up = [[courant[d, s] >= 0.0 for s in range(SPECIES)] for d in range(3)]
    size = [[jnp.abs(courant[d, s]) for s in range(SPECIES)] for d in range(3)]
    return goes_up, size


def weights_of(size, reaction, factor):
    weights = [[factor * reaction[s, e] for e in range(SPECIES)] for s in range(SPECIES)]
    for s in range(SPECIES):
        weights[s][s] = weights[s][s] + (1.0 - size[0][s] - size[1][s] - size[2][s])
    return weights


def moved(values, upwind, size, weights, s):
    total = weights[s][0] * values[0]
    for e in range(1, SPECIES):
        total = total + weights[s][e] * values[e]
    for d in range(3):
        total = total + size[d][s] * upwind[d]
    return total


def ends(table, below, above, ghosts):
    _, lanes = iotas()
    m, _ = chunk()
    ghosts[:EDGE_COARSE, :] = below[:EDGE_COARSE, :]
    ghosts[EDGE_COARSE:, :] = above[:EDGE_COARSE, :]

    def replace(side, source, name, high):
        for i in range(BOXES):
            col, half, found = [table[STRIDE * i + f] for f in (COL, HALF, name)]
            inside = 32 * lax.rem(col, 4) + 8 * (lanes // 32) + lax.rem(lanes, 16) // 2
            for s in range(SPECIES):
                other = take(line(source, EDGE_COARSE + (2 * s + side) * QUADS + col // 4), inside, 1)
                other = jnp.where(half == high, other, 0.0)
                ghost = jnp.where(found >= 0, line(source, 8 * s + jnp.maximum(found, 0)), other)
                at = EDGE_COARSE * side + 8 * s + i
                ghosts[at : at + 1, :] = ghost[:1]

    @pl.when(m == 0)
    def _():
        replace(0, below, BOTTOM, 1)

    @pl.when(m == CHUNKS - 1)
    def _():
        replace(1, above, TOP, 0)


def fine_step(i, table, fine, coarse, ghosts, sides, goes_up, size, weights, write):
    rows, lanes = iotas()
    field = lambda f: table[STRIDE * i + f]
    col, half = field(COL), field(HALF)
    lower_col, upper_col = lax.rem(col + GY - 1, GY), lax.rem(col + 1, GY)
    y = lax.rem(lanes, 16)
    found = [field(f) for f in (WEST, EAST, SOUTH, NORTH)]
    there = [source >= 0 for source in found]
    at = [jnp.maximum(source, 0) for source in found]
    beside = 32 * lax.rem(col, 4) + 8 * (col // 4) + y // 2
    lane_x = [jnp.where(there[f], 16 * at[f] + y, beside) for f in range(2)]
    own_x, line_x = lanes - y, 8 * (lanes // 32)
    lane_y = [
        jnp.where(there[2], own_x + 15, 32 * lax.rem(lower_col, 4) + line_x + 7),
        jnp.where(there[3], own_x, 32 * lax.rem(upper_col, 4) + line_x),
    ]
    row_of = [[jnp.where(is_there, rows, 4 * r + rows // 2) for is_there in there] for r in range(2)]
    kind = [jnp.where(is_there, 0, 1) for is_there in there]
    values = [[fine[r][i, s] for s in range(SPECIES)] for r in range(2)]
    for s in range(SPECIES):
        up_x, up_y, up_z = [goes_up[d][s] for d in range(3)]
        shift_x, edge_x = jnp.where(up_x, 16, 112), lanes // 16 == jnp.where(up_x, 0, 7)
        shift_y, edge_y = jnp.where(up_y, 1, 127), y == jnp.where(up_y, 0, 15)
        shift_z, edge_z = jnp.where(up_z, 1, 7), rows == jnp.where(up_z, 0, 7)
        is_there = jnp.where(up_y, found[2], found[3]) >= 0
        box_y = jnp.where(up_y, at[2], at[3])
        quad_y = jnp.where(up_y, lower_col, upper_col) // 4
        coarse_y = coarse[quad_y, s, half]
        index_x = jnp.where(up_x, lane_x[0], lane_x[1])
        index_y = jnp.where(up_y, lane_y[0], lane_y[1])

        low, high = values[0][s], values[1][s]
        first = pltpu.roll(jnp.where(up_z, low, high), shift_z, 0)
        second = pltpu.roll(jnp.where(up_z, high, low), shift_z, 0)
        second = jnp.where(edge_z, first, second)
        first = jnp.where(edge_z, line(ghosts, jnp.where(up_z, 0, EDGE_COARSE) + 8 * s + i), first)
        from_z = (jnp.where(up_z, first, second), jnp.where(up_z, second, first))

        for r in range(2):
            value = values[r][s]
            west = sides(0, kind[0], s, jnp.where(there[0], r, half))
            east = sides(1, kind[1], s, jnp.where(there[1], r, half))
            ghost = take(jnp.where(up_x, west, east), jnp.where(up_x, row_of[r][0], row_of[r][1]), 0)
            ghost = take(ghost, index_x, 1)
            from_x = jnp.where(edge_x, ghost, pltpu.roll(value, shift_x, 1))
            ghost = take(
                jnp.where(is_there, fine[r][box_y, s], coarse_y), jnp.where(up_y, row_of[r][2], row_of[r][3]), 0
            )
            ghost = take(ghost, index_y, 1)
            from_y = jnp.where(edge_y, ghost, pltpu.roll(value, shift_y, 1))
            write(r, s, moved(values[r], (from_x, from_y, from_z[r]), size, weights, s))


def sides_of(outer, inner):
    _, part = chunk()

    def pick(side, kind, s, at):
        one, other = outer[kind, s, at], inner[kind, s, at]
        return jnp.where(part == side, one, other)

    return pick


def first_kernel(
    table, courant, reaction, fine0, fine1, coarse, below, above, outer, inner,
    new0, new1, middle, provisional, up_out, down_out, outer_out, inner_out, ghosts,
):
    rows, lanes = iotas()
    m, _ = chunk()
    goes_up, size = signs_of(courant)
    weights = weights_of(size, reaction, 1.0)
    x = lax.rem(lanes // 8, 4)
    y = lax.rem(lanes, 8)
    sides = sides_of(outer, inner)
    ends(table, below, above, ghosts)

    def coarse_quad(q, carry):
        before, after = lax.rem(q + QUADS - 1, QUADS), lax.rem(q + 1, QUADS)
        values = [[coarse[q, s, h] for s in range(SPECIES)] for h in range(2)]
        column = 32 * (lanes // 32) + 8 * q + y
        for s in range(SPECIES):
            up_x, up_y, up_z = [goes_up[d][s] for d in range(3)]
            at = [EDGE_COARSE + (2 * s + h) * QUADS + q for h in range(2)]
            lows, highs = [line(below, k) for k in at], [line(above, k) for k in at]
            bottoms = (jnp.where(m > 0, lows[0], 0.0), jnp.where(m > 0, lows[1], lows[0]))
            tops = (
                jnp.where(m < CHUNKS - 1, highs[0], highs[1]),
                jnp.where(m < CHUNKS - 1, highs[1], 0.0),
            )
            for h in range(2):
                value = values[h][s]
                ghost = take(jnp.where(up_x, sides(0, 1, s, h), sides(1, 1, s, h)), column, 1)
                from_x = pltpu.roll(value, jnp.where(up_x, 8, 120), 1)
                from_x = jnp.where(x == jnp.where(up_x, 0, 3), ghost, from_x)

                beside = coarse[jnp.where(up_y, before, after), s, h]
                ghost = jnp.where(lanes // 32 == jnp.where(up_y, 3, 0), beside, value)
                ghost = pltpu.roll(ghost, jnp.where(up_y, 25, 103), 1)
                from_y = pltpu.roll(value, jnp.where(up_y, 1, 127), 1)
                from_y = jnp.where(y == jnp.where(up_y, 0, 7), ghost, from_y)

                ghost = jnp.where(up_z, bottoms[h], tops[h])
                from_z = pltpu.roll(value, jnp.where(up_z, 1, 7), 0)
                from_z = jnp.where(rows == jnp.where(up_z, 0, 7), ghost, from_z)

                result = moved(values[h], (from_x, from_y, from_z), size, weights, s)
                provisional[q, s, h] = result
                middle[q, s, h] = 0.5 * (value + result)
        return carry

    lax.fori_loop(0, QUADS, coarse_quad, 0, unroll=4)
    new = (new0, new1)
    weights = weights_of(size, reaction, 0.5)

    def box(i, carry):
        def write(r, s, result):
            new[r][i, s] = result

        fine_step(i, table, (fine0, fine1), coarse, ghosts, sides, goes_up, size, weights, write)
        return carry

    lax.fori_loop(0, BOXES, box, 0, unroll=8)
    edges(new, middle, up_out, down_out, outer_out, inner_out)


def tools_of(courant, coarse_new, folded0, folded1):
    up = [[jnp.maximum(courant[d, s], 0.0) for s in range(SPECIES)] for d in range(3)]
    down = [[jnp.minimum(courant[d, s], 0.0) for s in range(SPECIES)] for d in range(3)]
    taken = lax.broadcasted_iota(jnp.int32, (128, 128), 0)
    given = lax.broadcasted_iota(jnp.int32, (128, 128), 1)
    given_y, fine_y = lax.rem(given, 8), lax.rem(taken, 16)
    same_x = lax.rem(given // 8, 4) == taken // 32

    def summing(rule):
        return jnp.where(same_x & rule(given_y, fine_y), 1.0, 0.0).astype(F32)

    def product(values, matrix):
        return jnp.dot(values, matrix, precision=lax.Precision.HIGHEST, preferred_element_type=F32)

    def fold(tiles, matrix):
        for refs, folded in zip(tiles, (folded0, folded1)):
            pairs = sum(
                ref.reshape(BOXES * SPECIES * 8, 128)[pl.ds(odd, BOXES * SPECIES * 4, stride=2), :]
                for ref in refs
                for odd in range(2)
            )
            folded[...] = product(pairs, matrix)

    def folded_tile(i, s):
        at = pl.ds((i * SPECIES + s) * 4, 4)
        return jnp.concatenate([folded0[at, :], folded1[at, :]])

    def add(q, s, h, where, change):
        coarse_new[q, s, h] = coarse_new[q, s, h] + jnp.where(where, change, 0.0)

    def change_of(here, across, both, beside, rate_out, rate_in, sign):
        return sign * (rate_out * (here - 0.5 * both) + rate_in * (across - 0.125 * beside))

    return up, down, summing, product, fold, folded_tile, add, change_of


def beside_kernel(table, courant, old0, old1, coarse, fine0, fine1, middle, provisional, coarse_new, folded0, folded1):
    _, lanes = iotas()
    y = lax.rem(lanes, 8)
    group = lanes // 32
    up, down, summing, _, fold, folded_tile, add, change_of = tools_of(courant, coarse_new, folded0, folded1)
    coarse_new[...] = provisional[...]

    def rule(given_y, fine_y):
        return ((fine_y == 0) & (given_y == 7)) | ((fine_y == 15) & (given_y == 0))

    fold(((old0, fine0), (old1, fine1)), summing(rule))

    def open_y(i, carry):
        col, half, south, north = [table[STRIDE * i + f] for f in (COL, HALF, SOUTH, NORTH)]
        south_col, north_col = lax.rem(col + GY - 1, GY), lax.rem(col + 1, GY)
        south_quad, north_quad = south_col // 4, north_col // 4
        at_south = (group == lax.rem(south_col, 4)) & (y == 7) & (south < 0)
        at_north = (group == lax.rem(north_col, 4)) & (y == 0) & (north < 0)
        for s in range(SPECIES):
            beside = folded_tile(i, s)
            tile = coarse[col // 4, s, half]
            here = coarse[south_quad, s, half]
            both = here + middle[south_quad, s, half]
            change = change_of(here, turn(tile, -25, 1), both, beside, up[1][s], down[1][s], 1.0)
            add(south_quad, s, half, at_south, change)
            here = coarse[north_quad, s, half]
            both = here + middle[north_quad, s, half]
            change = change_of(here, turn(tile, 25, 1), both, beside, down[1][s], up[1][s], -1.0)
            add(north_quad, s, half, at_north, change)
        return carry

    lax.fori_loop(0, BOXES, open_y, 0, unroll=8)


def second_kernel(
    table, courant, reaction, old0, old1, coarse, old_below, old_above, old_outer, old_inner,
    fine0, fine1, middle, below, above, outer, inner, corrected, out,
    coarse_new, ghosts, result0, result1, folded0, folded1,
):
    rows, lanes = iotas()
    m, part = chunk()
    goes_up, size = signs_of(courant)
    weights = weights_of(size, reaction, 0.5)
    up, down, summing, product, fold, folded_tile, add, change_of = tools_of(courant, coarse_new, folded0, folded1)
    x = lax.rem(lanes // 8, 4)
    y = lax.rem(lanes, 8)
    group = lanes // 32
    ends(table, below, above, ghosts)
    coarse_new[...] = corrected[...]

    sides = sides_of(outer, inner)

    def box_step(i, carry):
        def write(r, s, result):
            (result0, result1)[r][i, s] = result

        fine_step(i, table, (fine0, fine1), middle, ghosts, sides, goes_up, size, weights, write)
        return carry

    lax.fori_loop(0, BOXES, box_step, 0, unroll=8)

    place = lax.rem(lanes, 64)
    rest = jnp.maximum(place - 32, 0)
    slot = lax.rem(rest, 8)
    is_second = (slot >= 2) & (slot < 6)
    depth = jnp.where(place < 32, place // 16, 2 + 2 * (rest // 8) + jnp.where(is_second, 1, 0))
    depth = jnp.minimum(depth, 7)
    rest_y = jnp.where(is_second, slot - 2, slot)
    rest_y = jnp.where(slot >= 4, jnp.where(is_second, slot + 10, slot + 8), rest_y)
    shell_y = jnp.where(place < 32, lax.rem(place, 16), rest_y)
    shell_index = 16 * jnp.where(part > 0, 7 - depth, depth) + shell_y

    def pack_box(i, carry):
        t = table[STRIDE * i + SLOT]
        k = lax.rem(t, 2)
        mine = lanes // 64 == k
        for s in range(SPECIES):
            for r, result in enumerate((result0, result1)):
                at = (2 * s + r) * 8
                packed = take(result[i, s], shell_index, 1)
                out[t // 2, at : at + 8, :] = jnp.where(mine, packed, out[t // 2, at : at + 8, :])
            if s < SPECIES - 1:
                plane = jnp.where(m == 0, result0[i, s, 0:2, :], result1[i, s, 6:8, :])
                out[t // 2, pl.ds(PLANE_ROWS + 8 * k + 2 * s, 2), :] = plane
        return carry

    lax.fori_loop(0, BOXES, pack_box, 0, unroll=4)
    mean_matrix = summing(lambda given_y, fine_y: fine_y // 2 == given_y)

    def open_z(high, row, source, old_source, rate_out, rate_in, sign):
        folded0[:EDGE_COARSE, :] = product(source[:EDGE_COARSE, :] + old_source[:EDGE_COARSE, :], mean_matrix)
        for i in range(BOXES):
            col, half, is_open = [table[STRIDE * i + f] for f in (COL, HALF, OPEN_Z)]
            q = col // 4
            where = (rows == row) & (group == lax.rem(col, 4)) & (half == high) & (is_open > 0)
            for s in range(SPECIES):
                beside = jnp.broadcast_to(folded0[8 * s + i : 8 * s + i + 1, :], (8, 128))
                here = coarse[q, s, 1 - high]
                across = line(old_source, EDGE_COARSE + (2 * s + high) * QUADS + q)
                both = here + middle[q, s, 1 - high]
                change = change_of(here, across, both, beside, rate_out[s], rate_in[s], sign)
                add(q, s, 1 - high, where, change)

    @pl.when(m == CHUNKS - 1)
    def _():
        open_z(1, 7, above, old_above, up[2], down[2], 1.0)

    @pl.when(m == 0)
    def _():
        open_z(0, 0, below, old_below, down[2], up[2], -1.0)

    row_index = 2 * lax.rem(rows, 4)
    last = part > 0
    edge = jnp.where(last, 3, 0)
    sign = jnp.where(last, 1.0, -1.0)
    sums = []
    for s in range(SPECIES):
        totals = [old_outer[0, s, r] + outer[0, s, r] for r in range(2)]
        totals = [take(total + turn(total, -1, 0), row_index, 0) for total in totals]
        total = jnp.where(rows < 4, totals[0], totals[1])
        sums.append(total + turn(total, -1, 1))

    def open_x(q, carry):
        column = 32 * group + 8 * q + y
        for h in range(2):
            box = table[BESIDE + 2 * (4 * q) + h]
            for o in range(1, 4):
                box = jnp.where(group == o, table[BESIDE + 2 * (4 * q + o) + h], box)
            where = (box >= 0) & (x == edge)
            index = 16 * jnp.maximum(box, 0) + 2 * y
            for s in range(SPECIES):
                rate_out = jnp.where(last, up[0][s], down[0][s])
                rate_in = jnp.where(last, down[0][s], up[0][s])
                here = coarse[q, s, h]
                across = take(old_outer[1, s, h], column, 1)
                both = here + middle[q, s, h]
                beside = take(sums[s], index, 1)
                add(q, s, h, where, change_of(here, across, both, beside, rate_out, rate_in, sign))
        return carry

    lax.fori_loop(0, QUADS, open_x, 0, unroll=4)
    fold(((result0,), (result1,)), mean_matrix)

    def cover(i, carry):
        col, half = [table[STRIDE * i + f] for f in (COL, HALF)]
        q = col // 4
        where = group == lax.rem(col, 4)
        for s in range(SPECIES):
            coarse_new[q, s, half] = jnp.where(where, 0.125 * folded_tile(i, s), coarse_new[q, s, half])
        return carry

    lax.fori_loop(0, BOXES, cover, 0, unroll=8)
    for q in range(QUADS):
        for p in range(3):
            at = SHELL_ROWS + 8 * p
            tiles = [turn(coarse_new[q, 2 * p + k // 2, k % 2], 32 * k, 1) for k in range(4 if p < 2 else 2)]
            for o in range(4):
                tile = tiles[0]
                for k in range(1, len(tiles)):
                    tile = jnp.where(group == (o + k) % 4, tiles[k], tile)
                out[4 * q + o, at : at + 8, :] = tile

    def pack_last(i, carry):
        t = table[STRIDE * i + SLOT]
        k, o = lax.rem(t, 2), lax.rem(t // 2, 4)
        plane = jnp.where(m == 0, result0[i, SPECIES - 1], turn(result1[i, SPECIES - 1], 2, 0))
        low = pltpu.roll(plane, lax.rem(32 * o + 64, 128), 1)
        high = pltpu.roll(turn(plane, 2, 0), 32 * o, 1)
        tile = jnp.where(rows < 2, low, high)
        tile = jnp.where(k > 0, turn(tile, 4, 0), tile)
        free = (rows // 4 == k) & (lax.rem(group + 4 - o, 4) >= 2)
        out[t // 2, PLANE_ROWS - 8 : PLANE_ROWS, :] = jnp.where(free, tile, out[t // 2, PLANE_ROWS - 8 : PLANE_ROWS, :])
        return carry

    lax.fori_loop(0, BOXES, pack_last, 0, unroll=8)


def call(kernel, out_shape, operands, smem, scratch=(), in_spec=VMEM, out_spec=VMEM):
    many = isinstance(out_shape, (list, tuple))
    specs = [out_spec] * len(out_shape) if many and not isinstance(out_spec, list) else out_spec
    return pl.pallas_call(
        kernel,
        out_shape=out_shape,
        in_specs=[SMEM] * smem + [in_spec] * (len(operands) - smem),
        out_specs=specs,
        scratch_shapes=list(scratch),
        compiler_params=pltpu.CompilerParams(vmem_limit_bytes=40 * 1024 * 1024),
    )(*operands)


def exchange(up_edge, down_edge, outer_edge, inner_edge):
    device = lambda g, m, part: g % GX * GY + device_of(m % CHUNKS, part, g % GX)
    all_of = [(g, m, part) for g in range(GX) for m in range(CHUNKS) for part in range(2)]
    axes = ("gx", "gy")
    send = lambda value, target: lax.ppermute(value, axes, [(device(*d), device(*target(*d))) for d in all_of])
    outer = send(outer_edge, lambda g, m, part: (g + 2 * part - 1, m, 1 - part))
    below = send(up_edge, lambda g, m, part: (g, m + 1, part))
    above = send(down_edge, lambda g, m, part: (g, m - 1, part))
    inner = send(inner_edge, lambda g, m, part: (g, m, 1 - part))
    return below, above, outer, inner


def spread(pieces):
    return lax.all_to_all(pieces, "gy", 0, 0, tiled=True)


def shards(coarse, fine, corners, ghost_source, courant, reaction):
    shape = lambda *dims: jax.ShapeDtypeStruct(dims, F32)
    pieces = shape(GY, PIECE_ROWS, 128)
    boxes = shape(BOXES, SPECIES, 8, 128)
    grid = shape(QUADS, SPECIES, 2, 8, 128)
    sent = (shape(EDGE_ROWS, 128),) * 2 + (shape(2, SPECIES, 2, 8, 128),) * 2
    whole = (pltpu.VMEM(coarse.shape, F32), pltpu.VMEM(fine.shape, F32))
    copies = pltpu.SemaphoreType.DMA((2 * SPECIES + 1,))
    integers = lambda *dims: pltpu.SMEM(dims, jnp.int32)
    placed = [pltpu.with_memory_space_constraint(value, pltpu.HBM) for value in (corners.T, ghost_source.T, coarse, fine)]
    sending, table = call(
        pack_kernel,
        [pltpu.VMEM(pieces.shape, F32), jax.ShapeDtypeStruct((TABLE,), jnp.int32)],
        placed,
        0,
        (
            *whole,
            pltpu.SemaphoreType.DMA((2 * SPECIES + 3,)),
            integers(2 * LIST_STRIDE),
            integers(2 * ROW_SLOTS),
            integers(3, 512),
            integers(6, 512),
            pltpu.VMEM((128, 128), F32),
        ),
        HBM,
        [VMEM, SMEM],
    )
    received = spread(sending)
    fine0, fine1, middle, *sending = call(compact_kernel, (boxes, boxes, grid) + sent, (table, received), 1)
    old = (fine0, fine1, middle, *exchange(*sending))
    between = (pltpu.VMEM(fine.shape[1:], F32),)
    held, _ = lax.optimization_barrier((fine, old[0]))
    interior = call(interior_kernel, shape(*fine.shape), (courant, reaction, held), 2, between)
    interior, *old = lax.optimization_barrier((interior, *old))
    old = tuple(old)
    ghosts = pltpu.VMEM((EDGE_ROWS, 128), F32)
    new0, new1, middle, provisional, *sending = call(
        first_kernel, (boxes, boxes, grid, grid) + sent, (table, courant, reaction) + old, 3, (ghosts,)
    )
    new = (new0, new1, middle, *exchange(*sending))
    folded = (pltpu.VMEM((BOXES * SPECIES * 4, 128), F32),) * 2
    operands = (table, courant) + old[:3] + new[:3] + (provisional,)
    corrected = call(beside_kernel, grid, operands, 2, folded)
    scratch = (
        pltpu.VMEM(grid.shape, F32),
        ghosts,
        pltpu.VMEM(boxes.shape, F32),
        pltpu.VMEM(boxes.shape, F32),
        *folded,
    )
    back = call(
        second_kernel, shape(GY, BACK_ROWS, 128), (table, courant, reaction) + old + new + (corrected,), 3, scratch
    )
    outputs = (shape(*coarse.shape), shape(*fine.shape))
    scratch = (
        *whole,
        copies,
        pltpu.VMEM((128, 128), F32),
        pltpu.VMEM((2, 128, 128), F32),
        pltpu.VMEM((2, 128, 128), F32),
    )
    return call(unpack_kernel, outputs, (table, spread(back), interior), 1, scratch, VMEM, HBM)


def solution(mesh):
    fine_spec = P(("gx", "gy"), None, None, None, None)
    coarse_spec = P(None, "gx", "gy", None)
    return jax.shard_map(
        shards,
        mesh=mesh,
        in_specs=(coarse_spec, fine_spec, P(), P(), P(), P()),
        out_specs=(coarse_spec, fine_spec),
        check_vma=False,
    )
```

```python
import jax
import jax.numpy as jnp
from jax import lax
from jax.experimental import pallas as pl
from jax.experimental.pallas import tpu as pltpu
from jax.sharding import PartitionSpec as P

CHIP_OF = (0, 1, 2, 3, 7, 6, 5, 4)
SPECIES = 5
GX = 16
GY = 16
BOXES = 8
CHUNKS = 8
QUADS = 4
ROW_SLOTS = 32
FINE_ROWS = 160
PIECE_ROWS = 184
EDGE_ROWS = 80
EDGE_COARSE = 40
STRIDE = 16
LIST_STRIDE = 40
F32 = jnp.float32
SLOT, COL, HALF, WEST, EAST, SOUTH, NORTH, BOTTOM, TOP, OPEN_Z = range(10)
BESIDE = BOXES * STRIDE
OWN = BESIDE + 2 * GY
TABLE = OWN + 4
SHELL_ROWS = 80
PLANE_ROWS = 104
BACK_ROWS = 120

VMEM = pl.BlockSpec(memory_space=pltpu.VMEM)
SMEM = pl.BlockSpec(memory_space=pltpu.SMEM)
HBM = pl.BlockSpec(memory_space=pltpu.HBM)


def device_of(m, part, row):
    turned = (GY // 2) * (row % 2) if isinstance(row, int) else (GY // 2) * lax.rem(row, 2)
    place = 2 * CHIP_OF[m] + part + turned
    return place % GY if isinstance(row, int) else lax.rem(place, GY)


def chunk():
    turned = (GY // 2) * lax.rem(lax.axis_index("gx"), 2)
    j = lax.rem(lax.axis_index("gy") + turned, GY)
    q = j // 2
    return jnp.where(q < 4, q, 11 - q), lax.rem(j, 2)


def fill_table(corners, sources, table, listed, ranks):
    row = lax.axis_index("gx")
    m, part = chunk()
    groups = (row, lax.rem(row + jnp.where(part > 0, 1, GX - 1), GX))

    def scan(t, counts):
        new_counts = []
        for r in range(2):
            live = corners[0, groups[r] * ROW_SLOTS + t] >= 0
            listed[r * LIST_STRIDE + counts[r]] = t
            ranks[r * ROW_SLOTS + t] = counts[r]
            new_counts.append(counts[r] + jnp.where(live, 1, 0))
        return tuple(new_counts)

    lax.fori_loop(0, ROW_SLOTS, scan, (jnp.int32(0), jnp.int32(0)), unroll=True)

    def rank(r, source):
        found = ranks[r * ROW_SLOTS + lax.rem(jnp.maximum(source, 0), ROW_SLOTS)]
        return jnp.where(source >= 0, found, -1)

    for k in range(2 * GY):
        table[BESIDE + k] = -1
    for k in range(2):
        slot = row * ROW_SLOTS + 2 * lax.axis_index("gy") + k
        table[OWN + 2 * k] = jnp.where(corners[0, slot] >= 0, 1, 0)
        table[OWN + 2 * k + 1] = corners[2, slot] // 128
    face = jnp.where(part > 0, 0, 1)
    for i in range(BOXES):
        t = listed[i]
        slot = groups[0] * ROW_SLOTS + t
        south, north, bottom, top = [sources[f, slot] for f in range(2, 6)]
        beside = rank(1, sources[1 - face, slot])
        half = corners[2, slot] // 128
        base = STRIDE * i
        table[base + SLOT] = t
        table[base + COL] = corners[1, slot] // 16
        table[base + HALF] = half
        table[base + WEST] = jnp.where(part > 0, i, beside)
        table[base + EAST] = jnp.where(part > 0, beside, i)
        table[base + SOUTH] = rank(0, south)
        table[base + NORTH] = rank(0, north)
        table[base + BOTTOM] = jnp.where(m > 0, i, rank(0, bottom))
        table[base + TOP] = jnp.where(m < CHUNKS - 1, i, rank(0, top))
        table[base + OPEN_Z] = jnp.where(jnp.where(half > 0, bottom, top) < 0, 1, 0)
        other = groups[1] * ROW_SLOTS + listed[LIST_STRIDE + i]
        spot = corners[1, other] // 16 * 2 + corners[2, other] // 128
        table[BESIDE + spot] = jnp.where(sources[face, other] < 0, i, -1)


def pack_kernel(
    corners_in, sources_in, coarse_in, fine_in, out, table, coarse, fine, loaded, listed, ranks, corners, sources,
    around,
):
    row, column = lax.axis_index("gx"), lax.axis_index("gy")
    blocks = [(k, s) for k in range(2) for s in range(SPECIES)]
    loads = [pltpu.make_async_copy(fine_in.at[k, s], fine.at[k, s], loaded.at[n]) for n, (k, s) in enumerate(blocks)]
    loads.append(pltpu.make_async_copy(coarse_in, coarse, loaded.at[len(blocks)]))
    integers = (
        pltpu.make_async_copy(corners_in, corners, loaded.at[len(blocks) + 1]),
        pltpu.make_async_copy(sources_in, sources, loaded.at[len(blocks) + 2]),
    )
    for load in (*integers, *loads):
        load.start()
    for load in (*integers, *loads[:SPECIES]):
        load.wait()
    fill_table(corners, sources, table, listed, ranks)
    for n, (k, s) in enumerate(blocks):
        if n == SPECIES:
            for load in loads[SPECIES:]:
                load.wait()
        turned = fine[k, s].reshape(256, 128).T
        at = (k * SPECIES + s) * 16
        for m in range(CHUNKS):
            for part in range(2):
                block = turned[16 * m : 16 * m + 16, 128 * part : 128 * part + 128]
                out[device_of(m, part, row), at : at + 16, :] = block
    for p in range(3):
        at = FINE_ROWS + 8 * p
        for part in range(2):
            blocks = []
            for s in (2 * p, 2 * p + 1):
                block = coarse[min(s, 4), 4 * part : 4 * part + 4].reshape(32, 128)
                blocks += [block, pltpu.roll(block, 64, 1)]
            for n, block in enumerate(blocks):
                around[pl.ds(pl.multiple_of(32 * lax.rem(column + n, 4), 32), 32), :] = block
            turned = around[...].T
            for m in range(CHUNKS):
                out[device_of(m, part, row), at : at + 8, :] = turned[8 * m : 8 * m + 8]


def unpack_kernel(table, received, interior, coarse_out, fine_out, coarse, fine, stored, around, shells, planes):
    row, column = lax.axis_index("gx"), lax.axis_index("gy")
    rows, lanes = iotas()
    stores = []

    def send(source, target):
        stores.append(pltpu.make_async_copy(source, target, stored.at[len(stores)]))
        stores[-1].start()

    left = lax.broadcasted_iota(jnp.int32, (32, 128), 1) < 64
    for p in range(3):
        at = SHELL_ROWS + 8 * p
        pieces = [received[device_of(m, part, row), at : at + 8, :] for part in range(2) for m in range(CHUNKS)]
        around[...] = jnp.concatenate(pieces).T
        for s in range(2 * p, min(2 * p + 2, SPECIES)):
            low, high = [
                around[pl.ds(pl.multiple_of(32 * lax.rem(column + 2 * (s - 2 * p) + h, 4), 32), 32), :] for h in range(2)
            ]
            coarse[s, 0:4] = jnp.where(left, low, pltpu.roll(high, 64, 1)).reshape(4, 8, 128)
            coarse[s, 4:8] = jnp.where(left, pltpu.roll(low, 64, 1), high).reshape(4, 8, 128)
    send(coarse, coarse_out)
    live = [table[OWN + 2 * k] > 0 for k in range(2)]
    high = [table[OWN + 2 * k + 1] > 0 for k in range(2)]
    in_plane = [jnp.where(high[k], lanes, 127 - lanes) < 2 for k in range(2)]
    turned = lax.rem(column, 4)
    for part in range(2):
        parts, last = [], []
        for k in range(2):
            source = jnp.where(high[k], device_of(0, part, row), device_of(CHUNKS - 1, part, row))
            parts.append(received[source, PLANE_ROWS + 8 * k : PLANE_ROWS + 8 * k + 8, :])
            tile = received[source, PLANE_ROWS - 8 : PLANE_ROWS, :]
            low = pltpu.roll(tile, lax.rem(192 - 32 * turned, 128), 1)
            rest = pltpu.roll(turn(tile, -2, 0), lax.rem(128 - 32 * turned, 128), 1)
            last.append(jnp.where(lanes < 64, low, rest))
        parts.append(jnp.where(rows < 4, last[0], last[1]))
        planes[part] = jnp.concatenate([*parts, jnp.zeros((104, 128), F32)]).T
    for s in range(SPECIES):
        for part in range(2):
            pieces = [received[device_of(m, part, row), 16 * s : 16 * s + 16, :] for m in range(CHUNKS)]
            shells[part] = jnp.concatenate(pieces).T
        for k in range(2):
            first = 8 * k + 2 * s if s < SPECIES - 1 else 16 + 4 * k
            shift = lax.rem(jnp.where(high[k], 128, 254) - first, 128)
            for x in range(16):
                part, at_x = x // 8, x % 8
                depth = at_x if part == 0 else 7 - at_x
                if depth < 2:
                    at = 64 * k + 16 * depth
                    tiles = [shells[part, at + 8 * j : at + 8 * j + 8, :] for j in range(2)]
                else:
                    at = 64 * k + 32 + 8 * ((depth - 2) // 2)
                    tile = shells[part, at : at + 8, :]
                    sides = (tile, tile) if depth % 2 == 0 else (turn(tile, -2, 0), turn(tile, 2, 0))
                    tiles = []
                    for j in range(2):
                        at = 16 * at_x + 8 * j
                        plane = pltpu.roll(planes[part, at : at + 8, :], shift, 1)
                        inner = jnp.where(in_plane[k], plane, interior[k, s, x, 8 * j : 8 * j + 8, :])
                        tiles.append(jnp.where(rows >= 6 if j else rows < 2, sides[j], inner))
                for j in range(2):
                    fine[k, s, x, 8 * j : 8 * j + 8, :] = jnp.where(live[k], tiles[j], 0.0)
            send(fine.at[k, s], fine_out.at[k, s])
    for store in stores:
        store.wait()


def interior_kernel(courant, reaction, fine, out, between):
    rows, lanes = iotas()
    goes_up, size = signs_of(courant)
    weights = weights_of(size, reaction, 0.5)

    def step(load, store, first, last):
        def plane(x, carry):
            values = [[load(s, x, j) for s in range(SPECIES)] for j in range(2)]
            for s in range(SPECIES):
                up_x, up_y, up_z = [goes_up[d][s] for d in range(3)]
                before = x + jnp.where(up_x, -1, 1)
                low, high = [pltpu.roll(values[j][s], jnp.where(up_y, 1, 7), 0) for j in range(2)]
                from_y = (
                    jnp.where((rows == 7) & jnp.logical_not(up_y), high, low),
                    jnp.where((rows == 0) & up_y, low, high),
                )
                for j in range(2):
                    from_z = pltpu.roll(values[j][s], jnp.where(up_z, 1, 127), 1)
                    from_z = jnp.where(lanes == jnp.where(up_z, 0, 127), 0.0, from_z)
                    upwind = (load(s, before, j), from_y[j], from_z)
                    store(s, x, j, moved(values[j], upwind, size, weights, s))
            return carry

        lax.fori_loop(first, last, plane, 0, unroll=True)

    for k in range(2):

        def put(ref):
            def store(s, x, j, tile):
                ref[s, x, 8 * j : 8 * j + 8, :] = tile

            return store

        def get(ref):
            return lambda s, x, j: ref[s, x, 8 * j : 8 * j + 8, :]

        step(get(fine.at[k]), put(between), 1, 15)
        step(get(between), put(out.at[k]), 2, 14)


def iotas():
    return lax.broadcasted_iota(jnp.int32, (8, 128), 0), lax.broadcasted_iota(jnp.int32, (8, 128), 1)


def take(tile, index, axis):
    return jnp.take_along_axis(tile, index, axis=axis, mode="promise_in_bounds")


def turn(tile, shift, axis):
    return pltpu.roll(tile, shift % tile.shape[axis], axis)


def line(ref, index):
    return jnp.broadcast_to(ref[pl.ds(index, 1), :], (8, 128))


def edges(fine, coarse, up_out, down_out, outer_out, inner_out):
    _, lanes = iotas()
    _, part = chunk()
    last = part > 0
    for s in range(SPECIES):
        up_out[8 * s : 8 * s + 8, :] = fine[1][:, s, 7, :]
        down_out[8 * s : 8 * s + 8, :] = fine[0][:, s, 0, :]
        for h in range(2):
            at = EDGE_COARSE + (2 * s + h) * QUADS
            up_out[at : at + QUADS, :] = coarse[:, s, h, 7, :]
            down_out[at : at + QUADS, :] = coarse[:, s, h, 0, :]
        for r in range(2):
            low = high = coarse_low = coarse_high = jnp.zeros((8, 128), F32)
            for i in range(BOXES):
                here = lanes // 16 == i
                low = jnp.where(here, turn(fine[r][i, s], 16 * i, 1), low)
                high = jnp.where(here, turn(fine[r][i, s], 16 * i + 16, 1), high)
            for q in range(QUADS):
                here = lax.rem(lanes // 8, 4) == q
                coarse_low = jnp.where(here, turn(coarse[q, s, r], 8 * q, 1), coarse_low)
                coarse_high = jnp.where(here, turn(coarse[q, s, r], 8 * q - 24, 1), coarse_high)
            outer_out[0, s, r] = jnp.where(last, high, low)
            inner_out[0, s, r] = jnp.where(last, low, high)
            outer_out[1, s, r] = jnp.where(last, coarse_high, coarse_low)
            inner_out[1, s, r] = jnp.where(last, coarse_low, coarse_high)


def compact_kernel(table, received, fine0, fine1, coarse, up_out, down_out, outer_out, inner_out):
    _, lanes = iotas()
    for i in range(BOXES):
        t = table[STRIDE * i + SLOT]
        start = pl.multiple_of(lax.rem(t, 2) * 80, 8)
        box = received[t // 2, pl.ds(start, 80), :].reshape(SPECIES, 2, 8, 128)
        fine0[i] = box[:, 0]
        fine1[i] = box[:, 1]
    for q in range(QUADS):
        for p in range(3):
            at = FINE_ROWS + 8 * p
            tiles = [received[4 * q + o, at : at + 8, :] for o in range(4)]
            for k in range(4 if p < 2 else 2):
                tile = tiles[0]
                for o in range(1, 4):
                    tile = jnp.where(lanes // 32 == (o + k) % 4, tiles[o], tile)
                coarse[q, 2 * p + k // 2, k % 2] = turn(tile, -32 * k, 1)
    edges((fine0, fine1), coarse, up_out, down_out, outer_out, inner_out)


def signs_of(courant):
    goes_up = [[courant[d, s] >= 0.0 for s in range(SPECIES)] for d in range(3)]
    size = [[jnp.abs(courant[d, s]) for s in range(SPECIES)] for d in range(3)]
    return goes_up, size


def weights_of(size, reaction, factor):
    weights = [[factor * reaction[s, e] for e in range(SPECIES)] for s in range(SPECIES)]
    for s in range(SPECIES):
        weights[s][s] = weights[s][s] + (1.0 - size[0][s] - size[1][s] - size[2][s])
    return weights


def moved(values, upwind, size, weights, s):
    total = weights[s][0] * values[0]
    for e in range(1, SPECIES):
        total = total + weights[s][e] * values[e]
    for d in range(3):
        total = total + size[d][s] * upwind[d]
    return total


def ends(table, below, above, ghosts):
    _, lanes = iotas()
    m, _ = chunk()
    ghosts[:EDGE_COARSE, :] = below[:EDGE_COARSE, :]
    ghosts[EDGE_COARSE:, :] = above[:EDGE_COARSE, :]

    def replace(side, source, name, high):
        for i in range(BOXES):
            col, half, found = [table[STRIDE * i + f] for f in (COL, HALF, name)]
            inside = 32 * lax.rem(col, 4) + 8 * (lanes // 32) + lax.rem(lanes, 16) // 2
            for s in range(SPECIES):
                other = take(line(source, EDGE_COARSE + (2 * s + side) * QUADS + col // 4), inside, 1)
                other = jnp.where(half == high, other, 0.0)
                ghost = jnp.where(found >= 0, line(source, 8 * s + jnp.maximum(found, 0)), other)
                at = EDGE_COARSE * side + 8 * s + i
                ghosts[at : at + 1, :] = ghost[:1]

    @pl.when(m == 0)
    def _():
        replace(0, below, BOTTOM, 1)

    @pl.when(m == CHUNKS - 1)
    def _():
        replace(1, above, TOP, 0)


def fine_step(i, table, fine, coarse, ghosts, sides, goes_up, size, weights, write):
    rows, lanes = iotas()
    field = lambda f: table[STRIDE * i + f]
    col, half = field(COL), field(HALF)
    lower_col, upper_col = lax.rem(col + GY - 1, GY), lax.rem(col + 1, GY)
    y = lax.rem(lanes, 16)
    found = [field(f) for f in (WEST, EAST, SOUTH, NORTH)]
    there = [source >= 0 for source in found]
    at = [jnp.maximum(source, 0) for source in found]
    beside = 32 * lax.rem(col, 4) + 8 * (col // 4) + y // 2
    lane_x = [jnp.where(there[f], 16 * at[f] + y, beside) for f in range(2)]
    own_x, line_x = lanes - y, 8 * (lanes // 32)
    lane_y = [
        jnp.where(there[2], own_x + 15, 32 * lax.rem(lower_col, 4) + line_x + 7),
        jnp.where(there[3], own_x, 32 * lax.rem(upper_col, 4) + line_x),
    ]
    row_of = [[jnp.where(is_there, rows, 4 * r + rows // 2) for is_there in there] for r in range(2)]
    kind = [jnp.where(is_there, 0, 1) for is_there in there]
    values = [[fine[r][i, s] for s in range(SPECIES)] for r in range(2)]
    for s in range(SPECIES):
        up_x, up_y, up_z = [goes_up[d][s] for d in range(3)]
        shift_x, edge_x = jnp.where(up_x, 16, 112), lanes // 16 == jnp.where(up_x, 0, 7)
        shift_y, edge_y = jnp.where(up_y, 1, 127), y == jnp.where(up_y, 0, 15)
        shift_z, edge_z = jnp.where(up_z, 1, 7), rows == jnp.where(up_z, 0, 7)
        is_there = jnp.where(up_y, found[2], found[3]) >= 0
        box_y = jnp.where(up_y, at[2], at[3])
        quad_y = jnp.where(up_y, lower_col, upper_col) // 4
        coarse_y = coarse[quad_y, s, half]
        index_x = jnp.where(up_x, lane_x[0], lane_x[1])
        index_y = jnp.where(up_y, lane_y[0], lane_y[1])

        low, high = values[0][s], values[1][s]
        first = pltpu.roll(jnp.where(up_z, low, high), shift_z, 0)
        second = pltpu.roll(jnp.where(up_z, high, low), shift_z, 0)
        second = jnp.where(edge_z, first, second)
        first = jnp.where(edge_z, line(ghosts, jnp.where(up_z, 0, EDGE_COARSE) + 8 * s + i), first)
        from_z = (jnp.where(up_z, first, second), jnp.where(up_z, second, first))

        for r in range(2):
            value = values[r][s]
            west = sides(0, kind[0], s, jnp.where(there[0], r, half))
            east = sides(1, kind[1], s, jnp.where(there[1], r, half))
            ghost = take(jnp.where(up_x, west, east), jnp.where(up_x, row_of[r][0], row_of[r][1]), 0)
            ghost = take(ghost, index_x, 1)
            from_x = jnp.where(edge_x, ghost, pltpu.roll(value, shift_x, 1))
            ghost = take(
                jnp.where(is_there, fine[r][box_y, s], coarse_y), jnp.where(up_y, row_of[r][2], row_of[r][3]), 0
            )
            ghost = take(ghost, index_y, 1)
            from_y = jnp.where(edge_y, ghost, pltpu.roll(value, shift_y, 1))
            write(r, s, moved(values[r], (from_x, from_y, from_z[r]), size, weights, s))


def sides_of(outer, inner):
    _, part = chunk()

    def pick(side, kind, s, at):
        one, other = outer[kind, s, at], inner[kind, s, at]
        return jnp.where(part == side, one, other)

    return pick


def first_kernel(
    table, courant, reaction, fine0, fine1, coarse, below, above, outer, inner,
    new0, new1, middle, provisional, up_out, down_out, outer_out, inner_out, ghosts,
):
    rows, lanes = iotas()
    m, _ = chunk()
    goes_up, size = signs_of(courant)
    weights = weights_of(size, reaction, 1.0)
    x = lax.rem(lanes // 8, 4)
    y = lax.rem(lanes, 8)
    sides = sides_of(outer, inner)
    ends(table, below, above, ghosts)

    def coarse_quad(q, carry):
        before, after = lax.rem(q + QUADS - 1, QUADS), lax.rem(q + 1, QUADS)
        values = [[coarse[q, s, h] for s in range(SPECIES)] for h in range(2)]
        column = 32 * (lanes // 32) + 8 * q + y
        for s in range(SPECIES):
            up_x, up_y, up_z = [goes_up[d][s] for d in range(3)]
            at = [EDGE_COARSE + (2 * s + h) * QUADS + q for h in range(2)]
            lows, highs = [line(below, k) for k in at], [line(above, k) for k in at]
            bottoms = (jnp.where(m > 0, lows[0], 0.0), jnp.where(m > 0, lows[1], lows[0]))
            tops = (
                jnp.where(m < CHUNKS - 1, highs[0], highs[1]),
                jnp.where(m < CHUNKS - 1, highs[1], 0.0),
            )
            for h in range(2):
                value = values[h][s]
                ghost = take(jnp.where(up_x, sides(0, 1, s, h), sides(1, 1, s, h)), column, 1)
                from_x = pltpu.roll(value, jnp.where(up_x, 8, 120), 1)
                from_x = jnp.where(x == jnp.where(up_x, 0, 3), ghost, from_x)

                beside = coarse[jnp.where(up_y, before, after), s, h]
                ghost = jnp.where(lanes // 32 == jnp.where(up_y, 3, 0), beside, value)
                ghost = pltpu.roll(ghost, jnp.where(up_y, 25, 103), 1)
                from_y = pltpu.roll(value, jnp.where(up_y, 1, 127), 1)
                from_y = jnp.where(y == jnp.where(up_y, 0, 7), ghost, from_y)

                ghost = jnp.where(up_z, bottoms[h], tops[h])
                from_z = pltpu.roll(value, jnp.where(up_z, 1, 7), 0)
                from_z = jnp.where(rows == jnp.where(up_z, 0, 7), ghost, from_z)

                result = moved(values[h], (from_x, from_y, from_z), size, weights, s)
                provisional[q, s, h] = result
                middle[q, s, h] = 0.5 * (value + result)
        return carry

    lax.fori_loop(0, QUADS, coarse_quad, 0, unroll=4)
    new = (new0, new1)
    weights = weights_of(size, reaction, 0.5)

    def box(i, carry):
        def write(r, s, result):
            new[r][i, s] = result

        fine_step(i, table, (fine0, fine1), coarse, ghosts, sides, goes_up, size, weights, write)
        return carry

    lax.fori_loop(0, BOXES, box, 0, unroll=8)
    edges(new, middle, up_out, down_out, outer_out, inner_out)


def tools_of(courant, coarse_new, folded0, folded1):
    up = [[jnp.maximum(courant[d, s], 0.0) for s in range(SPECIES)] for d in range(3)]
    down = [[jnp.minimum(courant[d, s], 0.0) for s in range(SPECIES)] for d in range(3)]
    taken = lax.broadcasted_iota(jnp.int32, (128, 128), 0)
    given = lax.broadcasted_iota(jnp.int32, (128, 128), 1)
    given_y, fine_y = lax.rem(given, 8), lax.rem(taken, 16)
    same_x = lax.rem(given // 8, 4) == taken // 32

    def summing(rule):
        return jnp.where(same_x & rule(given_y, fine_y), 1.0, 0.0).astype(F32)

    def product(values, matrix):
        return jnp.dot(values, matrix, precision=lax.Precision.HIGHEST, preferred_element_type=F32)

    def fold(tiles, matrix):
        for refs, folded in zip(tiles, (folded0, folded1)):
            pairs = sum(
                ref.reshape(BOXES * SPECIES * 8, 128)[pl.ds(odd, BOXES * SPECIES * 4, stride=2), :]
                for ref in refs
                for odd in range(2)
            )
            folded[...] = product(pairs, matrix)

    def folded_tile(i, s):
        at = pl.ds((i * SPECIES + s) * 4, 4)
        return jnp.concatenate([folded0[at, :], folded1[at, :]])

    def add(q, s, h, where, change):
        coarse_new[q, s, h] = coarse_new[q, s, h] + jnp.where(where, change, 0.0)

    def change_of(here, across, both, beside, rate_out, rate_in, sign):
        return sign * (rate_out * (here - 0.5 * both) + rate_in * (across - 0.125 * beside))

    return up, down, summing, product, fold, folded_tile, add, change_of


def beside_kernel(table, courant, old0, old1, coarse, fine0, fine1, middle, provisional, coarse_new, folded0, folded1):
    _, lanes = iotas()
    y = lax.rem(lanes, 8)
    group = lanes // 32
    up, down, summing, _, fold, folded_tile, add, change_of = tools_of(courant, coarse_new, folded0, folded1)
    coarse_new[...] = provisional[...]

    def rule(given_y, fine_y):
        return ((fine_y == 0) & (given_y == 7)) | ((fine_y == 15) & (given_y == 0))

    fold(((old0, fine0), (old1, fine1)), summing(rule))

    def open_y(i, carry):
        col, half, south, north = [table[STRIDE * i + f] for f in (COL, HALF, SOUTH, NORTH)]
        south_col, north_col = lax.rem(col + GY - 1, GY), lax.rem(col + 1, GY)
        south_quad, north_quad = south_col // 4, north_col // 4
        at_south = (group == lax.rem(south_col, 4)) & (y == 7) & (south < 0)
        at_north = (group == lax.rem(north_col, 4)) & (y == 0) & (north < 0)
        for s in range(SPECIES):
            beside = folded_tile(i, s)
            tile = coarse[col // 4, s, half]
            here = coarse[south_quad, s, half]
            both = here + middle[south_quad, s, half]
            change = change_of(here, turn(tile, -25, 1), both, beside, up[1][s], down[1][s], 1.0)
            add(south_quad, s, half, at_south, change)
            here = coarse[north_quad, s, half]
            both = here + middle[north_quad, s, half]
            change = change_of(here, turn(tile, 25, 1), both, beside, down[1][s], up[1][s], -1.0)
            add(north_quad, s, half, at_north, change)
        return carry

    lax.fori_loop(0, BOXES, open_y, 0, unroll=8)


def second_kernel(
    table, courant, reaction, old0, old1, coarse, old_below, old_above, old_outer, old_inner,
    fine0, fine1, middle, below, above, outer, inner, corrected, out,
    coarse_new, ghosts, result0, result1, folded0, folded1,
):
    rows, lanes = iotas()
    m, part = chunk()
    goes_up, size = signs_of(courant)
    weights = weights_of(size, reaction, 0.5)
    up, down, summing, product, fold, folded_tile, add, change_of = tools_of(courant, coarse_new, folded0, folded1)
    x = lax.rem(lanes // 8, 4)
    y = lax.rem(lanes, 8)
    group = lanes // 32
    ends(table, below, above, ghosts)
    coarse_new[...] = corrected[...]

    sides = sides_of(outer, inner)

    def box_step(i, carry):
        def write(r, s, result):
            (result0, result1)[r][i, s] = result

        fine_step(i, table, (fine0, fine1), middle, ghosts, sides, goes_up, size, weights, write)
        return carry

    lax.fori_loop(0, BOXES, box_step, 0, unroll=8)

    place = lax.rem(lanes, 64)
    rest = jnp.maximum(place - 32, 0)
    slot = lax.rem(rest, 8)
    is_second = (slot >= 2) & (slot < 6)
    depth = jnp.where(place < 32, place // 16, 2 + 2 * (rest // 8) + jnp.where(is_second, 1, 0))
    depth = jnp.minimum(depth, 7)
    rest_y = jnp.where(is_second, slot - 2, slot)
    rest_y = jnp.where(slot >= 4, jnp.where(is_second, slot + 10, slot + 8), rest_y)
    shell_y = jnp.where(place < 32, lax.rem(place, 16), rest_y)
    shell_index = 16 * jnp.where(part > 0, 7 - depth, depth) + shell_y

    def pack_box(i, carry):
        t = table[STRIDE * i + SLOT]
        k = lax.rem(t, 2)
        mine = lanes // 64 == k
        for s in range(SPECIES):
            for r, result in enumerate((result0, result1)):
                at = (2 * s + r) * 8
                packed = take(result[i, s], shell_index, 1)
                out[t // 2, at : at + 8, :] = jnp.where(mine, packed, out[t // 2, at : at + 8, :])
            if s < SPECIES - 1:
                plane = jnp.where(m == 0, result0[i, s, 0:2, :], result1[i, s, 6:8, :])
                out[t // 2, pl.ds(PLANE_ROWS + 8 * k + 2 * s, 2), :] = plane
        return carry

    lax.fori_loop(0, BOXES, pack_box, 0, unroll=8)
    mean_matrix = summing(lambda given_y, fine_y: fine_y // 2 == given_y)

    def open_z(high, row, source, old_source, rate_out, rate_in, sign):
        folded0[:EDGE_COARSE, :] = product(source[:EDGE_COARSE, :] + old_source[:EDGE_COARSE, :], mean_matrix)
        for i in range(BOXES):
            col, half, is_open = [table[STRIDE * i + f] for f in (COL, HALF, OPEN_Z)]
            q = col // 4
            where = (rows == row) & (group == lax.rem(col, 4)) & (half == high) & (is_open > 0)
            for s in range(SPECIES):
                beside = jnp.broadcast_to(folded0[8 * s + i : 8 * s + i + 1, :], (8, 128))
                here = coarse[q, s, 1 - high]
                across = line(old_source, EDGE_COARSE + (2 * s + high) * QUADS + q)
                both = here + middle[q, s, 1 - high]
                change = change_of(here, across, both, beside, rate_out[s], rate_in[s], sign)
                add(q, s, 1 - high, where, change)

    @pl.when(m == CHUNKS - 1)
    def _():
        open_z(1, 7, above, old_above, up[2], down[2], 1.0)

    @pl.when(m == 0)
    def _():
        open_z(0, 0, below, old_below, down[2], up[2], -1.0)

    row_index = 2 * lax.rem(rows, 4)
    last = part > 0
    edge = jnp.where(last, 3, 0)
    sign = jnp.where(last, 1.0, -1.0)
    sums = []
    for s in range(SPECIES):
        totals = [old_outer[0, s, r] + outer[0, s, r] for r in range(2)]
        totals = [take(total + turn(total, -1, 0), row_index, 0) for total in totals]
        total = jnp.where(rows < 4, totals[0], totals[1])
        sums.append(total + turn(total, -1, 1))

    def open_x(q, carry):
        column = 32 * group + 8 * q + y
        for h in range(2):
            box = table[BESIDE + 2 * (4 * q) + h]
            for o in range(1, 4):
                box = jnp.where(group == o, table[BESIDE + 2 * (4 * q + o) + h], box)
            where = (box >= 0) & (x == edge)
            index = 16 * jnp.maximum(box, 0) + 2 * y
            for s in range(SPECIES):
                rate_out = jnp.where(last, up[0][s], down[0][s])
                rate_in = jnp.where(last, down[0][s], up[0][s])
                here = coarse[q, s, h]
                across = take(old_outer[1, s, h], column, 1)
                both = here + middle[q, s, h]
                beside = take(sums[s], index, 1)
                add(q, s, h, where, change_of(here, across, both, beside, rate_out, rate_in, sign))
        return carry

    lax.fori_loop(0, QUADS, open_x, 0, unroll=4)
    fold(((result0,), (result1,)), mean_matrix)

    def cover(i, carry):
        col, half = [table[STRIDE * i + f] for f in (COL, HALF)]
        q = col // 4
        where = group == lax.rem(col, 4)
        for s in range(SPECIES):
            coarse_new[q, s, half] = jnp.where(where, 0.125 * folded_tile(i, s), coarse_new[q, s, half])
        return carry

    lax.fori_loop(0, BOXES, cover, 0, unroll=8)
    for q in range(QUADS):
        for p in range(3):
            at = SHELL_ROWS + 8 * p
            tiles = [turn(coarse_new[q, 2 * p + k // 2, k % 2], 32 * k, 1) for k in range(4 if p < 2 else 2)]
            for o in range(4):
                tile = tiles[0]
                for k in range(1, len(tiles)):
                    tile = jnp.where(group == (o + k) % 4, tiles[k], tile)
                out[4 * q + o, at : at + 8, :] = tile

    def pack_last(i, carry):
        t = table[STRIDE * i + SLOT]
        k, o = lax.rem(t, 2), lax.rem(t // 2, 4)
        plane = jnp.where(m == 0, result0[i, SPECIES - 1], turn(result1[i, SPECIES - 1], 2, 0))
        low = pltpu.roll(plane, lax.rem(32 * o + 64, 128), 1)
        high = pltpu.roll(turn(plane, 2, 0), 32 * o, 1)
        tile = jnp.where(rows < 2, low, high)
        tile = jnp.where(k > 0, turn(tile, 4, 0), tile)
        free = (rows // 4 == k) & (lax.rem(group + 4 - o, 4) >= 2)
        out[t // 2, PLANE_ROWS - 8 : PLANE_ROWS, :] = jnp.where(free, tile, out[t // 2, PLANE_ROWS - 8 : PLANE_ROWS, :])
        return carry

    lax.fori_loop(0, BOXES, pack_last, 0, unroll=8)


def call(kernel, out_shape, operands, smem, scratch=(), in_spec=VMEM, out_spec=VMEM):
    many = isinstance(out_shape, (list, tuple))
    specs = [out_spec] * len(out_shape) if many and not isinstance(out_spec, list) else out_spec
    return pl.pallas_call(
        kernel,
        out_shape=out_shape,
        in_specs=[SMEM] * smem + [in_spec] * (len(operands) - smem),
        out_specs=specs,
        scratch_shapes=list(scratch),
        compiler_params=pltpu.CompilerParams(vmem_limit_bytes=40 * 1024 * 1024),
    )(*operands)


def exchange(up_edge, down_edge, outer_edge, inner_edge):
    device = lambda g, m, part: g % GX * GY + device_of(m % CHUNKS, part, g % GX)
    all_of = [(g, m, part) for g in range(GX) for m in range(CHUNKS) for part in range(2)]
    axes = ("gx", "gy")
    send = lambda value, target: lax.ppermute(value, axes, [(device(*d), device(*target(*d))) for d in all_of])
    outer = send(outer_edge, lambda g, m, part: (g + 2 * part - 1, m, 1 - part))
    below = send(up_edge, lambda g, m, part: (g, m + 1, part))
    above = send(down_edge, lambda g, m, part: (g, m - 1, part))
    inner = send(inner_edge, lambda g, m, part: (g, m, 1 - part))
    return below, above, outer, inner


def spread(pieces):
    return lax.all_to_all(pieces, "gy", 0, 0, tiled=True)


def shards(coarse, fine, corners, ghost_source, courant, reaction):
    shape = lambda *dims: jax.ShapeDtypeStruct(dims, F32)
    pieces = shape(GY, PIECE_ROWS, 128)
    boxes = shape(BOXES, SPECIES, 8, 128)
    grid = shape(QUADS, SPECIES, 2, 8, 128)
    sent = (shape(EDGE_ROWS, 128),) * 2 + (shape(2, SPECIES, 2, 8, 128),) * 2
    whole = (pltpu.VMEM(coarse.shape, F32), pltpu.VMEM(fine.shape, F32))
    copies = pltpu.SemaphoreType.DMA((2 * SPECIES + 1,))
    integers = lambda *dims: pltpu.SMEM(dims, jnp.int32)
    placed = [pltpu.with_memory_space_constraint(value, pltpu.HBM) for value in (corners.T, ghost_source.T, coarse, fine)]
    sending, table = call(
        pack_kernel,
        [pltpu.VMEM(pieces.shape, F32), jax.ShapeDtypeStruct((TABLE,), jnp.int32)],
        placed,
        0,
        (
            *whole,
            pltpu.SemaphoreType.DMA((2 * SPECIES + 3,)),
            integers(2 * LIST_STRIDE),
            integers(2 * ROW_SLOTS),
            integers(3, 512),
            integers(6, 512),
            pltpu.VMEM((128, 128), F32),
        ),
        HBM,
        [VMEM, SMEM],
    )
    received = spread(sending)
    fine0, fine1, middle, *sending = call(compact_kernel, (boxes, boxes, grid) + sent, (table, received), 1)
    old = (fine0, fine1, middle, *exchange(*sending))
    between = (pltpu.VMEM(fine.shape[1:], F32),)
    held, _ = lax.optimization_barrier((fine, old[0]))
    interior = call(interior_kernel, shape(*fine.shape), (courant, reaction, held), 2, between)
    interior, *old = lax.optimization_barrier((interior, *old))
    old = tuple(old)
    ghosts = pltpu.VMEM((EDGE_ROWS, 128), F32)
    new0, new1, middle, provisional, *sending = call(
        first_kernel, (boxes, boxes, grid, grid) + sent, (table, courant, reaction) + old, 3, (ghosts,)
    )
    new = (new0, new1, middle, *exchange(*sending))
    folded = (pltpu.VMEM((BOXES * SPECIES * 4, 128), F32),) * 2
    operands = (table, courant) + old[:3] + new[:3] + (provisional,)
    corrected = call(beside_kernel, grid, operands, 2, folded)
    scratch = (
        pltpu.VMEM(grid.shape, F32),
        ghosts,
        pltpu.VMEM(boxes.shape, F32),
        pltpu.VMEM(boxes.shape, F32),
        *folded,
    )
    back = call(
        second_kernel, shape(GY, BACK_ROWS, 128), (table, courant, reaction) + old + new + (corrected,), 3, scratch
    )
    outputs = (shape(*coarse.shape), shape(*fine.shape))
    scratch = (
        *whole,
        copies,
        pltpu.VMEM((128, 128), F32),
        pltpu.VMEM((2, 128, 128), F32),
        pltpu.VMEM((2, 128, 128), F32),
    )
    return call(unpack_kernel, outputs, (table, spread(back), interior), 1, scratch, VMEM, HBM)


def solution(mesh):
    fine_spec = P(("gx", "gy"), None, None, None, None)
    coarse_spec = P(None, "gx", "gy", None)
    return jax.shard_map(
        shards,
        mesh=mesh,
        in_specs=(coarse_spec, fine_spec, P(), P(), P(), P()),
        out_specs=(coarse_spec, fine_spec),
        check_vma=False,
    )
```
